32 devices in a mesh: lat: 4 (over y, x), tm: 8 (over z, core).
Axes of the slice: x: 2, y: 2, z: 4, core: 2. Of those that a mesh axis runs over, the one named last changes fastest.
Arguments:
- light_field: float32 [2, 1024, 2048], P(None, 'lat', 'tm'), may hold values from -6 to 6
- lateral_phase: float32 [1024], replicated, may hold values from -3.140625 to 3.140625
- spectral_phase: float32 [2048], replicated, may hold values from -3.140625 to 3.140625
- occupation: float32 [128, 1024], P(None, 'lat'), may hold values from -0.5 to 1
- bin_decay: float32 [32], replicated, may hold values from 2e-05 to 0.05
- bin_detune: float32 [32], replicated, may hold values from -0.3 to 0.3
- group_bin: int32 [128], replicated, may hold values from 0 to 31
Outputs:
- output_field: float32 [2, 1024, 2048], P(None, 'lat', 'tm')
The draws below stay inside these ranges and needn't reach their ends.
All inputs are finite; a program needn't handle non-finite values.
Results may differ from the reference program's by a relative error of at most 0.0003.
Values sent between devices are 32-bit elements; how exact they have to be, the bound alone decides.
A program may use at most 128 MiB of HBM per device.

```python
import math
import jax
import jax.numpy as jnp
from jax import lax

NX = 1024
GROUPS = 128
BINS = 32
STEPS = 2
NT = 2048


def place_ends(drawn, own_key, smallest, top_value):
    dims = drawn.shape
    spot = [jax.random.randint(jax.random.fold_in(own_key, axis), (), 0, dims[axis]) for axis in range(len(dims))]
    drawn = drawn.at[tuple(spot)].set(smallest)
    longest = dims.index(max(dims))
    spot[longest] = (spot[longest] + 1) % dims[longest]
    return drawn.at[tuple(spot)].set(top_value)


def levels(rng, dims, shards, smallest, top_value):
    factor_of = 1.0
    for dim, blocks in shards:
        steps = jax.random.uniform(jax.random.fold_in(jax.random.fold_in(rng, 6), dim), (blocks,), jnp.float32, smallest / len(shards), top_value / len(shards))
        factor_of = factor_of * jnp.repeat(jnp.exp(steps), dims[dim] // blocks).reshape((-1,) + (1,) * (len(dims) - 1 - dim))
    return factor_of


def scatter_about(stream_key, dims, spread, most, pieces=(), kind=jnp.bfloat16):
    entries = jax.random.normal(stream_key, dims, jnp.float32) * spread
    if len(pieces) > 0:
        entries = levels(stream_key, dims, pieces, -0.22, 0.18) * entries
    return jnp.clip(entries, min=-most, max=most).astype(kind)


def setup_inputs(seed: int = 0) -> dict:
    streams_of = jax.random.split(jax.random.key(seed), 8)
    return {
        "light_field": scatter_about(streams_of[0], (2, NX, NT), 1.0, 6.0, ((1, 4), (2, 8)), jnp.float32),
        "lateral_phase": jnp.clip(jax.random.uniform(streams_of[1], (NX,), jnp.float32, -3.140625, 3.140625), -3.140625, 3.140625),
        "spectral_phase": jnp.clip(jax.random.uniform(streams_of[2], (NT,), jnp.float32, -3.140625, 3.140625), -3.140625, 3.140625),
        "occupation": jnp.clip(-0.5 + 1.5 * jax.random.uniform(streams_of[3], (GROUPS, NX), jnp.float32) ** levels(streams_of[3], (GROUPS, NX), ((1, 4),), -0.2, 0.2), -0.5, 1.0),
        "bin_decay": jnp.clip(jnp.exp(jax.random.uniform(streams_of[4], (BINS,), jnp.float32, math.log(1.9999999494757503e-05), math.log(0.05))), 1.9999999494757503e-05, 0.05),
        "bin_detune": jnp.clip(jax.random.uniform(streams_of[5], (BINS,), jnp.float32, -0.3, 0.3), -0.3, 0.3),
        "group_bin": place_ends(jax.random.randint(streams_of[6], (GROUPS,), 0, BINS), jax.random.fold_in(streams_of[6], 1), 0, BINS - 1).astype(jnp.int32),
    }


GAIN_SCALE = 0.5

def reference(light_field, lateral_phase, spectral_phase, occupation, bin_decay, bin_detune, group_bin):
    decay_rate = bin_decay[group_bin]
    detuning = bin_detune[group_bin]
    propagator = jnp.exp(-decay_rate) * (jnp.cos(detuning) - 1j * jnp.sin(detuning))
    drive = jnp.sqrt(-jnp.expm1(-2.0 * decay_rate))
    coupling = drive[:, None] * occupation
    weight = GAIN_SCALE / jnp.sqrt(jnp.float32(occupation.shape[0]))
    current = light_field[0] + 1j * light_field[1]
    lateral_turn = jnp.exp(1j * lateral_phase)[:, None]
    spectral_turn = jnp.exp(1j * spectral_phase)[None, :]

    def advance(polar_state, column):
        polar_state = propagator[:, None] * polar_state + coupling * column[None, :]
        return (polar_state, lax.optimization_barrier(jnp.sum(polar_state, axis=0)))
    for repeat in range(STEPS):
        current = jnp.fft.ifft(jnp.fft.fft(current, axis=0) * lateral_turn, axis=0)
        current = jnp.fft.ifft(jnp.fft.fft(current, axis=1) * spectral_turn, axis=1)
        initial = jnp.zeros(coupling.shape, current.dtype)
        ignored, summed = lax.scan(advance, initial, current.T)
        current = current + 1j * weight * summed.T
    return jnp.stack([jnp.real(current), jnp.imag(current)]).astype(jnp.float32)
```

```python
import functools
import math

import jax
import jax.numpy as jnp
import numpy as np
from jax import lax
from jax.experimental import pallas as pl
from jax.experimental.pallas import tpu as pltpu
from jax.sharding import PartitionSpec as P

STRETCH = 128
STEPS = 2


GAIN_SCALE = 0.5


def carried_in(value, axis, join, neutral):
    count, mine = (lax.axis_size(axis), lax.axis_index(axis))
    pieces = jax.tree.map(lambda part: lax.all_gather(part, axis), value)
    so_far = jax.tree.map(
        lambda part, zero: jnp.full_like(part, 0) + jnp.asarray(zero, part.dtype), value, neutral
    )

    def lap(position, so_far):
        longer = join(so_far, jax.tree.map(lambda part: part[position], pieces))
        return jax.tree.map(lambda new, old: jnp.where(position < mine, new, old), longer, so_far)

    return lax.fori_loop(0, count - 1, lap, so_far)


def complex_einsum(form, left, right):
    exact = lax.Precision.HIGHEST
    real_part = jnp.einsum(form, left[0], right[0], precision=exact) - jnp.einsum(
        form, left[1], right[1], precision=exact
    )
    imag_part = jnp.einsum(form, left[0], right[1], precision=exact) + jnp.einsum(
        form, left[1], right[0], precision=exact
    )
    return (real_part, imag_part)


def complex_times(left, right):
    return (left[0] * right[0] - left[1] * right[1], left[0] * right[1] + left[1] * right[0])


def angle_table(height, breadth, modulus, sign):
    first = jnp.arange(height, dtype=jnp.int32)[:, None]
    second = jnp.arange(breadth, dtype=jnp.int32)[None, :]
    turns = (first * second % modulus).astype(jnp.float32) * (2.0 * math.pi / modulus)
    return (jnp.cos(turns), sign * jnp.sin(turns))


def time_forward(grid, small_table, twiddle, long_table):
    mixed = complex_einsum("ka,rab->rkb", small_table, grid)
    mixed = complex_times(mixed, twiddle)
    return complex_einsum("rkb,bq->rkq", mixed, long_table)


def time_inverse(spectrum, small_table, twiddle, long_table, length):
    mixed = complex_einsum("rkq,qb->rkb", spectrum, long_table)
    mixed = complex_times(mixed, twiddle)
    result = complex_einsum("ak,rkb->rab", small_table, mixed)
    return (result[0] / length, result[1] / length)


def powers(decay_rate, detuning, exponent):
    magnitude = jnp.exp(-decay_rate * exponent)
    phase_angle = detuning * exponent
    return (magnitude * jnp.cos(phase_angle), -magnitude * jnp.sin(phase_angle))


def on_device(
    light_field, lateral_phase, spectral_phase, occupation, bin_decay, bin_detune, group_bin
):
    lat_count = lax.axis_size("lat")
    time_count = lax.axis_size("tm")
    height = light_field.shape[1]
    span = light_field.shape[2]
    lateral_total = height * lat_count
    time_total = span * time_count
    groups = occupation.shape[0]
    slab = height // time_count
    narrow = span // lat_count
    exact = lax.Precision.HIGHEST
    lat_forward = angle_table(lateral_total, lateral_total, lateral_total, -1.0)
    lat_backward = angle_table(lateral_total, lateral_total, lateral_total, 1.0)
    lateral_turn = (jnp.cos(lateral_phase)[:, None], jnp.sin(lateral_phase)[:, None])
    small_back = angle_table(time_count, time_count, time_count, 1.0)
    twiddle_back = angle_table(time_count, span, time_total, 1.0)
    long_back = angle_table(span, span, span, 1.0)
    spectral_grid = spectral_phase.reshape(span, time_count).T
    spectral_turn = (jnp.cos(spectral_grid), jnp.sin(spectral_grid))
    bins = jnp.arange(bin_decay.shape[0], dtype=jnp.int32)
    onehot = (group_bin[:, None] == bins[None, :]).astype(jnp.float32)
    decay_rate = jnp.dot(onehot, bin_decay, precision=exact)
    detuning = jnp.dot(onehot, bin_detune, precision=exact)
    coupling = jnp.sqrt(-jnp.expm1(-2.0 * decay_rate))[:, None] * occupation
    lags = jnp.arange(STRETCH + 1, dtype=jnp.float32)[:, None]
    lag_powers = powers(decay_rate, detuning, lags)
    lag_grid = (
        jnp.arange(STRETCH, dtype=jnp.int32)[:, None]
        - jnp.arange(STRETCH, dtype=jnp.int32)[None, :]
    )
    inside = (lag_grid >= 0)[None]
    clipped = jnp.maximum(lag_grid, 0)
    leading = (lag_powers[0][1:].T, lag_powers[1][1:].T)
    trailing = (lag_powers[0][:STRETCH][::-1], lag_powers[1][:STRETCH][::-1])
    stretch_step = (lag_powers[0][STRETCH][:, None], lag_powers[1][STRETCH][:, None])
    device_step = powers(decay_rate, detuning, jnp.float32(span))
    weight = GAIN_SCALE / math.sqrt(groups)
    small_forward = angle_table(time_count, time_count, time_count, -1.0)
    twiddle_forward = angle_table(time_count, span, time_total, -1.0)
    long_forward = angle_table(span, span, span, -1.0)
    current = light_field
    block_toeplitz = (
        jnp.where(
            inside,
            jnp.take(
                jnp.dot(coupling.T, lag_powers[0][:STRETCH].T, precision=exact), clipped, axis=1
            ),
            0.0,
        ),
        jnp.where(
            inside,
            jnp.take(
                jnp.dot(coupling.T, lag_powers[1][:STRETCH].T, precision=exact), clipped, axis=1
            ),
            0.0,
        ),
    )
    for repeat in range(STEPS):
        diffract_stacked = current.reshape(2, height, lat_count, narrow)
        lateral_block = lax.all_to_all(
            diffract_stacked, "lat", split_axis=2, concat_axis=1, tiled=True
        )
        piece = (lateral_block[0, :, 0, :], lateral_block[1, :, 0, :])
        lateral_spectrum = complex_einsum("kx,xn->kn", lat_forward, piece)
        lateral_spectrum = complex_times(lateral_spectrum, lateral_turn)
        lateral_result = complex_einsum("xk,kn->xn", lat_backward, lateral_spectrum)
        lateral_joined = (
            jnp.stack([lateral_result[0], lateral_result[1]])[:, :, None, :] / lateral_total
        )
        diffract_turned = lax.all_to_all(
            lateral_joined, "lat", split_axis=1, concat_axis=2, tiled=True
        )
        stacked = diffract_turned.reshape(2, height, span).reshape(2, time_count, slab, span)
        rows = lax.all_to_all(stacked, "tm", split_axis=1, concat_axis=3, tiled=True)[:, 0]
        rows_here = rows.shape[1]
        grid = (
            rows[0].reshape(rows_here, time_count, span),
            rows[1].reshape(rows_here, time_count, span),
        )
        spectrum = time_forward(grid, small_forward, twiddle_forward, long_forward)
        spectrum = complex_times(spectrum, spectral_turn)
        result = time_inverse(spectrum, small_back, twiddle_back, long_back, time_total)
        joined = jnp.stack(
            [result[0].reshape(rows_here, time_total), result[1].reshape(rows_here, time_total)]
        )[:, None]
        turned = lax.all_to_all(joined, "tm", split_axis=3, concat_axis=1, tiled=True)
        current = turned.reshape(2, height, span)
        amplify_rows_here = current.shape[1]
        length = current.shape[2]
        count = length // STRETCH
        amplify_grid = (
            current[0].reshape(amplify_rows_here, count, STRETCH),
            current[1].reshape(amplify_rows_here, count, STRETCH),
        )
        direct = complex_einsum("xji,xci->xcj", block_toeplitz, amplify_grid)
        projected = complex_einsum("xci,ig->cgx", amplify_grid, trailing)
        stretch_ends = (coupling[None] * projected[0], coupling[None] * projected[1])

        def chain_step(running, ends):
            moved = complex_times(stretch_step, running)
            return ((moved[0] + ends[0], moved[1] + ends[1]), running)

        zero_state = jnp.zeros((groups, amplify_rows_here), jnp.float32)
        running, chain = lax.scan(chain_step, (zero_state, zero_state), stretch_ends)

        def combine(earlier, later):
            joint = complex_times((earlier[0], earlier[1]), (later[0], later[1]))
            carried = complex_times(
                (later[0][:, None], later[1][:, None]), (earlier[2], earlier[3])
            )
            return (joint[0], joint[1], carried[0] + later[2], carried[1] + later[3])

        identity = (
            jnp.ones((groups,), jnp.float32),
            jnp.zeros((groups,), jnp.float32),
            jnp.zeros_like(running[0]),
            jnp.zeros_like(running[1]),
        )
        prefix = carried_in(
            (device_step[0], device_step[1], running[0], running[1]), "tm", combine, identity
        )
        starts = powers(
            decay_rate, detuning, (jnp.arange(count, dtype=jnp.float32) * STRETCH)[:, None]
        )
        before = complex_times(
            (starts[0][:, :, None], starts[1][:, :, None]), (prefix[2][None], prefix[3][None])
        )
        states = (before[0] + chain[0], before[1] + chain[1])
        delayed = complex_einsum("cgx,gj->xcj", states, leading)
        summed_re = (direct[0] + delayed[0]).reshape(amplify_rows_here, length)
        summed_im = (direct[1] + delayed[1]).reshape(amplify_rows_here, length)
        current = jnp.stack([current[0] - weight * summed_im, current[1] + weight * summed_re])
    return current


LATS, TIMES, SIDE, BIN_COUNT = 4, 8, 256, 32
TOTAL = LATS * TIMES
WIDE = LATS * SIDE
LONG = TIMES * SIDE
ROWS = SIDE // TIMES
F32, BF16 = jnp.float32, jnp.bfloat16
MESH = pl.DeviceIdType.MESH


@functools.cache
def constants():
    j = np.arange(SIDE)
    w = np.exp(-2j * np.pi * (np.outer(j, j) % SIDE) / SIDE)
    big = np.block([[w.real, w.imag], [-w.imag, w.real]]).astype(np.float32)
    big_hi = big.astype(jnp.bfloat16)
    big_lo = (big - big_hi.astype(np.float32)).astype(jnp.bfloat16)
    tw8 = np.exp(-2j * np.pi * np.outer(np.arange(TIMES), j) / LONG)
    tau = np.exp(-1j * np.pi * np.arange(LONG).reshape(TIMES, SIDE) / LONG)
    tau2 = np.exp(-1j * np.pi * j / SIDE)[None]
    rows = np.concatenate([tw8, tau, tau2, np.zeros((7, SIDE))])
    rows = np.stack([rows.real, rows.imag]).astype(np.float32)
    tw4 = np.exp(-2j * np.pi * np.outer(j, np.arange(LATS)) / WIDE)
    cols = np.concatenate([tw4.real, tw4.imag], axis=1).astype(np.float32)
    return (big_hi, big_lo, rows, cols)


def halves(x):
    hi = x.astype(BF16)
    return hi, (x - hi.astype(F32)).astype(BF16)


def dot(a, b):
    return jnp.dot(a, b, preferred_element_type=F32)


def dot3(a, b):
    return dot(a[0], b[0]) + dot(a[1], b[0]) + dot(a[0], b[1])


def cmul(a, b):
    return (a[0] * b[0] - a[1] * b[1], a[0] * b[1] + a[1] * b[0])


def conj(a):
    return (a[0], -a[1])


def small_fft(items, sign):
    count = len(items)
    if count == 1:
        return items
    even, odd = small_fft(items[0::2], sign), small_fft(items[1::2], sign)
    low, high = [], []
    for k in range(count // 2):
        re, im = odd[k]
        if 8 * k == count:
            r = math.sqrt(0.5)
            re, im = (re - sign * im) * r, (im + sign * re) * r
        elif 4 * k == count:
            re, im = -sign * im, sign * re
        elif 8 * k == 3 * count:
            r = math.sqrt(0.5)
            re, im = (-re - sign * im) * r, (-im + sign * re) * r
        low.append((even[k][0] + re, even[k][1] + im))
        high.append((even[k][0] - re, even[k][1] - im))
    return low + high


def lane_iota(shape):
    return lax.broadcasted_iota(jnp.int32, shape, len(shape) - 1)


def roll(x, shift):
    shift = shift % 128
    return pltpu.roll(x, shift, axis=x.ndim - 1) if shift else x


def pack(re, im):
    tiles = []
    first = lane_iota((re.shape[0], 128)) < 64
    for p in range(re.shape[1] // 128):
        a, b = re[:, 128 * p : 128 * p + 128], im[:, 128 * p : 128 * p + 128]
        tiles.append(jnp.where(first, a, roll(b, 64)))
        tiles.append(jnp.where(first, roll(a, 64), b))
    return tiles


def unpack(tiles):
    first = lane_iota(tiles[0].shape) < 64
    re, im = [], []
    for p in range(0, len(tiles), 2):
        a, b = tiles[p], tiles[p + 1]
        re.append(jnp.where(first, a, roll(b, 64)))
        im.append(jnp.where(first, roll(a, 64), b))
    return jnp.concatenate(re, axis=1), jnp.concatenate(im, axis=1)


def turn(x):
    first = lane_iota(x.shape) < 64
    y = roll(x, 64)
    return jnp.where(first, -y, y)


def kernel(
    lf, latp, specp, occ, dec_ref, det_ref, gb_ref, wh, wl, rows_ref, cols_ref,
    out,
    s1, r1, s2, r2, s3, r3, s4, r4,
    tw_c, tw_s, ph_c, ph_s, ct, q_hi, q_lo, p_hi, p_lo, kev, kod, kfe, kfo, spec,
    ss1, rs1, ss2, rs2, ss3, rs3, ss4, rs4,
):
    l, m = lax.axis_index("lat"), lax.axis_index("tm")
    me = l * TIMES + m
    weight = GAIN_SCALE / math.sqrt(occ.shape[0])

    def other(d):
        t = lax.rem(me + d, TOTAL)
        return t, t // TIMES, lax.rem(t, TIMES)

    barrier = pltpu.get_barrier_semaphore()

    def greet(d, carry):
        t, tl, tm = other(d)
        pl.semaphore_signal(barrier, inc=1, device_id=(tl, tm), device_id_type=MESH)
        return carry

    lax.fori_loop(1, TOTAL, greet, 0)

    def remote(src, dst, send, recv, tl, tm):
        return pltpu.make_async_remote_copy(
            src_ref=src, dst_ref=dst, send_sem=send, recv_sem=recv,
            device_id=(tl, tm), device_id_type=MESH,
        )

    def lat_send(s, r, ss, rs, d):
        t = lax.rem(l + d, LATS)
        return remote(s.at[t], r.at[l], ss.at[t], rs.at[l], t, m)

    def lat_recv(s, r, ss, rs, d):
        t = lax.rem(l + d, LATS)
        return remote(s.at[t], r.at[t], ss.at[t], rs.at[t], t, m)

    def to_rows(d):
        t, tl, tm = other(d)
        src = s2.at[tl, pl.ds(pl.multiple_of(tm * ROWS, ROWS), ROWS)]
        return remote(src, r2.at[m, l], ss2.at[t], rs2.at[me], tl, tm)

    def from_columns(d):
        t, tl, tm = other(d)
        return remote(r2.at[tm, tl], r2.at[tm, tl], ss2.at[t], rs2.at[t], tl, tm)

    def to_columns(d):
        t, tl, tm = other(d)
        return remote(s3.at[tm, tl], r3.at[l, m], ss3.at[t], rs3.at[me], tl, tm)

    def from_rows(d):
        t, tl, tm = other(d)
        return remote(r3.at[tl, tm], r3.at[tl, tm], ss3.at[t], rs3.at[t], tl, tm)

    def each(make, act):
        def body(d, carry):
            act(make(d))
            return carry

        lax.fori_loop(1, TOTAL, body, 0)

    for t, tile in enumerate(pack(lf[0], lf[1])):
        s1[t] = tile
    pl.semaphore_wait(barrier, TOTAL - 1)
    first = [lat_send(s1, r1, ss1, rs1, d) for d in range(1, LATS)]
    for copy in first:
        copy.start()
    r1[l] = s1[l]

    whole = (SIDE, 128)
    sign = jnp.where(lane_iota(whole) < 64, -1.0, 1.0)
    phase = latp[...]
    turn_c, turn_s = jnp.cos(phase) * (1.0 / WIDE), jnp.sin(phase) * (1.0 / WIDE)
    for k in range(LATS):
        tw_c[k] = jnp.broadcast_to(cols_ref[:, k : k + 1], whole)
        tw_s[k] = jnp.broadcast_to(cols_ref[:, LATS + k : LATS + k + 1], whole) * sign
        ph_c[k] = jnp.broadcast_to(turn_c[:, k : k + 1], whole)
        ph_s[k] = jnp.broadcast_to(turn_s[:, k : k + 1], whole) * sign
    spec[0] = jnp.cos(specp[...]) * (1.0 / LONG)
    spec[1] = jnp.sin(specp[...]) * (1.0 / LONG)

    dec_row, det_row = dec_ref[...], det_ref[...]
    square = (BIN_COUNT, BIN_COUNT)
    eye = lax.broadcasted_iota(jnp.int32, square, 0) == lax.broadcasted_iota(jnp.int32, square, 1)
    dec_col = jnp.sum(jnp.where(eye, dec_row, 0.0), axis=1, keepdims=True)
    det_col = jnp.sum(jnp.where(eye, det_row, 0.0), axis=1, keepdims=True)
    lag = lane_iota((BIN_COUNT, SIDE)).astype(F32)

    def power(exponent, rate, angle):
        size = jnp.exp(-rate * exponent)
        return size * jnp.cos(angle * exponent), -size * jnp.sin(angle * exponent)

    def bin_of(q):
        part = lax.rem(q, 64)
        within = lax.rem(part, 16)
        return jnp.where(within < 8, (part // 16) * 8 + within, -1)

    q_row = lax.broadcasted_iota(jnp.int32, (128, BIN_COUNT), 0)
    spread = (bin_of(q_row) == lane_iota((128, BIN_COUNT))).astype(BF16)
    q_lane = lane_iota((BIN_COUNT, 128))
    pick = bin_of(q_lane) == lax.broadcasted_iota(jnp.int32, (BIN_COUNT, 128), 0)
    dec_lane = jnp.sum(jnp.where(pick, dec_col, 0.0), axis=0, keepdims=True)
    det_lane = jnp.sum(jnp.where(pick, det_col, 0.0), axis=0, keepdims=True)
    ahead = power(lag, dec_col, det_col)
    is_re = lax.broadcasted_iota(jnp.int32, (128, SIDE), 0) < 64
    (re_hi, re_lo), (im_hi, im_lo) = halves(ahead[0]), halves(ahead[1])
    for ref, re, im in ((q_hi, re_hi, im_hi), (q_lo, re_lo, im_lo)):
        re, im = dot(spread, re), dot(spread, im)
        ref[:, :SIDE] = jnp.where(is_re, re, -im).astype(BF16)
        ref[:, SIDE:] = jnp.where(is_re, im, re).astype(BF16)
    lane = lane_iota((BIN_COUNT, SIDE))
    inner = lax.rem(lane, 16)
    held = jnp.where(inner < 8, (lane // 64) * 8 + inner, -1)
    held = held == lax.broadcasted_iota(jnp.int32, (BIN_COUNT, SIDE), 0)
    held_b = held.astype(BF16)
    step_dec = jnp.sum(jnp.where(held, dec_col, 0.0), axis=0, keepdims=True)
    step_det = jnp.sum(jnp.where(held, det_col, 0.0), axis=0, keepdims=True)
    behind = power(SIDE - lag, dec_col, det_col)
    for ref, which in ((p_hi, 0), (p_lo, 1)):
        re = halves(behind[0])[which].astype(F32).T.astype(BF16)
        im = halves(behind[1])[which].astype(F32).T.astype(BF16)
        re, im = dot(re, held_b), dot(im, held_b)
        ref[:SIDE, :SIDE] = re.astype(BF16)
        ref[:SIDE, SIDE:] = im.astype(BF16)
        ref[SIDE:, :SIDE] = (-im).astype(BF16)
        ref[SIDE:, SIDE:] = re.astype(BF16)
    y = 2.0 * dec_lane
    series = jnp.ones_like(y)
    for n in range(9, 1, -1):
        series = 1.0 - series * y * (1.0 / n)
    drive = jnp.sqrt(y * series)
    bins_here = bin_of(lax.broadcasted_iota(jnp.int32, (128, occ.shape[0]), 0))
    member = (bins_here == gb_ref[...]).astype(BF16)
    occ_hi, occ_lo = halves(occ[...])
    ct[...] = (dot(member, occ_hi) + dot(member, occ_lo)).T * drive

    def wide_dft(re, im):
        x = halves(jnp.concatenate([re, im], axis=1))
        y = dot3(x, (wh[...], wl[...]))
        return y[:, :SIDE], y[:, SIDE:]

    def wide_inverse(re, im):
        return conj(wide_dft(re, -im))

    def row(k):
        return rows_ref[0, k : k + 1, :], rows_ref[1, k : k + 1, :]

    def stack(items):
        return tuple(jnp.concatenate([item[c] for item in items], axis=0) for c in (0, 1))

    def unstack(value):
        return [tuple(v[ROWS * k : ROWS * (k + 1)] for v in value) for k in range(TIMES)]

    def time_dft(items):
        items = small_fft(items, -1)
        return wide_dft(*stack([cmul(item, row(k)) for k, item in enumerate(items)]))

    def time_inverse_dft(value):
        items = unstack(wide_inverse(*value))
        return small_fft([cmul(item, conj(row(k))) for k, item in enumerate(items)], 1)

    def twist(items, back):
        rows = [row(TIMES + k) for k in range(TIMES)]
        return [cmul(x, conj(r) if back else r) for x, r in zip(items, rows)]

    def column_dft(x, back):
        hi, lo = halves(x)
        w = (wh[:, :SIDE], wl[:, :SIDE])
        y = dot3(w, (hi, lo))
        tops, bottoms = y[:SIDE], y[SIDE:]
        parts = []
        for k in range(x.shape[1] // 128):
            top, bottom = tops[:, 128 * k : 128 * k + 128], bottoms[:, 128 * k : 128 * k + 128]
            parts.append(top + turn(bottom) if back else top - turn(bottom))
        return parts

    def diffract(groups):
        spectrum = []
        for x in groups:
            a, b, c, d = x[0] + x[2], x[0] - x[2], x[1] + x[3], turn(x[1] - x[3])
            for k, y in enumerate((a + c, b - d, a - c, b + d)):
                spectrum.append(y * tw_c[k] + roll(y, 64) * tw_s[k] if k else y)
        spectrum = column_dft(jnp.concatenate(spectrum, axis=1), False)
        spectrum = [
            y * ph_c[i % LATS] + roll(y, 64) * ph_s[i % LATS] for i, y in enumerate(spectrum)
        ]
        result = column_dft(jnp.concatenate(spectrum, axis=1), True)
        done = []
        for g in range(len(groups)):
            x = []
            for k in range(LATS):
                y = result[g * LATS + k]
                x.append(y * tw_c[k] - roll(y, 64) * tw_s[k] if k else y)
            a, b, c, d = x[0] + x[2], x[0] - x[2], x[1] + x[3], turn(x[1] - x[3])
            done.append([a + c, b + d, a - c, b - d])
        return done

    for d in range(1, LATS):
        lat_recv(s1, r1, ss1, rs1, d).wait_recv()
    for a, tile in enumerate(diffract([[r1[a] for a in range(LATS)]])[0]):
        s2[a] = tile
    each(to_rows, lambda copy: copy.start())
    r2[m, l] = s2[l, pl.ds(pl.multiple_of(m * ROWS, ROWS), ROWS)]

    mine = ct[pl.ds(pl.multiple_of(m * ROWS, ROWS), ROWS), :]
    first_half = lane_iota((1, 128)) < 64
    scaled = []
    for k in range(TIMES):
        far = power(float(SIDE * k), dec_lane, det_lane)
        scaled.append(mine * jnp.where(first_half, far[0], far[1]))
    q = (q_hi[...], q_lo[...])
    response = dot3(halves(jnp.concatenate(scaled, axis=0)), q)
    response = unstack((response[:, :SIDE], response[:, SIDE:]))
    even = time_dft(response)
    kev[0] = LONG * (1.0 - (0.5 * weight) * even[1])
    kev[1] = (LONG * 0.5 * weight) * even[0]
    odd = time_dft(twist(response, False))
    kod[0] = (-0.5 * weight / LONG) * odd[1]
    kod[1] = (0.5 * weight / LONG) * odd[0]

    each(from_columns, lambda copy: copy.wait_recv())
    field = []
    for k in range(TIMES):
        field.append(unpack([r2[k, a] for a in range(LATS)]))
    turn_row = stack([
        tuple(jnp.broadcast_to(spec[c, k : k + 1, :], (ROWS, SIDE)) for c in (0, 1))
        for k in range(TIMES)
    ])
    once = cmul(time_dft(field), turn_row)
    twisted = time_dft(twist(time_inverse_dft(once), False))
    twisted = time_inverse_dft(cmul(twisted, (kod[0], kod[1])))
    late = time_dft(twist(twisted, True))
    straight = cmul(once, (kev[0], kev[1]))
    once = cmul((straight[0] + late[0], straight[1] + late[1]), turn_row)
    field = time_inverse_dft(once)
    flat = stack(field)
    ends = dot3(halves(jnp.concatenate(flat, axis=1)), (p_hi[...], p_lo[...]))
    ends = unstack((ends[:, :SIDE], ends[:, SIDE:]))
    step = power(float(SIDE), step_dec, step_det)
    state = (jnp.zeros((ROWS, SIDE), F32), jnp.zeros((ROWS, SIDE), F32))
    slot = lax.rem(lane_iota((8, SIDE)) // 16, 4)
    for k in range(TIMES):
        folded = []
        for c in (0, 1):
            total = jnp.zeros((8, SIDE), F32)
            for g in range(4):
                total = jnp.where(slot == g, state[c][8 * g : 8 * g + 8], total)
            folded.append(total)
        tiles, extra = pack(*field[k]), pack(*folded)
        for a in range(LATS):
            s3[k, a, :ROWS, :] = tiles[a]
            s3[k, a, ROWS:, :] = extra[a]
        moved = cmul(state, step)
        state = (moved[0] + ends[k][0], moved[1] + ends[k][1])
    each(to_columns, lambda copy: copy.start())
    r3[l, m] = s3[m, l]

    t2 = row(2 * TIMES)
    q = (q_hi[...], q_lo[...])
    response = dot3(halves(jnp.where(lane_iota(whole) < 64, ct[...], 0.0)), q)
    response = (response[:, :SIDE], response[:, SIDE:])
    even, odd = wide_dft(*response), wide_dft(*cmul(response, t2))
    gain = 0.5 * weight / SIDE
    kfe[0], kfe[1] = -gain * even[1], gain * even[0]
    kfo[0], kfo[1] = -gain * odd[1], gain * odd[0]

    each(from_rows, lambda copy: copy.wait_recv())
    tiles, states = [], []
    for a in range(LATS):
        tiles.append(r3[a, :, :ROWS, :].reshape(SIDE, 128))
        extra = r3[a, :, ROWS:, :].reshape(8 * TIMES, 128)
        extra = [roll(extra, -16 * g).reshape(TIMES, 8, 128) for g in range(4)]
        states.append(jnp.stack(extra, axis=1).reshape(SIDE, 128))
    tiles, states = diffract([tiles, states])
    slot = lax.rem(lane_iota((ROWS, 128)), 64) // 8
    for a in range(LATS):
        s4[a, :SIDE, :] = tiles[a]
        total = jnp.zeros((ROWS, 128), F32)
        for g in range(8):
            total = jnp.where(slot == g, roll(states[a][ROWS * g : ROWS * (g + 1)], 8 * g), total)
        s4[a, SIDE:, :] = total
    last = [lat_send(s4, r4, ss4, rs4, d) for d in range(1, LATS)]
    for copy in last:
        copy.start()
    r4[l] = s4[l]
    for d in range(1, LATS):
        lat_recv(s4, r4, ss4, rs4, d).wait_recv()

    field = unpack([r4[a, :SIDE, :] for a in range(LATS)])
    slot = lax.rem(lane_iota((ROWS, 128)), 64) // 16
    carried = []
    for g in range(8):
        total = jnp.zeros((ROWS, 128), F32)
        for a in range(LATS):
            total = jnp.where(slot == a, roll(r4[a, SIDE:, :], 16 * a - 8 * g), total)
        carried.append(total)
    carried = halves(jnp.concatenate(carried, axis=0) * ct[...])
    carried = dot3(carried, (q_hi[...], q_lo[...]))
    even = wide_inverse(*cmul(wide_dft(*field), (kfe[0], kfe[1])))
    odd = wide_inverse(*cmul(wide_dft(*cmul(field, t2)), (kfo[0], kfo[1])))
    odd = cmul(odd, conj(t2))
    out[0] = field[0] + even[0] + odd[0] - weight * carried[:, SIDE:]
    out[1] = field[1] + even[1] + odd[1] + weight * carried[:, :SIDE]

    for copy in first + last:
        copy.wait_send()
    each(to_rows, lambda copy: copy.wait_send())
    each(to_columns, lambda copy: copy.wait_send())


def fused(light_field, lateral_phase, spectral_phase, occupation, bin_decay, bin_detune, group_bin):
    tile = (SIDE, 128)
    vmem, sems = pltpu.VMEM, pltpu.SemaphoreType.DMA
    exchange = [
        vmem((LATS,) + tile, F32), vmem((LATS,) + tile, F32),
        vmem((LATS,) + tile, F32), vmem((TIMES, LATS, ROWS, 128), F32),
        vmem((TIMES, LATS, ROWS + 8, 128), F32), vmem((LATS, TIMES, ROWS + 8, 128), F32),
        vmem((LATS, SIDE + ROWS, 128), F32), vmem((LATS, SIDE + ROWS, 128), F32),
    ]
    tables = [vmem((LATS,) + tile, F32)] * 4 + [vmem(tile, F32)]
    tables += [vmem((128, 2 * SIDE), BF16)] * 2 + [vmem((2 * SIDE, 2 * SIDE), BF16)] * 2
    tables += [vmem((2, SIDE, SIDE), F32)] * 4 + [vmem((2, TIMES, SIDE), F32)]
    semaphores = [sems((LATS,))] * 2 + [sems((TOTAL,))] * 4 + [sems((LATS,))] * 2
    return pl.pallas_call(
        kernel,
        out_shape=jax.ShapeDtypeStruct(light_field.shape, F32),
        in_specs=[pl.BlockSpec(memory_space=pltpu.VMEM)] * 11,
        out_specs=pl.BlockSpec(memory_space=pltpu.VMEM),
        scratch_shapes=exchange + tables + semaphores,
        compiler_params=pltpu.CompilerParams(
            collective_id=0, has_side_effects=True, vmem_limit_bytes=50 * 1024 * 1024
        ),
    )(
        light_field,
        lateral_phase.reshape(SIDE, LATS),
        spectral_phase.reshape(SIDE, TIMES).T,
        occupation,
        bin_decay[None],
        bin_detune[None],
        group_bin[None],
        *[jnp.asarray(c) for c in constants()],
    )


def solution(mesh):
    def local(light_field, *rest):
        fits = (lax.axis_size("lat"), lax.axis_size("tm")) == (LATS, TIMES)
        fits = fits and light_field.shape == (2, SIDE, SIDE)
        fits = fits and rest[2].shape == (128, SIDE) and rest[3].shape == (BIN_COUNT,)
        return (fused if fits else on_device)(light_field, *rest)

    return jax.shard_map(
        local,
        mesh=mesh,
        in_specs=(P(None, "lat", "tm"), P(), P(), P(None, "lat"), P(), P(), P()),
        out_specs=P(None, "lat", "tm"),
        check_vma=False,
    )
```

```python
import functools
import math

import jax
import jax.numpy as jnp
import numpy as np
from jax import lax
from jax.experimental import pallas as pl
from jax.experimental.pallas import tpu as pltpu
from jax.sharding import PartitionSpec as P

STRETCH = 128
STEPS = 2


GAIN_SCALE = 0.5


def carried_in(value, axis, join, neutral):
    count, mine = (lax.axis_size(axis), lax.axis_index(axis))
    pieces = jax.tree.map(lambda part: lax.all_gather(part, axis), value)
    so_far = jax.tree.map(
        lambda part, zero: jnp.full_like(part, 0) + jnp.asarray(zero, part.dtype), value, neutral
    )

    def lap(position, so_far):
        longer = join(so_far, jax.tree.map(lambda part: part[position], pieces))
        return jax.tree.map(lambda new, old: jnp.where(position < mine, new, old), longer, so_far)

    return lax.fori_loop(0, count - 1, lap, so_far)


def complex_einsum(form, left, right):
    exact = lax.Precision.HIGHEST
    real_part = jnp.einsum(form, left[0], right[0], precision=exact) - jnp.einsum(
        form, left[1], right[1], precision=exact
    )
    imag_part = jnp.einsum(form, left[0], right[1], precision=exact) + jnp.einsum(
        form, left[1], right[0], precision=exact
    )
    return (real_part, imag_part)


def complex_times(left, right):
    return (left[0] * right[0] - left[1] * right[1], left[0] * right[1] + left[1] * right[0])


def angle_table(height, breadth, modulus, sign):
    first = jnp.arange(height, dtype=jnp.int32)[:, None]
    second = jnp.arange(breadth, dtype=jnp.int32)[None, :]
    turns = (first * second % modulus).astype(jnp.float32) * (2.0 * math.pi / modulus)
    return (jnp.cos(turns), sign * jnp.sin(turns))


def time_forward(grid, small_table, twiddle, long_table):
    mixed = complex_einsum("ka,rab->rkb", small_table, grid)
    mixed = complex_times(mixed, twiddle)
    return complex_einsum("rkb,bq->rkq", mixed, long_table)


def time_inverse(spectrum, small_table, twiddle, long_table, length):
    mixed = complex_einsum("rkq,qb->rkb", spectrum, long_table)
    mixed = complex_times(mixed, twiddle)
    result = complex_einsum("ak,rkb->rab", small_table, mixed)
    return (result[0] / length, result[1] / length)


def powers(decay_rate, detuning, exponent):
    magnitude = jnp.exp(-decay_rate * exponent)
    phase_angle = detuning * exponent
    return (magnitude * jnp.cos(phase_angle), -magnitude * jnp.sin(phase_angle))


def on_device(
    light_field, lateral_phase, spectral_phase, occupation, bin_decay, bin_detune, group_bin
):
    lat_count = lax.axis_size("lat")
    time_count = lax.axis_size("tm")
    height = light_field.shape[1]
    span = light_field.shape[2]
    lateral_total = height * lat_count
    time_total = span * time_count
    groups = occupation.shape[0]
    slab = height // time_count
    narrow = span // lat_count
    exact = lax.Precision.HIGHEST
    lat_forward = angle_table(lateral_total, lateral_total, lateral_total, -1.0)
    lat_backward = angle_table(lateral_total, lateral_total, lateral_total, 1.0)
    lateral_turn = (jnp.cos(lateral_phase)[:, None], jnp.sin(lateral_phase)[:, None])
    small_back = angle_table(time_count, time_count, time_count, 1.0)
    twiddle_back = angle_table(time_count, span, time_total, 1.0)
    long_back = angle_table(span, span, span, 1.0)
    spectral_grid = spectral_phase.reshape(span, time_count).T
    spectral_turn = (jnp.cos(spectral_grid), jnp.sin(spectral_grid))
    bins = jnp.arange(bin_decay.shape[0], dtype=jnp.int32)
    onehot = (group_bin[:, None] == bins[None, :]).astype(jnp.float32)
    decay_rate = jnp.dot(onehot, bin_decay, precision=exact)
    detuning = jnp.dot(onehot, bin_detune, precision=exact)
    coupling = jnp.sqrt(-jnp.expm1(-2.0 * decay_rate))[:, None] * occupation
    lags = jnp.arange(STRETCH + 1, dtype=jnp.float32)[:, None]
    lag_powers = powers(decay_rate, detuning, lags)
    lag_grid = (
        jnp.arange(STRETCH, dtype=jnp.int32)[:, None]
        - jnp.arange(STRETCH, dtype=jnp.int32)[None, :]
    )
    inside = (lag_grid >= 0)[None]
    clipped = jnp.maximum(lag_grid, 0)
    leading = (lag_powers[0][1:].T, lag_powers[1][1:].T)
    trailing = (lag_powers[0][:STRETCH][::-1], lag_powers[1][:STRETCH][::-1])
    stretch_step = (lag_powers[0][STRETCH][:, None], lag_powers[1][STRETCH][:, None])
    device_step = powers(decay_rate, detuning, jnp.float32(span))
    weight = GAIN_SCALE / math.sqrt(groups)
    small_forward = angle_table(time_count, time_count, time_count, -1.0)
    twiddle_forward = angle_table(time_count, span, time_total, -1.0)
    long_forward = angle_table(span, span, span, -1.0)
    current = light_field
    block_toeplitz = (
        jnp.where(
            inside,
            jnp.take(
                jnp.dot(coupling.T, lag_powers[0][:STRETCH].T, precision=exact), clipped, axis=1
            ),
            0.0,
        ),
        jnp.where(
            inside,
            jnp.take(
                jnp.dot(coupling.T, lag_powers[1][:STRETCH].T, precision=exact), clipped, axis=1
            ),
            0.0,
        ),
    )
    for repeat in range(STEPS):
        diffract_stacked = current.reshape(2, height, lat_count, narrow)
        lateral_block = lax.all_to_all(
            diffract_stacked, "lat", split_axis=2, concat_axis=1, tiled=True
        )
        piece = (lateral_block[0, :, 0, :], lateral_block[1, :, 0, :])
        lateral_spectrum = complex_einsum("kx,xn->kn", lat_forward, piece)
        lateral_spectrum = complex_times(lateral_spectrum, lateral_turn)
        lateral_result = complex_einsum("xk,kn->xn", lat_backward, lateral_spectrum)
        lateral_joined = (
            jnp.stack([lateral_result[0], lateral_result[1]])[:, :, None, :] / lateral_total
        )
        diffract_turned = lax.all_to_all(
            lateral_joined, "lat", split_axis=1, concat_axis=2, tiled=True
        )
        stacked = diffract_turned.reshape(2, height, span).reshape(2, time_count, slab, span)
        rows = lax.all_to_all(stacked, "tm", split_axis=1, concat_axis=3, tiled=True)[:, 0]
        rows_here = rows.shape[1]
        grid = (
            rows[0].reshape(rows_here, time_count, span),
            rows[1].reshape(rows_here, time_count, span),
        )
        spectrum = time_forward(grid, small_forward, twiddle_forward, long_forward)
        spectrum = complex_times(spectrum, spectral_turn)
        result = time_inverse(spectrum, small_back, twiddle_back, long_back, time_total)
        joined = jnp.stack(
            [result[0].reshape(rows_here, time_total), result[1].reshape(rows_here, time_total)]
        )[:, None]
        turned = lax.all_to_all(joined, "tm", split_axis=3, concat_axis=1, tiled=True)
        current = turned.reshape(2, height, span)
        amplify_rows_here = current.shape[1]
        length = current.shape[2]
        count = length // STRETCH
        amplify_grid = (
            current[0].reshape(amplify_rows_here, count, STRETCH),
            current[1].reshape(amplify_rows_here, count, STRETCH),
        )
        direct = complex_einsum("xji,xci->xcj", block_toeplitz, amplify_grid)
        projected = complex_einsum("xci,ig->cgx", amplify_grid, trailing)
        stretch_ends = (coupling[None] * projected[0], coupling[None] * projected[1])

        def chain_step(running, ends):
            moved = complex_times(stretch_step, running)
            return ((moved[0] + ends[0], moved[1] + ends[1]), running)

        zero_state = jnp.zeros((groups, amplify_rows_here), jnp.float32)
        running, chain = lax.scan(chain_step, (zero_state, zero_state), stretch_ends)

        def combine(earlier, later):
            joint = complex_times((earlier[0], earlier[1]), (later[0], later[1]))
            carried = complex_times(
                (later[0][:, None], later[1][:, None]), (earlier[2], earlier[3])
            )
            return (joint[0], joint[1], carried[0] + later[2], carried[1] + later[3])

        identity = (
            jnp.ones((groups,), jnp.float32),
            jnp.zeros((groups,), jnp.float32),
            jnp.zeros_like(running[0]),
            jnp.zeros_like(running[1]),
        )
        prefix = carried_in(
            (device_step[0], device_step[1], running[0], running[1]), "tm", combine, identity
        )
        starts = powers(
            decay_rate, detuning, (jnp.arange(count, dtype=jnp.float32) * STRETCH)[:, None]
        )
        before = complex_times(
            (starts[0][:, :, None], starts[1][:, :, None]), (prefix[2][None], prefix[3][None])
        )
        states = (before[0] + chain[0], before[1] + chain[1])
        delayed = complex_einsum("cgx,gj->xcj", states, leading)
        summed_re = (direct[0] + delayed[0]).reshape(amplify_rows_here, length)
        summed_im = (direct[1] + delayed[1]).reshape(amplify_rows_here, length)
        current = jnp.stack([current[0] - weight * summed_im, current[1] + weight * summed_re])
    return current


LATS, TIMES, SIDE, BIN_COUNT = 4, 8, 256, 32
TOTAL = LATS * TIMES
WIDE = LATS * SIDE
LONG = TIMES * SIDE
ROWS = SIDE // TIMES
PART = ROWS // 2
F32, BF16 = jnp.float32, jnp.bfloat16
MESH = pl.DeviceIdType.MESH


@functools.cache
def constants():
    j = np.arange(SIDE)
    w = np.exp(-2j * np.pi * (np.outer(j, j) % SIDE) / SIDE)
    big = np.block([[w.real, w.imag], [-w.imag, w.real]]).astype(np.float32)
    big_hi = big.astype(jnp.bfloat16)
    big_lo = (big - big_hi.astype(np.float32)).astype(jnp.bfloat16)
    tw8 = np.exp(-2j * np.pi * np.outer(np.arange(TIMES), j) / LONG)
    tau = np.exp(-1j * np.pi * np.arange(LONG).reshape(TIMES, SIDE) / LONG)
    tau2 = np.exp(-1j * np.pi * j / SIDE)[None]
    rows = np.concatenate([tw8, tau, tau2, np.zeros((7, SIDE))])
    rows = np.stack([rows.real, rows.imag]).astype(np.float32)
    tw4 = np.exp(-2j * np.pi * np.outer(j, np.arange(LATS)) / WIDE)
    cols = np.concatenate([tw4.real, tw4.imag], axis=1).astype(np.float32)
    return (big_hi, big_lo, rows, cols)


def halves(x):
    hi = x.astype(BF16)
    return hi, (x - hi.astype(F32)).astype(BF16)


def dot(a, b):
    return jnp.dot(a, b, preferred_element_type=F32)


def dot3(a, b):
    return dot(a[0], b[0]) + dot(a[1], b[0]) + dot(a[0], b[1])


def cmul(a, b):
    return (a[0] * b[0] - a[1] * b[1], a[0] * b[1] + a[1] * b[0])


def conj(a):
    return (a[0], -a[1])


def small_fft(items, sign):
    count = len(items)
    if count == 1:
        return items
    even, odd = small_fft(items[0::2], sign), small_fft(items[1::2], sign)
    low, high = [], []
    for k in range(count // 2):
        re, im = odd[k]
        if 8 * k == count:
            r = math.sqrt(0.5)
            re, im = (re - sign * im) * r, (im + sign * re) * r
        elif 4 * k == count:
            re, im = -sign * im, sign * re
        elif 8 * k == 3 * count:
            r = math.sqrt(0.5)
            re, im = (-re - sign * im) * r, (-im + sign * re) * r
        low.append((even[k][0] + re, even[k][1] + im))
        high.append((even[k][0] - re, even[k][1] - im))
    return low + high


def lane_iota(shape):
    return lax.broadcasted_iota(jnp.int32, shape, len(shape) - 1)


def roll(x, shift):
    shift = shift % 128
    return pltpu.roll(x, shift, axis=x.ndim - 1) if shift else x


def pack(re, im):
    tiles = []
    first = lane_iota((re.shape[0], 128)) < 64
    for p in range(re.shape[1] // 128):
        a, b = re[:, 128 * p : 128 * p + 128], im[:, 128 * p : 128 * p + 128]
        tiles.append(jnp.where(first, a, roll(b, 64)))
        tiles.append(jnp.where(first, roll(a, 64), b))
    return tiles


def unpack(tiles):
    first = lane_iota(tiles[0].shape) < 64
    re, im = [], []
    for p in range(0, len(tiles), 2):
        a, b = tiles[p], tiles[p + 1]
        re.append(jnp.where(first, a, roll(b, 64)))
        im.append(jnp.where(first, roll(a, 64), b))
    return jnp.concatenate(re, axis=1), jnp.concatenate(im, axis=1)


def turn(x):
    first = lane_iota(x.shape) < 64
    y = roll(x, 64)
    return jnp.where(first, -y, y)


def kernel(
    lf_hbm, latp, specp, occ_hbm, dec_ref, det_ref, gb_ref, wh_hbm, wl_hbm, rows_hbm, cols_hbm,
    out,
    s1, r1, s2, r2, s3a, r3a, s3b, r3b, s4, r4,
    tw_c, tw_s, ph_c, ph_s, ct, q_hi, q_lo, p_hi, p_lo, kev, kod, kfe, kfo, spec,
    lf, occ, wh, wl, rows_ref, cols_ref,
    ss1, rs1, ss2, rs2, ss3, rs3, ss4, rs4, load_sem,
):
    loads = []
    for i, (src, dst) in enumerate((
        (lf_hbm, lf), (cols_hbm, cols_ref), (wh_hbm, wh), (wl_hbm, wl), (occ_hbm, occ),
        (rows_hbm, rows_ref),
    )):
        loads.append(pltpu.make_async_copy(src, dst, load_sem.at[i]))
        loads[-1].start()
    l, m = lax.axis_index("lat"), lax.axis_index("tm")
    me = l * TIMES + m
    weight = GAIN_SCALE / math.sqrt(occ.shape[0])

    half = TIMES // 2

    def other(d):
        side = lax.rem(m // half + 1 + d // (TOTAL // 2), 2)
        tm = side * half + lax.rem(m + d, half)
        tl = lax.rem(l + lax.rem(d // half, LATS), LATS)
        return tl * TIMES + tm, tl, tm

    def each(act):
        act(0)

        def body(d, carry):
            act(d)
            act(d + TOTAL // 2)
            return carry

        lax.fori_loop(1, TOTAL // 2, body, 0)

    barrier = pltpu.get_barrier_semaphore()

    def greet(d):
        t, tl, tm = other(d)
        pl.semaphore_signal(barrier, inc=1, device_id=(tl, tm), device_id_type=MESH)

    each(greet)

    def remote(src, dst, send, recv, tl, tm):
        return pltpu.make_async_remote_copy(
            src_ref=src, dst_ref=dst, send_sem=send, recv_sem=recv,
            device_id=(tl, tm), device_id_type=MESH,
        )

    def lat_send(s, r, ss, rs, d):
        t = lax.rem(l + d, LATS)
        return remote(s.at[t], r.at[l], ss.at[t], rs.at[l], t, m)

    def lat_recv(s, r, ss, rs, d):
        t = lax.rem(l + d, LATS)
        return remote(s.at[t], r.at[t], ss.at[t], rs.at[t], t, m)

    def to_rows(h, d):
        t, tl, tm = other(d)
        src = s2.at[tl, pl.ds(pl.multiple_of(tm * ROWS + h * PART, PART), PART)]
        return remote(src, r2.at[h, m, l], ss2.at[h, t], rs2.at[h, me], tl, tm)

    def from_columns(h, d):
        t, tl, tm = other(d)
        return remote(r2.at[h, tm, tl], r2.at[h, tm, tl], ss2.at[h, t], rs2.at[h, t], tl, tm)

    s3, r3 = (s3a, s3b), (r3a, r3b)

    def to_columns(h, d):
        t, tl, tm = other(d)
        return remote(s3[h].at[tm, tl], r3[h].at[l, m], ss3.at[h, t], rs3.at[h, me], tl, tm)

    def from_rows(h, d):
        t, tl, tm = other(d)
        here = r3[h].at[tl, tm]
        return remote(here, here, ss3.at[h, t], rs3.at[h, t], tl, tm)

    loads[0].wait()
    for t, tile in enumerate(pack(lf[0], lf[1])):
        s1[t] = tile
    pl.semaphore_wait(barrier, TOTAL - 1)
    first = [lat_send(s1, r1, ss1, rs1, d) for d in range(1, LATS)]
    for copy in first:
        copy.start()
    r1[l] = s1[l]

    loads[1].wait()
    whole = (SIDE, 128)
    group = lax.rem(lane_iota(whole), 64) // 16
    sign = jnp.where(lane_iota(whole) < 64, -1.0, 1.0)
    phase = latp[...]
    turn_c, turn_s = jnp.cos(phase) * (1.0 / WIDE), jnp.sin(phase) * (1.0 / WIDE)
    for k in range(LATS):
        tw_c[k] = jnp.broadcast_to(cols_ref[:, k : k + 1], whole)
        tw_s[k] = jnp.broadcast_to(cols_ref[:, LATS + k : LATS + k + 1], whole) * sign
        ph_c[k] = jnp.broadcast_to(turn_c[:, k : k + 1], whole)
        ph_s[k] = jnp.broadcast_to(turn_s[:, k : k + 1], whole) * sign

    def wide_dft(re, im):
        x = halves(jnp.concatenate([re, im], axis=1))
        y = dot3(x, (wh[...], wl[...]))
        return y[:, :SIDE], y[:, SIDE:]

    def wide_inverse(re, im):
        return conj(wide_dft(re, -im))

    def row(k):
        return rows_ref[0, k : k + 1, :], rows_ref[1, k : k + 1, :]

    def stack(items):
        return tuple(jnp.concatenate([item[c] for item in items], axis=0) for c in (0, 1))

    def unstack(value):
        return [tuple(v[PART * k : PART * (k + 1)] for v in value) for k in range(TIMES)]

    def time_dft(items):
        items = small_fft(items, -1)
        return wide_dft(*stack([cmul(item, row(k)) for k, item in enumerate(items)]))

    def time_inverse_dft(value):
        items = unstack(wide_inverse(*value))
        return small_fft([cmul(item, conj(row(k))) for k, item in enumerate(items)], 1)

    def twist(items, back):
        rows = [row(TIMES + k) for k in range(TIMES)]
        return [cmul(x, conj(r) if back else r) for x, r in zip(items, rows)]

    def column_dft(x, low, high):
        w = [
            jnp.concatenate([ref[low:high, :SIDE], ref[SIDE + low : SIDE + high, :SIDE]], axis=0)
            for ref in (wh, wl)
        ]
        y = dot3(w, halves(x))
        count = high - low
        return [
            (y[:count, k : k + 128], y[count:, k : k + 128]) for k in range(0, x.shape[1], 128)
        ]

    def lateral_spectrum(x, states):
        spectrum = []
        for x in (x, states) if states else (x,):
            a, b, c, d = x[0] + x[2], x[0] - x[2], x[1] + x[3], turn(x[1] - x[3])
            for k, y in enumerate((a + c, b - d, a - c, b + d)):
                spectrum.append(y * tw_c[k] + roll(y, 64) * tw_s[k] if k else y)
        turns = [(ph_c[k], ph_s[k]) for k in range(LATS)]
        if states:
            tile, across, along = spectrum[LATS], turns[0][0], turns[0][1]
            for k in range(1, LATS):
                tile = jnp.where(group == k, roll(spectrum[LATS + k], 16 * k), tile)
                across = jnp.where(group == k, turns[k][0], across)
                along = jnp.where(group == k, turns[k][1], along)
            spectrum[LATS:] = [tile]
            turns.append((across, along))
        spectrum = column_dft(jnp.concatenate(spectrum, axis=1), 0, SIDE)
        done = []
        for (top, bottom), (across, along) in zip(spectrum, turns):
            y = top - turn(bottom)
            done.append(y * across + roll(y, 64) * along)
        return jnp.concatenate(done, axis=1)

    def lateral_inverse(spectrum, low, high):
        result = [top + turn(bottom) for top, bottom in column_dft(spectrum, low, high)]
        groups = [result[:LATS]]
        if len(result) > LATS:
            groups.append([roll(result[LATS], -16 * k) for k in range(LATS)])
        done = []
        for result in groups:
            x = []
            for k, y in enumerate(result):
                if k:
                    y = y * tw_c[k, low:high, :] - roll(y, 64) * tw_s[k, low:high, :]
                x.append(y)
            a, b, c, d = x[0] + x[2], x[0] - x[2], x[1] + x[3], turn(x[1] - x[3])
            done.append([a + c, b + d, a - c, b - d])
        return done

    loads[2].wait()
    loads[3].wait()
    for d in range(1, LATS):
        lat_recv(s1, r1, ss1, rs1, d).wait_recv()
    spectrum = lateral_spectrum([r1[a] for a in range(LATS)], None)
    for a, tile in enumerate(lateral_inverse(spectrum, 0, SIDE)[0]):
        s2[a] = tile
    for h in range(2):
        each(lambda d, h=h: to_rows(h, d).start())
    for h in range(2):
        r2[h, m, l] = s2[l, pl.ds(pl.multiple_of(m * ROWS + h * PART, PART), PART)]

    loads[4].wait()
    loads[5].wait()
    spec[0] = jnp.cos(specp[...]) * (1.0 / LONG)
    spec[1] = jnp.sin(specp[...]) * (1.0 / LONG)

    dec_row, det_row = dec_ref[...], det_ref[...]
    square = (BIN_COUNT, BIN_COUNT)
    eye = lax.broadcasted_iota(jnp.int32, square, 0) == lax.broadcasted_iota(jnp.int32, square, 1)
    dec_col = jnp.sum(jnp.where(eye, dec_row, 0.0), axis=1, keepdims=True)
    det_col = jnp.sum(jnp.where(eye, det_row, 0.0), axis=1, keepdims=True)
    lag = lane_iota((BIN_COUNT, SIDE)).astype(F32)

    def power(exponent, rate, angle):
        size = jnp.exp(-rate * exponent)
        return size * jnp.cos(angle * exponent), -size * jnp.sin(angle * exponent)

    def bin_of(q):
        part = lax.rem(q, 64)
        within = lax.rem(part, 16)
        return jnp.where(within < 8, (part // 16) * 8 + within, -1)

    q_row = lax.broadcasted_iota(jnp.int32, (128, BIN_COUNT), 0)
    spread = (bin_of(q_row) == lane_iota((128, BIN_COUNT))).astype(BF16)
    q_lane = lane_iota((BIN_COUNT, 128))
    pick = bin_of(q_lane) == lax.broadcasted_iota(jnp.int32, (BIN_COUNT, 128), 0)
    dec_lane = jnp.sum(jnp.where(pick, dec_col, 0.0), axis=0, keepdims=True)
    det_lane = jnp.sum(jnp.where(pick, det_col, 0.0), axis=0, keepdims=True)
    ahead = power(lag, dec_col, det_col)
    is_re = lax.broadcasted_iota(jnp.int32, (128, SIDE), 0) < 64
    (re_hi, re_lo), (im_hi, im_lo) = halves(ahead[0]), halves(ahead[1])
    for ref, re, im in ((q_hi, re_hi, im_hi), (q_lo, re_lo, im_lo)):
        re, im = dot(spread, re), dot(spread, im)
        ref[:, :SIDE] = jnp.where(is_re, re, -im).astype(BF16)
        ref[:, SIDE:] = jnp.where(is_re, im, re).astype(BF16)
    lane = lane_iota((BIN_COUNT, SIDE))
    inner = lax.rem(lane, 16)
    held = jnp.where(inner < 8, (lane // 64) * 8 + inner, -1)
    held = held == lax.broadcasted_iota(jnp.int32, (BIN_COUNT, SIDE), 0)
    held_b = held.astype(BF16)
    step_dec = jnp.sum(jnp.where(held, dec_col, 0.0), axis=0, keepdims=True)
    step_det = jnp.sum(jnp.where(held, det_col, 0.0), axis=0, keepdims=True)
    behind = power(SIDE - lag, dec_col, det_col)
    for ref, which in ((p_hi, 0), (p_lo, 1)):
        re = halves(behind[0])[which].astype(F32).T.astype(BF16)
        im = halves(behind[1])[which].astype(F32).T.astype(BF16)
        re, im = dot(re, held_b), dot(im, held_b)
        ref[:SIDE, :SIDE] = re.astype(BF16)
        ref[:SIDE, SIDE:] = im.astype(BF16)
        ref[SIDE:, :SIDE] = (-im).astype(BF16)
        ref[SIDE:, SIDE:] = re.astype(BF16)
    y = 2.0 * dec_lane
    series = jnp.ones_like(y)
    for n in range(9, 1, -1):
        series = 1.0 - series * y * (1.0 / n)
    drive = jnp.sqrt(y * series)
    bins_here = bin_of(lax.broadcasted_iota(jnp.int32, (128, occ.shape[0]), 0))
    member = (bins_here == gb_ref[...]).astype(BF16)
    occ_hi, occ_lo = halves(occ[...])
    ct[...] = (dot(member, occ_hi) + dot(member, occ_lo)).T * drive

    first_half = lane_iota((1, 128)) < 64
    far = []
    for k in range(TIMES):
        far.append(jnp.where(first_half, *power(float(SIDE * k), dec_lane, det_lane)))
    for h in range(2):
        mine = ct[pl.ds(pl.multiple_of(m * ROWS + h * PART, PART), PART), :]
        q = (q_hi[...], q_lo[...])
        response = jnp.concatenate([mine * f for f in far], axis=0)
        response = dot3(halves(response), q)
        response = unstack((response[:, :SIDE], response[:, SIDE:]))
        even = time_dft(response)
        kev[h, 0] = LONG * (1.0 - (0.5 * weight) * even[1])
        kev[h, 1] = (LONG * 0.5 * weight) * even[0]
        odd = time_dft(twist(response, False))
        kod[h, 0] = (-0.5 * weight / LONG) * odd[1]
        kod[h, 1] = (0.5 * weight / LONG) * odd[0]

    step = power(float(SIDE), step_dec, step_det)
    slot = lax.rem(lane_iota((8, SIDE)) // 16, 4)
    folded = [[jnp.zeros((8, SIDE), F32) for c in (0, 1)] for k in range(TIMES)]
    for h in range(2):
        each(lambda d, h=h: from_columns(h, d).wait_recv())
        field = [unpack([r2[h, k, a] for a in range(LATS)]) for k in range(TIMES)]
        turn_row = stack([
            tuple(jnp.broadcast_to(spec[c, k : k + 1, :], (PART, SIDE)) for c in (0, 1))
            for k in range(TIMES)
        ])
        once = cmul(time_dft(field), turn_row)
        twisted = time_dft(twist(time_inverse_dft(once), False))
        twisted = time_inverse_dft(cmul(twisted, (kod[h, 0], kod[h, 1])))
        late = time_dft(twist(twisted, True))
        straight = cmul(once, (kev[h, 0], kev[h, 1]))
        once = cmul((straight[0] + late[0], straight[1] + late[1]), turn_row)
        field = time_inverse_dft(once)
        for k in range(TIMES):
            for a, tile in enumerate(pack(*field[k])):
                s3[h][k, a, :PART, :] = tile
        if h == 0:
            each(lambda d: to_columns(0, d).start())
        flat = stack(field)
        ends = dot3(halves(jnp.concatenate(flat, axis=1)), (p_hi[...], p_lo[...]))
        ends = unstack((ends[:, :SIDE], ends[:, SIDE:]))
        state = (jnp.zeros((PART, SIDE), F32), jnp.zeros((PART, SIDE), F32))
        for k in range(TIMES):
            for c in (0, 1):
                for g in range(2):
                    piece = state[c][8 * g : 8 * g + 8]
                    folded[k][c] = jnp.where(slot == 2 * h + g, piece, folded[k][c])
            moved = cmul(state, step)
            state = (moved[0] + ends[k][0], moved[1] + ends[k][1])
    for k in range(TIMES):
        for a, tile in enumerate(pack(*folded[k])):
            s3b[k, a, PART:, :] = tile
    each(lambda d: to_columns(1, d).start())
    for h in range(2):
        r3[h][l, m] = s3[h][m, l]

    t2 = rows_ref[0, 2 * TIMES : 2 * TIMES + 1, :], rows_ref[1, 2 * TIMES : 2 * TIMES + 1, :]
    q = (q_hi[...], q_lo[...])
    response = dot3(halves(jnp.where(lane_iota(whole) < 64, ct[...], 0.0)), q)
    response = (response[:, :SIDE], response[:, SIDE:])
    even, odd = wide_dft(*response), wide_dft(*cmul(response, t2))
    gain = 0.5 * weight / SIDE
    kfe[0], kfe[1] = -gain * even[1], gain * even[0]
    kfo[0], kfo[1] = -gain * odd[1], gain * odd[0]

    for h in range(2):
        each(lambda d, h=h: from_rows(h, d).wait_recv())
    tiles, states = [], []
    for a in range(LATS):
        both = jnp.stack([r3a[a], r3b[a, :, :PART, :]], axis=1)
        tiles.append(both.reshape(SIDE, 128))
        extra = r3b[a, :, PART:, :].reshape(8 * TIMES, 128)
        extra = [roll(extra, -16 * g).reshape(TIMES, 8, 128) for g in range(4)]
        states.append(jnp.stack(extra, axis=1).reshape(SIDE, 128))
    spectrum = lateral_spectrum(tiles, states)
    span = SIDE // 2
    fold = span // 8
    slot = lax.rem(lane_iota((fold, 128)), 64) // 8
    last = []
    for h in range(2):
        tiles, states = lateral_inverse(spectrum, span * h, span * (h + 1))
        for a in range(LATS):
            s4[h, a, :span, :] = tiles[a]
            total = jnp.zeros((fold, 128), F32)
            for g in range(8):
                piece = roll(states[a][fold * g : fold * (g + 1)], 8 * g)
                total = jnp.where(slot == g, piece, total)
            s4[h, a, span:, :] = total
        for d in range(1, LATS):
            last.append(lat_send(s4.at[h], r4.at[h], ss4.at[h], rs4.at[h], d))
            last[-1].start()
        r4[h, l] = s4[h, l]

    slot = lax.rem(lane_iota((fold, 128)), 64) // 16
    for h in range(2):
        for d in range(1, LATS):
            lat_recv(s4.at[h], r4.at[h], ss4.at[h], rs4.at[h], d).wait_recv()
        here = pl.ds(span * h, span)
        field = unpack([r4[h, a, :span, :] for a in range(LATS)])
        carried = []
        for g in range(8):
            total = jnp.zeros((fold, 128), F32)
            for a in range(LATS):
                piece = roll(r4[h, a, span:, :], 16 * a - 8 * g)
                total = jnp.where(slot == a, piece, total)
            carried.append(total)
        carried = halves(jnp.concatenate(carried, axis=0) * ct[here, :])
        carried = dot3(carried, (q_hi[...], q_lo[...]))
        even = wide_inverse(*cmul(wide_dft(*field), (kfe[0, here, :], kfe[1, here, :])))
        odd = wide_dft(*cmul(field, t2))
        odd = wide_inverse(*cmul(odd, (kfo[0, here, :], kfo[1, here, :])))
        odd = cmul(odd, conj(t2))
        out[0, here, :] = field[0] + even[0] + odd[0] - weight * carried[:, SIDE:]
        out[1, here, :] = field[1] + even[1] + odd[1] + weight * carried[:, :SIDE]

    for copy in first + last:
        copy.wait_send()
    for h in range(2):
        each(lambda d, h=h: to_rows(h, d).wait_send())
        each(lambda d, h=h: to_columns(h, d).wait_send())


def fused(light_field, lateral_phase, spectral_phase, occupation, bin_decay, bin_detune, group_bin):
    tile = (SIDE, 128)
    vmem, sems = pltpu.VMEM, pltpu.SemaphoreType.DMA
    exchange = [
        vmem((LATS,) + tile, F32), vmem((LATS,) + tile, F32),
        vmem((LATS,) + tile, F32), vmem((2, TIMES, LATS, PART, 128), F32),
        vmem((TIMES, LATS, PART, 128), F32), vmem((LATS, TIMES, PART, 128), F32),
        vmem((TIMES, LATS, PART + 8, 128), F32), vmem((LATS, TIMES, PART + 8, 128), F32),
        vmem((2, LATS, 9 * SIDE // 16, 128), F32), vmem((2, LATS, 9 * SIDE // 16, 128), F32),
    ]
    tables = [vmem((LATS,) + tile, F32)] * 4 + [vmem(tile, F32)]
    tables += [vmem((128, 2 * SIDE), BF16)] * 2 + [vmem((2 * SIDE, 2 * SIDE), BF16)] * 2
    tables += [vmem((2, 2, SIDE // 2, SIDE), F32)] * 2 + [vmem((2, SIDE, SIDE), F32)] * 2
    tables += [vmem((2, TIMES, SIDE), F32)]
    fixed = constants()
    tables += [vmem(light_field.shape, F32), vmem(occupation.shape, F32)]
    tables += [vmem(c.shape, c.dtype) for c in fixed]
    semaphores = [sems((LATS,))] * 2 + [sems((2, TOTAL))] * 4 + [sems((2, LATS))] * 2
    semaphores += [sems((2 + len(fixed),))]
    in_vmem, anywhere = pl.BlockSpec(memory_space=pltpu.VMEM), pl.BlockSpec(memory_space=pl.ANY)
    return pl.pallas_call(
        kernel,
        out_shape=jax.ShapeDtypeStruct(light_field.shape, F32),
        in_specs=[anywhere] + [in_vmem] * 2 + [anywhere] + [in_vmem] * 3 + [anywhere] * len(fixed),
        out_specs=pl.BlockSpec(memory_space=pltpu.VMEM),
        scratch_shapes=exchange + tables + semaphores,
        compiler_params=pltpu.CompilerParams(
            collective_id=0, has_side_effects=True, vmem_limit_bytes=56 * 1024 * 1024
        ),
    )(
        light_field,
        lateral_phase.reshape(SIDE, LATS),
        spectral_phase.reshape(SIDE, TIMES).T,
        occupation,
        bin_decay[None],
        bin_detune[None],
        group_bin[None],
        *[jnp.asarray(c) for c in fixed],
    )


def solution(mesh):
    def local(light_field, *rest):
        fits = (lax.axis_size("lat"), lax.axis_size("tm")) == (LATS, TIMES)
        fits = fits and light_field.shape == (2, SIDE, SIDE)
        fits = fits and rest[2].shape == (128, SIDE) and rest[3].shape == (BIN_COUNT,)
        return (fused if fits else on_device)(light_field, *rest)

    return jax.shard_map(
        local,
        mesh=mesh,
        in_specs=(P(None, "lat", "tm"), P(), P(), P(None, "lat"), P(), P(), P()),
        out_specs=P(None, "lat", "tm"),
        check_vma=False,
    )
```

```python
import functools
import math

import jax
import jax.numpy as jnp
import numpy as np
from jax import lax
from jax.experimental import pallas as pl
from jax.experimental.pallas import tpu as pltpu
from jax.sharding import PartitionSpec as P

STRETCH = 128
STEPS = 2


GAIN_SCALE = 0.5


def carried_in(value, axis, join, neutral):
    count, mine = (lax.axis_size(axis), lax.axis_index(axis))
    pieces = jax.tree.map(lambda part: lax.all_gather(part, axis), value)
    so_far = jax.tree.map(
        lambda part, zero: jnp.full_like(part, 0) + jnp.asarray(zero, part.dtype), value, neutral
    )

    def lap(position, so_far):
        longer = join(so_far, jax.tree.map(lambda part: part[position], pieces))
        return jax.tree.map(lambda new, old: jnp.where(position < mine, new, old), longer, so_far)

    return lax.fori_loop(0, count - 1, lap, so_far)


def complex_einsum(form, left, right):
    exact = lax.Precision.HIGHEST
    real_part = jnp.einsum(form, left[0], right[0], precision=exact) - jnp.einsum(
        form, left[1], right[1], precision=exact
    )
    imag_part = jnp.einsum(form, left[0], right[1], precision=exact) + jnp.einsum(
        form, left[1], right[0], precision=exact
    )
    return (real_part, imag_part)


def complex_times(left, right):
    return (left[0] * right[0] - left[1] * right[1], left[0] * right[1] + left[1] * right[0])


def angle_table(height, breadth, modulus, sign):
    first = jnp.arange(height, dtype=jnp.int32)[:, None]
    second = jnp.arange(breadth, dtype=jnp.int32)[None, :]
    turns = (first * second % modulus).astype(jnp.float32) * (2.0 * math.pi / modulus)
    return (jnp.cos(turns), sign * jnp.sin(turns))


def time_forward(grid, small_table, twiddle, long_table):
    mixed = complex_einsum("ka,rab->rkb", small_table, grid)
    mixed = complex_times(mixed, twiddle)
    return complex_einsum("rkb,bq->rkq", mixed, long_table)


def time_inverse(spectrum, small_table, twiddle, long_table, length):
    mixed = complex_einsum("rkq,qb->rkb", spectrum, long_table)
    mixed = complex_times(mixed, twiddle)
    result = complex_einsum("ak,rkb->rab", small_table, mixed)
    return (result[0] / length, result[1] / length)


def powers(decay_rate, detuning, exponent):
    magnitude = jnp.exp(-decay_rate * exponent)
    phase_angle = detuning * exponent
    return (magnitude * jnp.cos(phase_angle), -magnitude * jnp.sin(phase_angle))


def on_device(
    light_field, lateral_phase, spectral_phase, occupation, bin_decay, bin_detune, group_bin
):
    lat_count = lax.axis_size("lat")
    time_count = lax.axis_size("tm")
    height = light_field.shape[1]
    span = light_field.shape[2]
    lateral_total = height * lat_count
    time_total = span * time_count
    groups = occupation.shape[0]
    slab = height // time_count
    narrow = span // lat_count
    exact = lax.Precision.HIGHEST
    lat_forward = angle_table(lateral_total, lateral_total, lateral_total, -1.0)
    lat_backward = angle_table(lateral_total, lateral_total, lateral_total, 1.0)
    lateral_turn = (jnp.cos(lateral_phase)[:, None], jnp.sin(lateral_phase)[:, None])
    small_back = angle_table(time_count, time_count, time_count, 1.0)
    twiddle_back = angle_table(time_count, span, time_total, 1.0)
    long_back = angle_table(span, span, span, 1.0)
    spectral_grid = spectral_phase.reshape(span, time_count).T
    spectral_turn = (jnp.cos(spectral_grid), jnp.sin(spectral_grid))
    bins = jnp.arange(bin_decay.shape[0], dtype=jnp.int32)
    onehot = (group_bin[:, None] == bins[None, :]).astype(jnp.float32)
    decay_rate = jnp.dot(onehot, bin_decay, precision=exact)
    detuning = jnp.dot(onehot, bin_detune, precision=exact)
    coupling = jnp.sqrt(-jnp.expm1(-2.0 * decay_rate))[:, None] * occupation
    lags = jnp.arange(STRETCH + 1, dtype=jnp.float32)[:, None]
    lag_powers = powers(decay_rate, detuning, lags)
    lag_grid = (
        jnp.arange(STRETCH, dtype=jnp.int32)[:, None]
        - jnp.arange(STRETCH, dtype=jnp.int32)[None, :]
    )
    inside = (lag_grid >= 0)[None]
    clipped = jnp.maximum(lag_grid, 0)
    leading = (lag_powers[0][1:].T, lag_powers[1][1:].T)
    trailing = (lag_powers[0][:STRETCH][::-1], lag_powers[1][:STRETCH][::-1])
    stretch_step = (lag_powers[0][STRETCH][:, None], lag_powers[1][STRETCH][:, None])
    device_step = powers(decay_rate, detuning, jnp.float32(span))
    weight = GAIN_SCALE / math.sqrt(groups)
    small_forward = angle_table(time_count, time_count, time_count, -1.0)
    twiddle_forward = angle_table(time_count, span, time_total, -1.0)
    long_forward = angle_table(span, span, span, -1.0)
    current = light_field
    block_toeplitz = (
        jnp.where(
            inside,
            jnp.take(
                jnp.dot(coupling.T, lag_powers[0][:STRETCH].T, precision=exact), clipped, axis=1
            ),
            0.0,
        ),
        jnp.where(
            inside,
            jnp.take(
                jnp.dot(coupling.T, lag_powers[1][:STRETCH].T, precision=exact), clipped, axis=1
            ),
            0.0,
        ),
    )
    for repeat in range(STEPS):
        diffract_stacked = current.reshape(2, height, lat_count, narrow)
        lateral_block = lax.all_to_all(
            diffract_stacked, "lat", split_axis=2, concat_axis=1, tiled=True
        )
        piece = (lateral_block[0, :, 0, :], lateral_block[1, :, 0, :])
        lateral_spectrum = complex_einsum("kx,xn->kn", lat_forward, piece)
        lateral_spectrum = complex_times(lateral_spectrum, lateral_turn)
        lateral_result = complex_einsum("xk,kn->xn", lat_backward, lateral_spectrum)
        lateral_joined = (
            jnp.stack([lateral_result[0], lateral_result[1]])[:, :, None, :] / lateral_total
        )
        diffract_turned = lax.all_to_all(
            lateral_joined, "lat", split_axis=1, concat_axis=2, tiled=True
        )
        stacked = diffract_turned.reshape(2, height, span).reshape(2, time_count, slab, span)
        rows = lax.all_to_all(stacked, "tm", split_axis=1, concat_axis=3, tiled=True)[:, 0]
        rows_here = rows.shape[1]
        grid = (
            rows[0].reshape(rows_here, time_count, span),
            rows[1].reshape(rows_here, time_count, span),
        )
        spectrum = time_forward(grid, small_forward, twiddle_forward, long_forward)
        spectrum = complex_times(spectrum, spectral_turn)
        result = time_inverse(spectrum, small_back, twiddle_back, long_back, time_total)
        joined = jnp.stack(
            [result[0].reshape(rows_here, time_total), result[1].reshape(rows_here, time_total)]
        )[:, None]
        turned = lax.all_to_all(joined, "tm", split_axis=3, concat_axis=1, tiled=True)
        current = turned.reshape(2, height, span)
        amplify_rows_here = current.shape[1]
        length = current.shape[2]
        count = length // STRETCH
        amplify_grid = (
            current[0].reshape(amplify_rows_here, count, STRETCH),
            current[1].reshape(amplify_rows_here, count, STRETCH),
        )
        direct = complex_einsum("xji,xci->xcj", block_toeplitz, amplify_grid)
        projected = complex_einsum("xci,ig->cgx", amplify_grid, trailing)
        stretch_ends = (coupling[None] * projected[0], coupling[None] * projected[1])

        def chain_step(running, ends):
            moved = complex_times(stretch_step, running)
            return ((moved[0] + ends[0], moved[1] + ends[1]), running)

        zero_state = jnp.zeros((groups, amplify_rows_here), jnp.float32)
        running, chain = lax.scan(chain_step, (zero_state, zero_state), stretch_ends)

        def combine(earlier, later):
            joint = complex_times((earlier[0], earlier[1]), (later[0], later[1]))
            carried = complex_times(
                (later[0][:, None], later[1][:, None]), (earlier[2], earlier[3])
            )
            return (joint[0], joint[1], carried[0] + later[2], carried[1] + later[3])

        identity = (
            jnp.ones((groups,), jnp.float32),
            jnp.zeros((groups,), jnp.float32),
            jnp.zeros_like(running[0]),
            jnp.zeros_like(running[1]),
        )
        prefix = carried_in(
            (device_step[0], device_step[1], running[0], running[1]), "tm", combine, identity
        )
        starts = powers(
            decay_rate, detuning, (jnp.arange(count, dtype=jnp.float32) * STRETCH)[:, None]
        )
        before = complex_times(
            (starts[0][:, :, None], starts[1][:, :, None]), (prefix[2][None], prefix[3][None])
        )
        states = (before[0] + chain[0], before[1] + chain[1])
        delayed = complex_einsum("cgx,gj->xcj", states, leading)
        summed_re = (direct[0] + delayed[0]).reshape(amplify_rows_here, length)
        summed_im = (direct[1] + delayed[1]).reshape(amplify_rows_here, length)
        current = jnp.stack([current[0] - weight * summed_im, current[1] + weight * summed_re])
    return current


LATS, TIMES, SIDE, BIN_COUNT = 4, 8, 256, 32
TOTAL = LATS * TIMES
WIDE = LATS * SIDE
LONG = TIMES * SIDE
ROWS = SIDE // TIMES
PART = ROWS // 2
F32, BF16 = jnp.float32, jnp.bfloat16
MESH = pl.DeviceIdType.MESH


@functools.cache
def constants():
    j = np.arange(SIDE)
    w = np.exp(-2j * np.pi * (np.outer(j, j) % SIDE) / SIDE)
    big = np.block([[w.real, w.imag], [-w.imag, w.real]]).astype(np.float32)
    big_hi = big.astype(jnp.bfloat16)
    big_lo = (big - big_hi.astype(np.float32)).astype(jnp.bfloat16)
    tw8 = np.exp(-2j * np.pi * np.outer(np.arange(TIMES), j) / LONG)
    tau = np.exp(-1j * np.pi * np.arange(LONG).reshape(TIMES, SIDE) / LONG)
    tau2 = np.exp(-1j * np.pi * j / SIDE)[None]
    rows = np.concatenate([tw8, tau, tau2, np.zeros((7, SIDE))])
    rows = np.stack([rows.real, rows.imag]).astype(np.float32)
    tw4 = np.exp(-2j * np.pi * np.outer(j, np.arange(LATS)) / WIDE)
    cols = np.concatenate([tw4.real, tw4.imag], axis=1).astype(np.float32)
    return (big_hi, big_lo, rows, cols)


def halves(x):
    hi = x.astype(BF16)
    return hi, (x - hi.astype(F32)).astype(BF16)


def dot(a, b):
    return jnp.dot(a, b, preferred_element_type=F32)


def dot3(a, b):
    return dot(a[0], b[0]) + dot(a[1], b[0]) + dot(a[0], b[1])


def cmul(a, b):
    return (a[0] * b[0] - a[1] * b[1], a[0] * b[1] + a[1] * b[0])


def conj(a):
    return (a[0], -a[1])


def small_fft(items, sign):
    count = len(items)
    if count == 1:
        return items
    even, odd = small_fft(items[0::2], sign), small_fft(items[1::2], sign)
    low, high = [], []
    for k in range(count // 2):
        re, im = odd[k]
        if 8 * k == count:
            r = math.sqrt(0.5)
            re, im = (re - sign * im) * r, (im + sign * re) * r
        elif 4 * k == count:
            re, im = -sign * im, sign * re
        elif 8 * k == 3 * count:
            r = math.sqrt(0.5)
            re, im = (-re - sign * im) * r, (-im + sign * re) * r
        low.append((even[k][0] + re, even[k][1] + im))
        high.append((even[k][0] - re, even[k][1] - im))
    return low + high


def lane_iota(shape):
    return lax.broadcasted_iota(jnp.int32, shape, len(shape) - 1)


def roll(x, shift):
    shift = shift % 128
    return pltpu.roll(x, shift, axis=x.ndim - 1) if shift else x


def pack(re, im):
    tiles = []
    first = lane_iota((re.shape[0], 128)) < 64
    for p in range(re.shape[1] // 128):
        a, b = re[:, 128 * p : 128 * p + 128], im[:, 128 * p : 128 * p + 128]
        tiles.append(jnp.where(first, a, roll(b, 64)))
        tiles.append(jnp.where(first, roll(a, 64), b))
    return tiles


def lane_part(shape):
    return lane_iota(shape) // 32


def pack_halves(re, im):
    part = lane_part((re[0].shape[0], 128))
    tiles = {}
    for l in range(LATS):
        for h in range(2):
            at = 2 * (l % 2) + h
            tile = None
            for q, source in enumerate((re[0], re[1], im[0], im[1])):
                piece = roll(source[:, 128 * (l // 2) : 128 * (l // 2) + 128], 32 * (q - at))
                tile = piece if tile is None else jnp.where(part == q, piece, tile)
            tiles[l, h] = tile
    return tiles


def unpack_halves(tiles):
    part = lane_part(tiles[0, 0].shape)
    done = []
    for q in range(4):
        joined = []
        for p in range(LATS // 2):
            value = None
            for at in range(4):
                piece = roll(tiles[2 * p + at // 2, at % 2], 32 * (at - q))
                value = piece if value is None else jnp.where(part == at, piece, value)
            joined.append(value)
        done.append(jnp.concatenate(joined, axis=1))
    return done[:2], done[2:]


def join_rows(a, b):
    count, width = a.shape
    a, b = (x.reshape(count // PART, PART, width) for x in (a, b))
    return jnp.stack([a, b], axis=1).reshape(2 * count, width)


def part_rows(x):
    x = x.reshape(x.shape[0] // ROWS, 2, PART, x.shape[1])
    return tuple(x[:, i].reshape(-1, x.shape[-1]) for i in (0, 1))


def turn(x):
    first = lane_iota(x.shape) < 64
    y = roll(x, 64)
    return jnp.where(first, -y, y)


def kernel(
    lf_hbm, latp, specp, occ_hbm, dec_ref, det_ref, gb_ref, wh_hbm, wl_hbm, rows_hbm, cols_hbm,
    out,
    s1, r1, s2, r2, s3a, r3a, s3b, r3b, s4a, r4a, s4b, r4b,
    tw_c, tw_s, th_c, th_s, ph_c, ph_s, ct, q_hi, q_lo, p_hi, p_lo, kev, kod, kfe, kfo, spec,
    lf, occ, wh, wl, rows_ref, cols_ref,
    ss1, rs1, ss2, rs2, ss3, rs3, ss4, rs4, load_sem,
):
    loads = []
    for i, (src, dst) in enumerate((
        (lf_hbm, lf), (cols_hbm, cols_ref), (wh_hbm, wh), (wl_hbm, wl), (occ_hbm, occ),
        (rows_hbm, rows_ref),
    )):
        loads.append(pltpu.make_async_copy(src, dst, load_sem.at[i]))
        loads[-1].start()
    l, m = lax.axis_index("lat"), lax.axis_index("tm")
    me = l * TIMES + m
    weight = GAIN_SCALE / math.sqrt(occ.shape[0])

    half = TIMES // 2

    def other(d):
        side = lax.rem(m // half + 1 + d // (TOTAL // 2), 2)
        tm = side * half + lax.rem(m + d, half)
        tl = lax.rem(l + lax.rem(d // half, LATS), LATS)
        return tl * TIMES + tm, tl, tm

    def each(act):
        act(0)

        def body(d, carry):
            act(d)
            act(d + TOTAL // 2)
            return carry

        lax.fori_loop(1, TOTAL // 2, body, 0)

    barrier = pltpu.get_barrier_semaphore()

    def greet(d):
        t, tl, tm = other(d)
        pl.semaphore_signal(barrier, inc=1, device_id=(tl, tm), device_id_type=MESH)

    each(greet)

    def remote(src, dst, send, recv, tl, tm):
        return pltpu.make_async_remote_copy(
            src_ref=src, dst_ref=dst, send_sem=send, recv_sem=recv,
            device_id=(tl, tm), device_id_type=MESH,
        )

    def lat_send(s, r, ss, rs, d):
        t = lax.rem(l + d, LATS)
        return remote(s.at[t], r.at[l], ss.at[t], rs.at[l], t, m)

    def lat_recv(s, r, ss, rs, d):
        t = lax.rem(l + d, LATS)
        return remote(s.at[t], r.at[t], ss.at[t], rs.at[t], t, m)

    def to_rows(h, d):
        t, tl, tm = other(d)
        src = s2.at[h, tl, pl.ds(pl.multiple_of(tm * PART, PART), PART)]
        return remote(src, r2.at[h, m, l], ss2.at[h, t], rs2.at[h, me], tl, tm)

    def from_columns(h, d):
        t, tl, tm = other(d)
        return remote(r2.at[h, tm, tl], r2.at[h, tm, tl], ss2.at[h, t], rs2.at[h, t], tl, tm)

    s3, r3 = (s3a, s3b), (r3a, r3b)

    def to_columns(h, d):
        t, tl, tm = other(d)
        return remote(s3[h].at[tm, tl], r3[h].at[l, m], ss3.at[h, t], rs3.at[h, me], tl, tm)

    def from_rows(h, d):
        t, tl, tm = other(d)
        here = r3[h].at[tl, tm]
        return remote(here, here, ss3.at[h, t], rs3.at[h, t], tl, tm)

    loads[0].wait()
    for (t, h), tile in pack_halves(part_rows(lf[0]), part_rows(lf[1])).items():
        s1[h, t] = tile
    pl.semaphore_wait(barrier, TOTAL - 1)
    first = [
        [lat_send(s1.at[h], r1.at[h], ss1.at[h], rs1.at[h], d) for d in range(1, LATS)]
        for h in range(2)
    ]
    for copy in first[0]:
        copy.start()
    for h in range(2):
        r1[h, l] = s1[h, l]

    loads[1].wait()
    whole = (SIDE, 128)
    group = lax.rem(lane_iota(whole), 64) // 16
    sign = jnp.where(lane_iota(whole) < 64, -1.0, 1.0)
    phase = latp[...]
    turn_c, turn_s = jnp.cos(phase) * (1.0 / WIDE), jnp.sin(phase) * (1.0 / WIDE)
    second_set = lax.rem(lane_part((SIDE // 2, 128)), 2) == 1
    second_key = lax.rem(lane_part(whole), 2) == 1
    for k in range(LATS):
        tw_c[k] = jnp.broadcast_to(cols_ref[:, k : k + 1], whole)
        tw_s[k] = jnp.broadcast_to(cols_ref[:, LATS + k : LATS + k + 1], whole) * sign
        ph_c[k] = jnp.broadcast_to(turn_c[:, k : k + 1], whole)
        ph_s[k] = jnp.broadcast_to(turn_s[:, k : k + 1], whole) * sign
        for full, parted in ((tw_c, th_c), (tw_s, th_s)):
            one, two = part_rows(full[k])
            parted[k] = jnp.where(second_set, two, one)

    def wide_dft(re, im):
        x = halves(jnp.concatenate([re, im], axis=1))
        y = dot3(x, (wh[...], wl[...]))
        return y[:, :SIDE], y[:, SIDE:]

    def wide_inverse(re, im):
        return conj(wide_dft(re, -im))

    def row(k):
        return rows_ref[0, k : k + 1, :], rows_ref[1, k : k + 1, :]

    def stack(items):
        return tuple(jnp.concatenate([item[c] for item in items], axis=0) for c in (0, 1))

    def unstack(value):
        return [tuple(v[ROWS * k : ROWS * (k + 1)] for v in value) for k in range(TIMES)]

    def time_dft(items):
        items = small_fft(items, -1)
        return wide_dft(*stack([cmul(item, row(k)) for k, item in enumerate(items)]))

    def time_inverse_dft(value):
        items = unstack(wide_inverse(*value))
        return small_fft([cmul(item, conj(row(k))) for k, item in enumerate(items)], 1)

    def twist(items, back):
        rows = [row(TIMES + k) for k in range(TIMES)]
        return [cmul(x, conj(r) if back else r) for x, r in zip(items, rows)]

    def column_dft(x, low, high):
        w = [
            jnp.concatenate([ref[low:high, :SIDE], ref[SIDE + low : SIDE + high, :SIDE]], axis=0)
            for ref in (wh, wl)
        ]
        y = dot3(w, halves(x))
        count = high - low
        return [
            (y[:count, k : k + 128], y[count:, k : k + 128]) for k in range(0, x.shape[1], 128)
        ]

    def butterfly(x, tables, back):
        a, b, c, d = x[0] + x[2], x[0] - x[2], x[1] + x[3], turn(x[1] - x[3])
        if back:
            return [a + c, b + d, a - c, b - d]
        across, along = tables
        y = [a + c, b - d, a - c, b + d]
        return [y[0]] + [y[k] * across[k] + roll(y[k], 64) * along[k] for k in (1, 2, 3)]

    def lateral_spectrum(x, states):
        y = butterfly(x, (th_c, th_s), False)
        spectrum, turns = [], []
        for k in (0, 2):
            one = jnp.where(second_set, roll(y[k + 1], 32), y[k])
            two = jnp.where(second_set, y[k + 1], roll(y[k], -32))
            spectrum.append(join_rows(one, two))
            turns.append(tuple(jnp.where(second_key, t[k + 1], t[k]) for t in (ph_c, ph_s)))
        if states:
            y = butterfly(states, (tw_c, tw_s), False)
            tile, across, along = y[0], ph_c[0], ph_s[0]
            for k in range(1, LATS):
                tile = jnp.where(group == k, roll(y[k], 16 * k), tile)
                across = jnp.where(group == k, ph_c[k], across)
                along = jnp.where(group == k, ph_s[k], along)
            spectrum.append(tile)
            turns.append((across, along))
        spectrum = column_dft(jnp.concatenate(spectrum, axis=1), 0, SIDE)
        done = []
        for (top, bottom), (across, along) in zip(spectrum, turns):
            y = top - turn(bottom)
            done.append(y * across + roll(y, 64) * along)
        return jnp.concatenate(done, axis=1)

    def untwiddle(y, tables, low, high):
        across, along = tables
        for k in (1, 2, 3):
            y[k] = y[k] * across[k, low:high, :] - roll(y[k], 64) * along[k, low:high, :]
        return butterfly(y, None, True)

    def lateral_inverse(spectrum, low, high):
        result = [top + turn(bottom) for top, bottom in column_dft(spectrum, low, high)]
        mask = second_set[: (high - low) // 2]
        y = []
        for tile in result[:2]:
            one, two = part_rows(tile)
            y.append(jnp.where(mask, roll(two, 32), one))
            y.append(jnp.where(mask, two, roll(one, -32)))
        done = [untwiddle(y, (th_c, th_s), low // 2, high // 2)]
        if len(result) > 2:
            y = [roll(result[2], -16 * k) for k in range(LATS)]
            done.append(untwiddle(y, (tw_c, tw_s), low, high))
        return done

    loads[2].wait()
    loads[3].wait()
    for copy in first[0]:
        copy.wait_send()
    for copy in first[1]:
        copy.start()
    for h in range(2):
        for d in range(1, LATS):
            lat_recv(s1.at[h], r1.at[h], ss1.at[h], rs1.at[h], d).wait_recv()
        spectrum = lateral_spectrum([r1[h, a] for a in range(LATS)], None)
        for a, tile in enumerate(lateral_inverse(spectrum, 0, SIDE)[0]):
            s2[h, a] = tile
        each(lambda d, h=h: to_rows(h, d).start())
        r2[h, m, l] = s2[h, l, pl.ds(pl.multiple_of(m * PART, PART), PART)]

    loads[4].wait()
    loads[5].wait()
    spec[0] = jnp.cos(specp[...]) * (1.0 / LONG)
    spec[1] = jnp.sin(specp[...]) * (1.0 / LONG)

    dec_row, det_row = dec_ref[...], det_ref[...]
    square = (BIN_COUNT, BIN_COUNT)
    eye = lax.broadcasted_iota(jnp.int32, square, 0) == lax.broadcasted_iota(jnp.int32, square, 1)
    dec_col = jnp.sum(jnp.where(eye, dec_row, 0.0), axis=1, keepdims=True)
    det_col = jnp.sum(jnp.where(eye, det_row, 0.0), axis=1, keepdims=True)
    lag = lane_iota((BIN_COUNT, SIDE)).astype(F32)

    def power(exponent, rate, angle):
        size = jnp.exp(-rate * exponent)
        return size * jnp.cos(angle * exponent), -size * jnp.sin(angle * exponent)

    def bin_of(q):
        part = lax.rem(q, 64)
        within = lax.rem(part, 16)
        return jnp.where(within < 8, (part // 16) * 8 + within, -1)

    q_row = lax.broadcasted_iota(jnp.int32, (128, BIN_COUNT), 0)
    spread = (bin_of(q_row) == lane_iota((128, BIN_COUNT))).astype(BF16)
    q_lane = lane_iota((BIN_COUNT, 128))
    pick = bin_of(q_lane) == lax.broadcasted_iota(jnp.int32, (BIN_COUNT, 128), 0)
    dec_lane = jnp.sum(jnp.where(pick, dec_col, 0.0), axis=0, keepdims=True)
    det_lane = jnp.sum(jnp.where(pick, det_col, 0.0), axis=0, keepdims=True)
    ahead = power(lag, dec_col, det_col)
    is_re = lax.broadcasted_iota(jnp.int32, (128, SIDE), 0) < 64
    (re_hi, re_lo), (im_hi, im_lo) = halves(ahead[0]), halves(ahead[1])
    for ref, re, im in ((q_hi, re_hi, im_hi), (q_lo, re_lo, im_lo)):
        re, im = dot(spread, re), dot(spread, im)
        ref[:, :SIDE] = jnp.where(is_re, re, -im).astype(BF16)
        ref[:, SIDE:] = jnp.where(is_re, im, re).astype(BF16)
    lane = lane_iota((BIN_COUNT, SIDE))
    inner = lax.rem(lane, 16)
    held = jnp.where(inner < 8, (lane // 64) * 8 + inner, -1)
    held = held == lax.broadcasted_iota(jnp.int32, (BIN_COUNT, SIDE), 0)
    held_b = held.astype(BF16)
    step_dec = jnp.sum(jnp.where(held, dec_col, 0.0), axis=0, keepdims=True)
    step_det = jnp.sum(jnp.where(held, det_col, 0.0), axis=0, keepdims=True)
    behind = power(SIDE - lag, dec_col, det_col)
    for ref, which in ((p_hi, 0), (p_lo, 1)):
        re = halves(behind[0])[which].astype(F32).T.astype(BF16)
        im = halves(behind[1])[which].astype(F32).T.astype(BF16)
        re, im = dot(re, held_b), dot(im, held_b)
        ref[:SIDE, :SIDE] = re.astype(BF16)
        ref[:SIDE, SIDE:] = im.astype(BF16)
        ref[SIDE:, :SIDE] = (-im).astype(BF16)
        ref[SIDE:, SIDE:] = re.astype(BF16)
    y = 2.0 * dec_lane
    series = jnp.ones_like(y)
    for n in range(9, 1, -1):
        series = 1.0 - series * y * (1.0 / n)
    drive = jnp.sqrt(y * series)
    bins_here = bin_of(lax.broadcasted_iota(jnp.int32, (128, occ.shape[0]), 0))
    member = (bins_here == gb_ref[...]).astype(BF16)
    occ_hi, occ_lo = halves(occ[...])
    ct[...] = (dot(member, occ_hi) + dot(member, occ_lo)).T * drive

    first_half = lane_iota((1, 128)) < 64
    far = []
    for k in range(TIMES):
        far.append(jnp.where(first_half, *power(float(SIDE * k), dec_lane, det_lane)))
    mine = ct[pl.ds(pl.multiple_of(m * ROWS, ROWS), ROWS), :]
    q = (q_hi[...], q_lo[...])
    response = dot3(halves(jnp.concatenate([mine * f for f in far], axis=0)), q)
    response = unstack((response[:, :SIDE], response[:, SIDE:]))
    even = time_dft(response)
    kev[0] = LONG * (1.0 - (0.5 * weight) * even[1])
    kev[1] = (LONG * 0.5 * weight) * even[0]
    odd = time_dft(twist(response, False))
    kod[0] = (-0.5 * weight / LONG) * odd[1]
    kod[1] = (0.5 * weight / LONG) * odd[0]

    for h in range(2):
        each(lambda d, h=h: from_columns(h, d).wait_recv())
    field = []
    for k in range(TIMES):
        re, im = unpack_halves({(a, h): r2[h, k, a] for a in range(LATS) for h in range(2)})
        field.append((jnp.concatenate(re, axis=0), jnp.concatenate(im, axis=0)))
    turn_row = stack([
        tuple(jnp.broadcast_to(spec[c, k : k + 1, :], (ROWS, SIDE)) for c in (0, 1))
        for k in range(TIMES)
    ])
    once = cmul(time_dft(field), turn_row)
    twisted = time_dft(twist(time_inverse_dft(once), False))
    twisted = time_inverse_dft(cmul(twisted, (kod[0], kod[1])))
    late = time_dft(twist(twisted, True))
    straight = cmul(once, (kev[0], kev[1]))
    once = cmul((straight[0] + late[0], straight[1] + late[1]), turn_row)
    field = time_inverse_dft(once)
    flat = stack(field)
    ends = dot3(halves(jnp.concatenate(flat, axis=1)), (p_hi[...], p_lo[...]))
    ends = unstack((ends[:, :SIDE], ends[:, SIDE:]))
    step = power(float(SIDE), step_dec, step_det)
    slot = lax.rem(lane_iota((8, SIDE)) // 16, 4)
    state = (jnp.zeros((ROWS, SIDE), F32), jnp.zeros((ROWS, SIDE), F32))
    for k in range(TIMES):
        folded = []
        for c in (0, 1):
            total = state[c][:8]
            for g in range(1, 4):
                total = jnp.where(slot == g, state[c][8 * g : 8 * g + 8], total)
            folded.append(total)
        for a, tile in enumerate(pack(*folded)):
            s3a[k, a, PART:, :] = tile
        moved = cmul(state, step)
        state = (moved[0] + ends[k][0], moved[1] + ends[k][1])
        re, im = ((v[:PART], v[PART:]) for v in field[k])
        for (a, h), tile in pack_halves(re, im).items():
            s3[h][k, a, :PART, :] = tile
    each(lambda d: to_columns(0, d).start())
    for h in range(2):
        r3[h][l, m] = s3[h][m, l]

    t2 = rows_ref[0, 2 * TIMES : 2 * TIMES + 1, :], rows_ref[1, 2 * TIMES : 2 * TIMES + 1, :]
    q = (q_hi[...], q_lo[...])
    response = dot3(halves(jnp.where(lane_iota(whole) < 64, ct[...], 0.0)), q)
    response = (response[:, :SIDE], response[:, SIDE:])
    even, odd = wide_dft(*response), wide_dft(*cmul(response, t2))
    gain = 0.5 * weight / SIDE
    kfe[0], kfe[1] = -gain * even[1], gain * even[0]
    kfo[0], kfo[1] = -gain * odd[1], gain * odd[0]

    each(lambda d: to_columns(0, d).wait_send())
    each(lambda d: to_columns(1, d).start())
    span = SIDE // 2
    fold = span // 8
    slot = lax.rem(lane_iota((fold, 128)), 64) // 8
    s4, r4 = (s4a, s4b), (r4a, r4b)
    last = []
    for h in range(2):
        each(lambda d, h=h: from_rows(h, d).wait_recv())
        tiles, states = [], []
        for a in range(LATS):
            tiles.append(r3[h][a, :, :PART, :].reshape(span, 128))
            if h == 0:
                extra = r3a[a, :, PART:, :].reshape(8 * TIMES, 128)
                extra = [roll(extra, -16 * g).reshape(TIMES, 8, 128) for g in range(4)]
                states.append(jnp.stack(extra, axis=1).reshape(SIDE, 128))
        spectrum = lateral_spectrum(tiles, states)
        for u in range(2):
            done = lateral_inverse(spectrum, span * u, span * (u + 1))
            for a in range(LATS):
                s4[h][u, a, : span // 2, :] = done[0][a]
                if h == 0:
                    total = done[1][a][:fold]
                    for g in range(1, 8):
                        piece = roll(done[1][a][fold * g : fold * (g + 1)], 8 * g)
                        total = jnp.where(slot == g, piece, total)
                    s4a[u, a, span // 2 :, :] = total
            for d in range(1, LATS):
                sems = ss4.at[h, u], rs4.at[h, u]
                last.append(lat_send(s4[h].at[u], r4[h].at[u], *sems, d))
                last[-1].start()
            r4[h][u, l] = s4[h][u, l]

    slot = lax.rem(lane_iota((fold, 128)), 64) // 16
    for u in range(2):
        for h in range(2):
            for d in range(1, LATS):
                sems = ss4.at[h, u], rs4.at[h, u]
                lat_recv(s4[h].at[u], r4[h].at[u], *sems, d).wait_recv()
        here = pl.ds(span * u, span)
        re, im = unpack_halves({
            (a, h): r4[h][u, a, : span // 2, :] for a in range(LATS) for h in range(2)
        })
        field = join_rows(*re), join_rows(*im)
        carried = []
        for g in range(8):
            total = jnp.zeros((fold, 128), F32)
            for a in range(LATS):
                piece = roll(r4a[u, a, span // 2 :, :], 16 * a - 8 * g)
                total = jnp.where(slot == a, piece, total)
            carried.append(total)
        carried = halves(jnp.concatenate(carried, axis=0) * ct[here, :])
        carried = dot3(carried, (q_hi[...], q_lo[...]))
        even = wide_inverse(*cmul(wide_dft(*field), (kfe[0, here, :], kfe[1, here, :])))
        odd = wide_dft(*cmul(field, t2))
        odd = wide_inverse(*cmul(odd, (kfo[0, here, :], kfo[1, here, :])))
        odd = cmul(odd, conj(t2))
        out[0, here, :] = field[0] + even[0] + odd[0] - weight * carried[:, SIDE:]
        out[1, here, :] = field[1] + even[1] + odd[1] + weight * carried[:, :SIDE]

    for copy in first[1] + last:
        copy.wait_send()
    for h in range(2):
        each(lambda d, h=h: to_rows(h, d).wait_send())
    each(lambda d: to_columns(1, d).wait_send())


def fused(light_field, lateral_phase, spectral_phase, occupation, bin_decay, bin_detune, group_bin):
    tile = (SIDE, 128)
    vmem, sems = pltpu.VMEM, pltpu.SemaphoreType.DMA
    exchange = [
        vmem((2, LATS, SIDE // 2, 128), F32), vmem((2, LATS, SIDE // 2, 128), F32),
        vmem((2, LATS, SIDE // 2, 128), F32), vmem((2, TIMES, LATS, PART, 128), F32),
        vmem((TIMES, LATS, PART + 8, 128), F32), vmem((LATS, TIMES, PART + 8, 128), F32),
        vmem((TIMES, LATS, PART, 128), F32), vmem((LATS, TIMES, PART, 128), F32),
        vmem((2, LATS, 5 * SIDE // 16, 128), F32), vmem((2, LATS, 5 * SIDE // 16, 128), F32),
        vmem((2, LATS, SIDE // 4, 128), F32), vmem((2, LATS, SIDE // 4, 128), F32),
    ]
    tables = [vmem((LATS,) + tile, F32)] * 2 + [vmem((LATS, SIDE // 2, 128), F32)] * 2
    tables += [vmem((LATS,) + tile, F32)] * 2 + [vmem(tile, F32)]
    tables += [vmem((128, 2 * SIDE), BF16)] * 2 + [vmem((2 * SIDE, 2 * SIDE), BF16)] * 2
    tables += [vmem((2, SIDE, SIDE), F32)] * 4
    tables += [vmem((2, TIMES, SIDE), F32)]
    fixed = constants()
    tables += [vmem(light_field.shape, F32), vmem(occupation.shape, F32)]
    tables += [vmem(c.shape, c.dtype) for c in fixed]
    semaphores = [sems((2, LATS))] * 2 + [sems((2, TOTAL))] * 4 + [sems((2, 2, LATS))] * 2
    semaphores += [sems((2 + len(fixed),))]
    in_vmem, anywhere = pl.BlockSpec(memory_space=pltpu.VMEM), pl.BlockSpec(memory_space=pl.ANY)
    return pl.pallas_call(
        kernel,
        out_shape=jax.ShapeDtypeStruct(light_field.shape, F32),
        in_specs=[anywhere] + [in_vmem] * 2 + [anywhere] + [in_vmem] * 3 + [anywhere] * len(fixed),
        out_specs=pl.BlockSpec(memory_space=pltpu.VMEM),
        scratch_shapes=exchange + tables + semaphores,
        compiler_params=pltpu.CompilerParams(
            collective_id=0, has_side_effects=True, vmem_limit_bytes=56 * 1024 * 1024
        ),
    )(
        light_field,
        lateral_phase.reshape(SIDE, LATS),
        spectral_phase.reshape(SIDE, TIMES).T,
        occupation,
        bin_decay[None],
        bin_detune[None],
        group_bin[None],
        *[jnp.asarray(c) for c in fixed],
    )


def solution(mesh):
    def local(light_field, *rest):
        fits = (lax.axis_size("lat"), lax.axis_size("tm")) == (LATS, TIMES)
        fits = fits and light_field.shape == (2, SIDE, SIDE)
        fits = fits and rest[2].shape == (128, SIDE) and rest[3].shape == (BIN_COUNT,)
        return (fused if fits else on_device)(light_field, *rest)

    return jax.shard_map(
        local,
        mesh=mesh,
        in_specs=(P(None, "lat", "tm"), P(), P(), P(None, "lat"), P(), P(), P()),
        out_specs=P(None, "lat", "tm"),
        check_vma=False,
    )
```

```python
import functools
import math

import jax
import jax.numpy as jnp
import numpy as np
from jax import lax
from jax.experimental import pallas as pl
from jax.experimental.pallas import tpu as pltpu
from jax.sharding import PartitionSpec as P

STRETCH = 128
STEPS = 2


GAIN_SCALE = 0.5


def carried_in(value, axis, join, neutral):
    count, mine = (lax.axis_size(axis), lax.axis_index(axis))
    pieces = jax.tree.map(lambda part: lax.all_gather(part, axis), value)
    so_far = jax.tree.map(
        lambda part, zero: jnp.full_like(part, 0) + jnp.asarray(zero, part.dtype), value, neutral
    )

    def lap(position, so_far):
        longer = join(so_far, jax.tree.map(lambda part: part[position], pieces))
        return jax.tree.map(lambda new, old: jnp.where(position < mine, new, old), longer, so_far)

    return lax.fori_loop(0, count - 1, lap, so_far)


def complex_einsum(form, left, right):
    exact = lax.Precision.HIGHEST
    real_part = jnp.einsum(form, left[0], right[0], precision=exact) - jnp.einsum(
        form, left[1], right[1], precision=exact
    )
    imag_part = jnp.einsum(form, left[0], right[1], precision=exact) + jnp.einsum(
        form, left[1], right[0], precision=exact
    )
    return (real_part, imag_part)


def complex_times(left, right):
    return (left[0] * right[0] - left[1] * right[1], left[0] * right[1] + left[1] * right[0])


def angle_table(height, breadth, modulus, sign):
    first = jnp.arange(height, dtype=jnp.int32)[:, None]
    second = jnp.arange(breadth, dtype=jnp.int32)[None, :]
    turns = (first * second % modulus).astype(jnp.float32) * (2.0 * math.pi / modulus)
    return (jnp.cos(turns), sign * jnp.sin(turns))


def time_forward(grid, small_table, twiddle, long_table):
    mixed = complex_einsum("ka,rab->rkb", small_table, grid)
    mixed = complex_times(mixed, twiddle)
    return complex_einsum("rkb,bq->rkq", mixed, long_table)


def time_inverse(spectrum, small_table, twiddle, long_table, length):
    mixed = complex_einsum("rkq,qb->rkb", spectrum, long_table)
    mixed = complex_times(mixed, twiddle)
    result = complex_einsum("ak,rkb->rab", small_table, mixed)
    return (result[0] / length, result[1] / length)


def powers(decay_rate, detuning, exponent):
    magnitude = jnp.exp(-decay_rate * exponent)
    phase_angle = detuning * exponent
    return (magnitude * jnp.cos(phase_angle), -magnitude * jnp.sin(phase_angle))


def on_device(
    light_field, lateral_phase, spectral_phase, occupation, bin_decay, bin_detune, group_bin
):
    lat_count = lax.axis_size("lat")
    time_count = lax.axis_size("tm")
    height = light_field.shape[1]
    span = light_field.shape[2]
    lateral_total = height * lat_count
    time_total = span * time_count
    groups = occupation.shape[0]
    slab = height // time_count
    narrow = span // lat_count
    exact = lax.Precision.HIGHEST
    lat_forward = angle_table(lateral_total, lateral_total, lateral_total, -1.0)
    lat_backward = angle_table(lateral_total, lateral_total, lateral_total, 1.0)
    lateral_turn = (jnp.cos(lateral_phase)[:, None], jnp.sin(lateral_phase)[:, None])
    small_back = angle_table(time_count, time_count, time_count, 1.0)
    twiddle_back = angle_table(time_count, span, time_total, 1.0)
    long_back = angle_table(span, span, span, 1.0)
    spectral_grid = spectral_phase.reshape(span, time_count).T
    spectral_turn = (jnp.cos(spectral_grid), jnp.sin(spectral_grid))
    bins = jnp.arange(bin_decay.shape[0], dtype=jnp.int32)
    onehot = (group_bin[:, None] == bins[None, :]).astype(jnp.float32)
    decay_rate = jnp.dot(onehot, bin_decay, precision=exact)
    detuning = jnp.dot(onehot, bin_detune, precision=exact)
    coupling = jnp.sqrt(-jnp.expm1(-2.0 * decay_rate))[:, None] * occupation
    lags = jnp.arange(STRETCH + 1, dtype=jnp.float32)[:, None]
    lag_powers = powers(decay_rate, detuning, lags)
    lag_grid = (
        jnp.arange(STRETCH, dtype=jnp.int32)[:, None]
        - jnp.arange(STRETCH, dtype=jnp.int32)[None, :]
    )
    inside = (lag_grid >= 0)[None]
    clipped = jnp.maximum(lag_grid, 0)
    leading = (lag_powers[0][1:].T, lag_powers[1][1:].T)
    trailing = (lag_powers[0][:STRETCH][::-1], lag_powers[1][:STRETCH][::-1])
    stretch_step = (lag_powers[0][STRETCH][:, None], lag_powers[1][STRETCH][:, None])
    device_step = powers(decay_rate, detuning, jnp.float32(span))
    weight = GAIN_SCALE / math.sqrt(groups)
    small_forward = angle_table(time_count, time_count, time_count, -1.0)
    twiddle_forward = angle_table(time_count, span, time_total, -1.0)
    long_forward = angle_table(span, span, span, -1.0)
    current = light_field
    block_toeplitz = (
        jnp.where(
            inside,
            jnp.take(
                jnp.dot(coupling.T, lag_powers[0][:STRETCH].T, precision=exact), clipped, axis=1
            ),
            0.0,
        ),
        jnp.where(
            inside,
            jnp.take(
                jnp.dot(coupling.T, lag_powers[1][:STRETCH].T, precision=exact), clipped, axis=1
            ),
            0.0,
        ),
    )
    for repeat in range(STEPS):
        diffract_stacked = current.reshape(2, height, lat_count, narrow)
        lateral_block = lax.all_to_all(
            diffract_stacked, "lat", split_axis=2, concat_axis=1, tiled=True
        )
        piece = (lateral_block[0, :, 0, :], lateral_block[1, :, 0, :])
        lateral_spectrum = complex_einsum("kx,xn->kn", lat_forward, piece)
        lateral_spectrum = complex_times(lateral_spectrum, lateral_turn)
        lateral_result = complex_einsum("xk,kn->xn", lat_backward, lateral_spectrum)
        lateral_joined = (
            jnp.stack([lateral_result[0], lateral_result[1]])[:, :, None, :] / lateral_total
        )
        diffract_turned = lax.all_to_all(
            lateral_joined, "lat", split_axis=1, concat_axis=2, tiled=True
        )
        stacked = diffract_turned.reshape(2, height, span).reshape(2, time_count, slab, span)
        rows = lax.all_to_all(stacked, "tm", split_axis=1, concat_axis=3, tiled=True)[:, 0]
        rows_here = rows.shape[1]
        grid = (
            rows[0].reshape(rows_here, time_count, span),
            rows[1].reshape(rows_here, time_count, span),
        )
        spectrum = time_forward(grid, small_forward, twiddle_forward, long_forward)
        spectrum = complex_times(spectrum, spectral_turn)
        result = time_inverse(spectrum, small_back, twiddle_back, long_back, time_total)
        joined = jnp.stack(
            [result[0].reshape(rows_here, time_total), result[1].reshape(rows_here, time_total)]
        )[:, None]
        turned = lax.all_to_all(joined, "tm", split_axis=3, concat_axis=1, tiled=True)
        current = turned.reshape(2, height, span)
        amplify_rows_here = current.shape[1]
        length = current.shape[2]
        count = length // STRETCH
        amplify_grid = (
            current[0].reshape(amplify_rows_here, count, STRETCH),
            current[1].reshape(amplify_rows_here, count, STRETCH),
        )
        direct = complex_einsum("xji,xci->xcj", block_toeplitz, amplify_grid)
        projected = complex_einsum("xci,ig->cgx", amplify_grid, trailing)
        stretch_ends = (coupling[None] * projected[0], coupling[None] * projected[1])

        def chain_step(running, ends):
            moved = complex_times(stretch_step, running)
            return ((moved[0] + ends[0], moved[1] + ends[1]), running)

        zero_state = jnp.zeros((groups, amplify_rows_here), jnp.float32)
        running, chain = lax.scan(chain_step, (zero_state, zero_state), stretch_ends)

        def combine(earlier, later):
            joint = complex_times((earlier[0], earlier[1]), (later[0], later[1]))
            carried = complex_times(
                (later[0][:, None], later[1][:, None]), (earlier[2], earlier[3])
            )
            return (joint[0], joint[1], carried[0] + later[2], carried[1] + later[3])

        identity = (
            jnp.ones((groups,), jnp.float32),
            jnp.zeros((groups,), jnp.float32),
            jnp.zeros_like(running[0]),
            jnp.zeros_like(running[1]),
        )
        prefix = carried_in(
            (device_step[0], device_step[1], running[0], running[1]), "tm", combine, identity
        )
        starts = powers(
            decay_rate, detuning, (jnp.arange(count, dtype=jnp.float32) * STRETCH)[:, None]
        )
        before = complex_times(
            (starts[0][:, :, None], starts[1][:, :, None]), (prefix[2][None], prefix[3][None])
        )
        states = (before[0] + chain[0], before[1] + chain[1])
        delayed = complex_einsum("cgx,gj->xcj", states, leading)
        summed_re = (direct[0] + delayed[0]).reshape(amplify_rows_here, length)
        summed_im = (direct[1] + delayed[1]).reshape(amplify_rows_here, length)
        current = jnp.stack([current[0] - weight * summed_im, current[1] + weight * summed_re])
    return current


LATS, TIMES, SIDE, BIN_COUNT = 4, 8, 256, 32
TOTAL = LATS * TIMES
WIDE = LATS * SIDE
LONG = TIMES * SIDE
ROWS = SIDE // TIMES
PART = ROWS // 2
F32, BF16 = jnp.float32, jnp.bfloat16
MESH = pl.DeviceIdType.MESH


@functools.cache
def constants():
    j = np.arange(SIDE)
    w = np.exp(-2j * np.pi * (np.outer(j, j) % SIDE) / SIDE)
    big = np.block([[w.real, w.imag], [-w.imag, w.real]]).astype(np.float32)
    big_hi = big.astype(jnp.bfloat16)
    big_lo = (big - big_hi.astype(np.float32)).astype(jnp.bfloat16)
    tw8 = np.exp(-2j * np.pi * np.outer(np.arange(TIMES), j) / LONG)
    tau = np.exp(-1j * np.pi * np.arange(LONG).reshape(TIMES, SIDE) / LONG)
    tau2 = np.exp(-1j * np.pi * j / SIDE)[None]
    ones = np.ones((TIMES, SIDE))
    rows = np.concatenate([tw8, tau, tau.conj(), ones, tau2, ones[1:]])
    rows = np.stack([rows.real, rows.imag]).astype(np.float32)
    tw4 = np.exp(-2j * np.pi * np.outer(j, np.arange(LATS)) / WIDE)
    cols = np.concatenate([tw4.real, tw4.imag], axis=1).astype(np.float32)
    return (big_hi, big_lo, rows, cols)


def halves(x):
    hi = x.astype(BF16)
    return hi, (x - hi.astype(F32)).astype(BF16)


def dot(a, b):
    return jnp.dot(a, b, preferred_element_type=F32)


def dot3(a, b):
    return dot(a[0], b[0]) + dot(a[1], b[0]) + dot(a[0], b[1])


def cmul(a, b):
    return (a[0] * b[0] - a[1] * b[1], a[0] * b[1] + a[1] * b[0])


def conj(a):
    return (a[0], -a[1])


def small_fft(items, sign):
    count = len(items)
    if count == 1:
        return items
    even, odd = small_fft(items[0::2], sign), small_fft(items[1::2], sign)
    low, high = [], []
    for k in range(count // 2):
        re, im = odd[k]
        if 8 * k == count:
            r = math.sqrt(0.5)
            re, im = (re - sign * im) * r, (im + sign * re) * r
        elif 4 * k == count:
            re, im = -sign * im, sign * re
        elif 8 * k == 3 * count:
            r = math.sqrt(0.5)
            re, im = (-re - sign * im) * r, (-im + sign * re) * r
        low.append((even[k][0] + re, even[k][1] + im))
        high.append((even[k][0] - re, even[k][1] - im))
    return low + high


def lane_iota(shape):
    return lax.broadcasted_iota(jnp.int32, shape, len(shape) - 1)


def roll(x, shift):
    shift = shift % 128
    return pltpu.roll(x, shift, axis=x.ndim - 1) if shift else x


def pack(re, im):
    tiles = []
    first = lane_iota((re.shape[0], 128)) < 64
    for p in range(re.shape[1] // 128):
        a, b = re[:, 128 * p : 128 * p + 128], im[:, 128 * p : 128 * p + 128]
        tiles.append(jnp.where(first, a, roll(b, 64)))
        tiles.append(jnp.where(first, roll(a, 64), b))
    return tiles


def lane_part(shape):
    return lane_iota(shape) // 32


def pack_halves(re, im):
    part = lane_part((re[0].shape[0], 128))
    tiles = {}
    for l in range(LATS):
        for h in range(2):
            at = 2 * (l % 2) + h
            tile = None
            for q, source in enumerate((re[0], re[1], im[0], im[1])):
                piece = roll(source[:, 128 * (l // 2) : 128 * (l // 2) + 128], 32 * (q - at))
                tile = piece if tile is None else jnp.where(part == q, piece, tile)
            tiles[l, h] = tile
    return tiles


def unpack_halves(tiles):
    part = lane_part(tiles[0, 0].shape)
    done = []
    for q in range(4):
        joined = []
        for p in range(LATS // 2):
            value = None
            for at in range(4):
                piece = roll(tiles[2 * p + at // 2, at % 2], 32 * (at - q))
                value = piece if value is None else jnp.where(part == at, piece, value)
            joined.append(value)
        done.append(jnp.concatenate(joined, axis=1))
    return done[:2], done[2:]


def join_rows(a, b):
    count, width = a.shape
    a, b = (x.reshape(count // PART, PART, width) for x in (a, b))
    return jnp.stack([a, b], axis=1).reshape(2 * count, width)


def part_rows(x):
    x = x.reshape(x.shape[0] // ROWS, 2, PART, x.shape[1])
    return tuple(x[:, i].reshape(-1, x.shape[-1]) for i in (0, 1))


def turn(x):
    first = lane_iota(x.shape) < 64
    y = roll(x, 64)
    return jnp.where(first, -y, y)


def kernel(
    lf_hbm, latp, specp, occ_hbm, dec_ref, det_ref, gb_ref, wh_hbm, wl_hbm, rows_hbm, cols_hbm,
    out,
    s1, r1, s2, r2, s3a, r3a, s3b, r3b, s4a, r4a, s4b, r4b,
    tw_c, tw_s, th_c, th_s, ph_c, ph_s, ct, q_hi, q_lo, p_hi, p_lo, mul, add, kf, xb, yb, kept, spec,
    lf, occ, wh, wl, rows_ref, cols_ref,
    ss1, rs1, ss2, rs2, ss3, rs3, ss4, rs4, load_sem,
):
    loads = []
    for i, (src, dst) in enumerate((
        (lf_hbm, lf), (cols_hbm, cols_ref), (wh_hbm, wh), (wl_hbm, wl), (occ_hbm, occ),
        (rows_hbm, rows_ref),
    )):
        loads.append(pltpu.make_async_copy(src, dst, load_sem.at[i]))
        loads[-1].start()
    l, m = lax.axis_index("lat"), lax.axis_index("tm")
    me = l * TIMES + m
    weight = GAIN_SCALE / math.sqrt(occ.shape[0])

    half = TIMES // 2

    def other(d):
        side = lax.rem(m // half + 1 + d // (TOTAL // 2), 2)
        tm = side * half + lax.rem(m + d, half)
        tl = lax.rem(l + lax.rem(d // half, LATS), LATS)
        return tl * TIMES + tm, tl, tm

    def each(act):
        act(0)

        def body(d, carry):
            act(d)
            act(d + TOTAL // 2)
            return carry

        lax.fori_loop(1, TOTAL // 2, body, 0)

    barrier = pltpu.get_barrier_semaphore()

    def greet(d):
        t, tl, tm = other(d)
        pl.semaphore_signal(barrier, inc=1, device_id=(tl, tm), device_id_type=MESH)

    each(greet)

    def remote(src, dst, send, recv, tl, tm):
        return pltpu.make_async_remote_copy(
            src_ref=src, dst_ref=dst, send_sem=send, recv_sem=recv,
            device_id=(tl, tm), device_id_type=MESH,
        )

    def lat_send(s, r, ss, rs, d):
        t = lax.rem(l + d, LATS)
        return remote(s.at[t], r.at[l], ss.at[t], rs.at[l], t, m)

    def lat_recv(s, r, ss, rs, d):
        t = lax.rem(l + d, LATS)
        return remote(s.at[t], r.at[t], ss.at[t], rs.at[t], t, m)

    def to_rows(h, d):
        t, tl, tm = other(d)
        src = s2.at[h, tl, pl.ds(pl.multiple_of(tm * PART, PART), PART)]
        return remote(src, r2.at[h, m, l], ss2.at[h, t], rs2.at[h, me], tl, tm)

    def from_columns(h, d):
        t, tl, tm = other(d)
        return remote(r2.at[h, tm, tl], r2.at[h, tm, tl], ss2.at[h, t], rs2.at[h, t], tl, tm)

    s3, r3 = (s3a, s3b), (r3a, r3b)

    def to_columns(h, d):
        t, tl, tm = other(d)
        return remote(s3[h].at[tm, tl], r3[h].at[l, m], ss3.at[h, t], rs3.at[h, me], tl, tm)

    def from_rows(h, d):
        t, tl, tm = other(d)
        here = r3[h].at[tl, tm]
        return remote(here, here, ss3.at[h, t], rs3.at[h, t], tl, tm)

    loads[0].wait()
    for (t, h), tile in pack_halves(part_rows(lf[0]), part_rows(lf[1])).items():
        s1[h, t] = tile
    pl.semaphore_wait(barrier, TOTAL - 1)
    first = [
        [lat_send(s1.at[h], r1.at[h], ss1.at[h], rs1.at[h], d) for d in range(1, LATS)]
        for h in range(2)
    ]
    for copy in first[0]:
        copy.start()
    for h in range(2):
        r1[h, l] = s1[h, l]

    loads[1].wait()
    whole = (SIDE, 128)
    group = lax.rem(lane_iota(whole), 64) // 16
    sign = jnp.where(lane_iota(whole) < 64, -1.0, 1.0)
    phase = latp[...]
    turn_c, turn_s = jnp.cos(phase) * (1.0 / WIDE), jnp.sin(phase) * (1.0 / WIDE)
    second_set = lax.rem(lane_part((SIDE // 2, 128)), 2) == 1
    second_key = lax.rem(lane_part(whole), 2) == 1
    for k in range(LATS):
        tw_c[k] = jnp.broadcast_to(cols_ref[:, k : k + 1], whole)
        tw_s[k] = jnp.broadcast_to(cols_ref[:, LATS + k : LATS + k + 1], whole) * sign
        ph_c[k] = jnp.broadcast_to(turn_c[:, k : k + 1], whole)
        ph_s[k] = jnp.broadcast_to(turn_s[:, k : k + 1], whole) * sign
        for full, parted in ((tw_c, th_c), (tw_s, th_s)):
            one, two = part_rows(full[k])
            parted[k] = jnp.where(second_set, two, one)

    def wide_dft(re, im):
        x = halves(jnp.concatenate([re, im], axis=1))
        y = dot3(x, (wh[...], wl[...]))
        return y[:, :SIDE], y[:, SIDE:]

    def wide_inverse(re, im):
        return conj(wide_dft(re, -im))

    def block(i):
        at = pl.ds(pl.multiple_of(8 * i, 8), 8)
        return rows_ref[0, at, :], rows_ref[1, at, :]

    def row(table, k):
        return table[0][k : k + 1], table[1][k : k + 1]

    def groups_of_rows(body):
        def step(g, carry):
            body([pl.ds(pl.multiple_of(ROWS * k + 8 * g, 8), 8) for k in range(TIMES)])
            return carry

        lax.fori_loop(0, ROWS // 8, step, 0)

    def time_dft(src, pre=None):
        def body(spots):
            items = [(src[0, at, :], src[1, at, :]) for at in spots]
            if pre is not None:
                items = [cmul(x, row(pre, k)) for k, x in enumerate(items)]
            items = small_fft(items, -1)
            for k, at in enumerate(spots):
                yb[0, at, :], yb[1, at, :] = cmul(items[k], row(block(0), k))

        groups_of_rows(body)
        return wide_dft(yb[0], yb[1])

    def time_inverse_dft(value, post):
        yb[0], yb[1] = wide_inverse(*value)

        def body(spots):
            items = [(yb[0, at, :], yb[1, at, :]) for at in spots]
            items = [cmul(x, conj(row(block(0), k))) for k, x in enumerate(items)]
            for k, x in enumerate(small_fft(items, 1)):
                xb[0, spots[k], :], xb[1, spots[k], :] = cmul(x, row(post, k))

        groups_of_rows(body)

    def column_dft(x, low, count):
        w = [
            jnp.concatenate([ref[pl.ds(at, count), :SIDE] for at in (low, SIDE + low)], axis=0)
            for ref in (wh, wl)
        ]
        y = dot3(w, halves(x))
        return [
            (y[:count, k : k + 128], y[count:, k : k + 128]) for k in range(0, x.shape[1], 128)
        ]

    def butterfly(x, tables, back):
        a, b, c, d = x[0] + x[2], x[0] - x[2], x[1] + x[3], turn(x[1] - x[3])
        if back:
            return [a + c, b + d, a - c, b - d]
        across, along = tables
        y = [a + c, b - d, a - c, b + d]
        return [y[0]] + [y[k] * across[k] + roll(y[k], 64) * along[k] for k in (1, 2, 3)]

    def lateral_spectrum(x, states):
        y = butterfly(x, (th_c, th_s), False)
        spectrum, turns = [], []
        for k in (0, 2):
            one = jnp.where(second_set, roll(y[k + 1], 32), y[k])
            two = jnp.where(second_set, y[k + 1], roll(y[k], -32))
            spectrum.append(join_rows(one, two))
            turns.append(tuple(jnp.where(second_key, t[k + 1], t[k]) for t in (ph_c, ph_s)))
        if states:
            y = butterfly(states, (tw_c, tw_s), False)
            tile, across, along = y[0], ph_c[0], ph_s[0]
            for k in range(1, LATS):
                tile = jnp.where(group == k, roll(y[k], 16 * k), tile)
                across = jnp.where(group == k, ph_c[k], across)
                along = jnp.where(group == k, ph_s[k], along)
            spectrum.append(tile)
            turns.append((across, along))
        spectrum = column_dft(jnp.concatenate(spectrum, axis=1), 0, SIDE)
        done = []
        for (top, bottom), (across, along) in zip(spectrum, turns):
            y = top - turn(bottom)
            done.append(y * across + roll(y, 64) * along)
        return jnp.concatenate(done, axis=1)

    def untwiddle(y, tables, low, count):
        across, along = tables
        here = pl.ds(low, count)
        for k in (1, 2, 3):
            y[k] = y[k] * across[k, here, :] - roll(y[k], 64) * along[k, here, :]
        return butterfly(y, None, True)

    def lateral_inverse(spectrum, low, half_low, count):
        result = [top + turn(bottom) for top, bottom in column_dft(spectrum, low, count)]
        mask = second_set[: count // 2]
        y = []
        for tile in result[:2]:
            one, two = part_rows(tile)
            y.append(jnp.where(mask, roll(two, 32), one))
            y.append(jnp.where(mask, two, roll(one, -32)))
        done = [untwiddle(y, (th_c, th_s), half_low, count // 2)]
        if len(result) > 2:
            y = [roll(result[2], -16 * k) for k in range(LATS)]
            done.append(untwiddle(y, (tw_c, tw_s), low, count))
        return done

    loads[2].wait()
    loads[3].wait()
    for copy in first[0]:
        copy.wait_send()
    for copy in first[1]:
        copy.start()

    def column_half(h, carry):
        for d in range(1, LATS):
            lat_recv(s1.at[h], r1.at[h], ss1.at[h], rs1.at[h], d).wait_recv()
        spectrum = lateral_spectrum([r1[h, a] for a in range(LATS)], None)
        for a, tile in enumerate(lateral_inverse(spectrum, 0, 0, SIDE)[0]):
            s2[h, a] = tile
        each(lambda d: to_rows(h, d).start())
        r2[h, m, l] = s2[h, l, pl.ds(pl.multiple_of(m * PART, PART), PART)]
        return carry

    lax.fori_loop(0, 2, column_half, 0)

    loads[4].wait()
    loads[5].wait()
    spec[0] = jnp.cos(specp[...]) * (1.0 / LONG)
    spec[1] = jnp.sin(specp[...]) * (1.0 / LONG)

    dec_row, det_row = dec_ref[...], det_ref[...]
    square = (BIN_COUNT, BIN_COUNT)
    eye = lax.broadcasted_iota(jnp.int32, square, 0) == lax.broadcasted_iota(jnp.int32, square, 1)
    dec_col = jnp.sum(jnp.where(eye, dec_row, 0.0), axis=1, keepdims=True)
    det_col = jnp.sum(jnp.where(eye, det_row, 0.0), axis=1, keepdims=True)
    lag = lane_iota((BIN_COUNT, SIDE)).astype(F32)

    def power(exponent, rate, angle):
        size = jnp.exp(-rate * exponent)
        return size * jnp.cos(angle * exponent), -size * jnp.sin(angle * exponent)

    def bin_of(q):
        part = lax.rem(q, 64)
        within = lax.rem(part, 16)
        return jnp.where(within < 8, (part // 16) * 8 + within, -1)

    q_row = lax.broadcasted_iota(jnp.int32, (128, BIN_COUNT), 0)
    spread = (bin_of(q_row) == lane_iota((128, BIN_COUNT))).astype(BF16)
    q_lane = lane_iota((BIN_COUNT, 128))
    pick = bin_of(q_lane) == lax.broadcasted_iota(jnp.int32, (BIN_COUNT, 128), 0)
    dec_lane = jnp.sum(jnp.where(pick, dec_col, 0.0), axis=0, keepdims=True)
    det_lane = jnp.sum(jnp.where(pick, det_col, 0.0), axis=0, keepdims=True)
    ahead = power(lag, dec_col, det_col)
    is_re = lax.broadcasted_iota(jnp.int32, (128, SIDE), 0) < 64
    (re_hi, re_lo), (im_hi, im_lo) = halves(ahead[0]), halves(ahead[1])
    for ref, re, im in ((q_hi, re_hi, im_hi), (q_lo, re_lo, im_lo)):
        re, im = dot(spread, re), dot(spread, im)
        ref[:, :SIDE] = jnp.where(is_re, re, -im).astype(BF16)
        ref[:, SIDE:] = jnp.where(is_re, im, re).astype(BF16)
    lane = lane_iota((BIN_COUNT, SIDE))
    inner = lax.rem(lane, 16)
    held = jnp.where(inner < 8, (lane // 64) * 8 + inner, -1)
    held = held == lax.broadcasted_iota(jnp.int32, (BIN_COUNT, SIDE), 0)
    held_b = held.astype(BF16)
    step_dec = jnp.sum(jnp.where(held, dec_col, 0.0), axis=0, keepdims=True)
    step_det = jnp.sum(jnp.where(held, det_col, 0.0), axis=0, keepdims=True)
    behind = power(SIDE - lag, dec_col, det_col)
    for ref, which in ((p_hi, 0), (p_lo, 1)):
        re = halves(behind[0])[which].astype(F32).T.astype(BF16)
        im = halves(behind[1])[which].astype(F32).T.astype(BF16)
        re, im = dot(re, held_b), dot(im, held_b)
        ref[:SIDE, :SIDE] = re.astype(BF16)
        ref[:SIDE, SIDE:] = im.astype(BF16)
        ref[SIDE:, :SIDE] = (-im).astype(BF16)
        ref[SIDE:, SIDE:] = re.astype(BF16)
    y = 2.0 * dec_lane
    series = jnp.ones_like(y)
    for n in range(9, 1, -1):
        series = 1.0 - series * y * (1.0 / n)
    drive = jnp.sqrt(y * series)
    bins_here = bin_of(lax.broadcasted_iota(jnp.int32, (128, occ.shape[0]), 0))
    member = (bins_here == gb_ref[...]).astype(BF16)
    occ_hi, occ_lo = halves(occ[...])
    ct[...] = (dot(member, occ_hi) + dot(member, occ_lo)).T * drive

    first_half = lane_iota((1, 128)) < 64
    far = []
    for k in range(TIMES):
        far.append(jnp.where(first_half, *power(float(SIDE * k), dec_lane, det_lane)))
    mine = ct[pl.ds(pl.multiple_of(m * ROWS, ROWS), ROWS), :]
    q = (q_hi[...], q_lo[...])
    response = dot3(halves(jnp.concatenate([mine * f for f in far], axis=0)), q)
    xb[0], xb[1] = response[:, :SIDE], response[:, SIDE:]

    def spectra(e, carry):
        mul[e, 0], mul[e, 1] = time_dft(xb, block(3 - 2 * e))
        return carry

    lax.fori_loop(0, 2, spectra, 0)
    gain = 0.5 * weight
    even = 1.0 - gain * mul[0, 1], gain * mul[0, 0]
    odd = (-gain / LONG) * mul[1, 1], (gain / LONG) * mul[1, 0]
    turn_row = tuple(
        jnp.concatenate(
            [jnp.broadcast_to(spec[c, k : k + 1, :], (ROWS, SIDE)) for k in range(TIMES)], axis=0
        )
        for c in (0, 1)
    )
    even = cmul(even, turn_row)
    for c in (0, 1):
        mul[0, c], mul[1, c], mul[2, c] = turn_row[c], odd[c], turn_row[c]
        add[0, c], add[1, c] = jnp.zeros((SIDE, SIDE), F32), jnp.zeros((SIDE, SIDE), F32)
        add[2, c] = LONG * even[c]
        kept[c] = jnp.zeros((SIDE, SIDE), F32)

    for h in range(2):
        each(lambda d, h=h: from_columns(h, d).wait_recv())

    def gather(k, carry):
        re, im = unpack_halves({(a, h): r2[h, k, a] for a in range(LATS) for h in range(2)})
        at = pl.ds(pl.multiple_of(ROWS * k, ROWS), ROWS)
        xb[0, at, :] = jnp.concatenate(re, axis=0)
        xb[1, at, :] = jnp.concatenate(im, axis=0)
        return carry

    lax.fori_loop(0, TIMES, gather, 0)

    def advance(i, carry):
        y = cmul(time_dft(xb), (mul[i, 0], mul[i, 1]))
        z = cmul((kept[0], kept[1]), (add[i, 0], add[i, 1]))
        y = y[0] + z[0], y[1] + z[1]

        @pl.when(i == 0)
        def keep():
            kept[0], kept[1] = y

        time_inverse_dft(y, block(1 + i))
        return carry

    lax.fori_loop(0, 3, advance, 0)
    flat = jnp.concatenate([xb[0], xb[1]], axis=1)
    ends = dot3(halves(flat), (p_hi[...], p_lo[...]))
    yb[0], yb[1] = ends[:, :SIDE], ends[:, SIDE:]
    step = power(float(SIDE), step_dec, step_det)
    slot = lax.rem(lane_iota((8, SIDE)) // 16, 4)

    def hand_out(k, state):
        folded = []
        for c in (0, 1):
            total = state[c][:8]
            for g in range(1, 4):
                total = jnp.where(slot == g, state[c][8 * g : 8 * g + 8], total)
            folded.append(total)
        for a, tile in enumerate(pack(*folded)):
            s3a[k, a, PART:, :] = tile
        at = pl.ds(pl.multiple_of(ROWS * k, ROWS), ROWS)
        moved = cmul(state, step)
        re, im = ((v[:PART], v[PART:]) for v in (xb[0, at, :], xb[1, at, :]))
        for (a, h), tile in pack_halves(re, im).items():
            s3[h][k, a, :PART, :] = tile
        return (moved[0] + yb[0, at, :], moved[1] + yb[1, at, :])

    zero = jnp.zeros((ROWS, SIDE), F32)
    lax.fori_loop(0, TIMES, hand_out, (zero, zero))
    each(lambda d: to_columns(0, d).start())
    for h in range(2):
        r3[h][l, m] = s3[h][m, l]

    q = (q_hi[...], q_lo[...])
    response = dot3(halves(jnp.where(lane_iota(whole) < 64, ct[...], 0.0)), q)
    yb[0], yb[1] = response[:, :SIDE], response[:, SIDE:]

    def own_spectra(e, carry):
        re, im = wide_dft(*cmul((yb[0], yb[1]), row(block(3 + e), 0)))
        kf[e, 0], kf[e, 1] = (-gain / SIDE) * im, (gain / SIDE) * re
        return carry

    lax.fori_loop(0, 2, own_spectra, 0)

    each(lambda d: to_columns(0, d).wait_send())
    each(lambda d: to_columns(1, d).start())
    span = SIDE // 2
    fold = span // 8
    slot = lax.rem(lane_iota((fold, 128)), 64) // 8
    s4, r4 = (s4a, s4b), (r4a, r4b)
    for h in range(2):
        each(lambda d, h=h: from_rows(h, d).wait_recv())
        tiles, states = [], []
        for a in range(LATS):
            tiles.append(r3[h][a, :, :PART, :].reshape(span, 128))
            if h == 0:
                extra = r3a[a, :, PART:, :].reshape(8 * TIMES, 128)
                extra = [roll(extra, -16 * g).reshape(TIMES, 8, 128) for g in range(4)]
                states.append(jnp.stack(extra, axis=1).reshape(SIDE, 128))
        spectrum = lateral_spectrum(tiles, states)

        def send_part(u, carry, h=h, spectrum=spectrum):
            low = pl.multiple_of(span * u, span)
            done = lateral_inverse(spectrum, low, pl.multiple_of(low // 2, span // 2), span)
            for a in range(LATS):
                s4[h][u, a, : span // 2, :] = done[0][a]
                if h == 0:
                    total = done[1][a][:fold]
                    for g in range(1, 8):
                        piece = roll(done[1][a][fold * g : fold * (g + 1)], 8 * g)
                        total = jnp.where(slot == g, piece, total)
                    s4a[u, a, span // 2 :, :] = total
            for d in range(1, LATS):
                sems = ss4.at[h, u], rs4.at[h, u]
                lat_send(s4[h].at[u], r4[h].at[u], *sems, d).start()
            r4[h][u, l] = s4[h][u, l]
            return carry

        lax.fori_loop(0, 2, send_part, 0)

    slot4 = lax.rem(lane_iota((fold, 128)), 64) // 16

    def finish(u, carry):
        for h in range(2):
            for d in range(1, LATS):
                sems = ss4.at[h, u], rs4.at[h, u]
                lat_recv(s4[h].at[u], r4[h].at[u], *sems, d).wait_recv()
        here = pl.ds(pl.multiple_of(span * u, span), span)
        re, im = unpack_halves({
            (a, h): r4[h][u, a, : span // 2, :] for a in range(LATS) for h in range(2)
        })
        field = join_rows(*re), join_rows(*im)
        carried = []
        for g in range(8):
            total = jnp.zeros((fold, 128), F32)
            for a in range(LATS):
                piece = roll(r4a[u, a, span // 2 :, :], 16 * a - 8 * g)
                total = jnp.where(slot4 == a, piece, total)
            carried.append(total)
        carried = halves(jnp.concatenate(carried, axis=0) * ct[here, :])
        carried = dot3(carried, (q_hi[...], q_lo[...]))
        out[0, here, :] = field[0] - weight * carried[:, SIDE:]
        out[1, here, :] = field[1] + weight * carried[:, :SIDE]

        def add_part(e, inner):
            twist = row(block(3 + e), 0)
            y = wide_dft(*cmul(field, twist))
            y = wide_inverse(*cmul(y, (kf[e, 0, here, :], kf[e, 1, here, :])))
            y = cmul(y, conj(twist))
            for c in (0, 1):
                out[c, here, :] = out[c, here, :] + y[c]
            return inner

        lax.fori_loop(0, 2, add_part, 0)
        return carry

    lax.fori_loop(0, 2, finish, 0)

    for copy in first[1]:
        copy.wait_send()
    for h in range(2):
        for u in range(2):
            for d in range(1, LATS):
                sems = ss4.at[h, u], rs4.at[h, u]
                lat_send(s4[h].at[u], r4[h].at[u], *sems, d).wait_send()
    for h in range(2):
        each(lambda d, h=h: to_rows(h, d).wait_send())
    each(lambda d: to_columns(1, d).wait_send())


def fused(light_field, lateral_phase, spectral_phase, occupation, bin_decay, bin_detune, group_bin):
    tile = (SIDE, 128)
    vmem, sems = pltpu.VMEM, pltpu.SemaphoreType.DMA
    exchange = [
        vmem((2, LATS, SIDE // 2, 128), F32), vmem((2, LATS, SIDE // 2, 128), F32),
        vmem((2, LATS, SIDE // 2, 128), F32), vmem((2, TIMES, LATS, PART, 128), F32),
        vmem((TIMES, LATS, PART + 8, 128), F32), vmem((LATS, TIMES, PART + 8, 128), F32),
        vmem((TIMES, LATS, PART, 128), F32), vmem((LATS, TIMES, PART, 128), F32),
        vmem((2, LATS, 5 * SIDE // 16, 128), F32), vmem((2, LATS, 5 * SIDE // 16, 128), F32),
        vmem((2, LATS, SIDE // 4, 128), F32), vmem((2, LATS, SIDE // 4, 128), F32),
    ]
    tables = [vmem((LATS,) + tile, F32)] * 2 + [vmem((LATS, SIDE // 2, 128), F32)] * 2
    tables += [vmem((LATS,) + tile, F32)] * 2 + [vmem(tile, F32)]
    tables += [vmem((128, 2 * SIDE), BF16)] * 2 + [vmem((2 * SIDE, 2 * SIDE), BF16)] * 2
    tables += [vmem((3, 2, SIDE, SIDE), F32)] * 2 + [vmem((2, 2, SIDE, SIDE), F32)]
    tables += [vmem((2, SIDE, SIDE), F32)] * 3
    tables += [vmem((2, TIMES, SIDE), F32)]
    fixed = constants()
    tables += [vmem(light_field.shape, F32), vmem(occupation.shape, F32)]
    tables += [vmem(c.shape, c.dtype) for c in fixed]
    semaphores = [sems((2, LATS))] * 2 + [sems((2, TOTAL))] * 4 + [sems((2, 2, LATS))] * 2
    semaphores += [sems((2 + len(fixed),))]
    in_vmem, anywhere = pl.BlockSpec(memory_space=pltpu.VMEM), pl.BlockSpec(memory_space=pl.ANY)
    return pl.pallas_call(
        kernel,
        out_shape=jax.ShapeDtypeStruct(light_field.shape, F32),
        in_specs=[anywhere] + [in_vmem] * 2 + [anywhere] + [in_vmem] * 3 + [anywhere] * len(fixed),
        out_specs=pl.BlockSpec(memory_space=pltpu.VMEM),
        scratch_shapes=exchange + tables + semaphores,
        compiler_params=pltpu.CompilerParams(
            collective_id=0, has_side_effects=True, vmem_limit_bytes=56 * 1024 * 1024
        ),
    )(
        light_field,
        lateral_phase.reshape(SIDE, LATS),
        spectral_phase.reshape(SIDE, TIMES).T,
        occupation,
        bin_decay[None],
        bin_detune[None],
        group_bin[None],
        *[jnp.asarray(c) for c in fixed],
    )


def solution(mesh):
    def local(light_field, *rest):
        fits = (lax.axis_size("lat"), lax.axis_size("tm")) == (LATS, TIMES)
        fits = fits and light_field.shape == (2, SIDE, SIDE)
        fits = fits and rest[2].shape == (128, SIDE) and rest[3].shape == (BIN_COUNT,)
        return (fused if fits else on_device)(light_field, *rest)

    return jax.shard_map(
        local,
        mesh=mesh,
        in_specs=(P(None, "lat", "tm"), P(), P(), P(None, "lat"), P(), P(), P()),
        out_specs=P(None, "lat", "tm"),
        check_vma=False,
    )
```

```python
import functools
import math

import jax
import jax.numpy as jnp
import numpy as np
from jax import lax
from jax.experimental import pallas as pl
from jax.experimental.pallas import tpu as pltpu
from jax.sharding import PartitionSpec as P

STRETCH = 128
STEPS = 2


GAIN_SCALE = 0.5


def carried_in(value, axis, join, neutral):
    count, mine = (lax.axis_size(axis), lax.axis_index(axis))
    pieces = jax.tree.map(lambda part: lax.all_gather(part, axis), value)
    so_far = jax.tree.map(
        lambda part, zero: jnp.full_like(part, 0) + jnp.asarray(zero, part.dtype), value, neutral
    )

    def lap(position, so_far):
        longer = join(so_far, jax.tree.map(lambda part: part[position], pieces))
        return jax.tree.map(lambda new, old: jnp.where(position < mine, new, old), longer, so_far)

    return lax.fori_loop(0, count - 1, lap, so_far)


def complex_einsum(form, left, right):
    exact = lax.Precision.HIGHEST
    real_part = jnp.einsum(form, left[0], right[0], precision=exact) - jnp.einsum(
        form, left[1], right[1], precision=exact
    )
    imag_part = jnp.einsum(form, left[0], right[1], precision=exact) + jnp.einsum(
        form, left[1], right[0], precision=exact
    )
    return (real_part, imag_part)


def complex_times(left, right):
    return (left[0] * right[0] - left[1] * right[1], left[0] * right[1] + left[1] * right[0])


def angle_table(height, breadth, modulus, sign):
    first = jnp.arange(height, dtype=jnp.int32)[:, None]
    second = jnp.arange(breadth, dtype=jnp.int32)[None, :]
    turns = (first * second % modulus).astype(jnp.float32) * (2.0 * math.pi / modulus)
    return (jnp.cos(turns), sign * jnp.sin(turns))


def time_forward(grid, small_table, twiddle, long_table):
    mixed = complex_einsum("ka,rab->rkb", small_table, grid)
    mixed = complex_times(mixed, twiddle)
    return complex_einsum("rkb,bq->rkq", mixed, long_table)


def time_inverse(spectrum, small_table, twiddle, long_table, length):
    mixed = complex_einsum("rkq,qb->rkb", spectrum, long_table)
    mixed = complex_times(mixed, twiddle)
    result = complex_einsum("ak,rkb->rab", small_table, mixed)
    return (result[0] / length, result[1] / length)


def powers(decay_rate, detuning, exponent):
    magnitude = jnp.exp(-decay_rate * exponent)
    phase_angle = detuning * exponent
    return (magnitude * jnp.cos(phase_angle), -magnitude * jnp.sin(phase_angle))


def on_device(
    light_field, lateral_phase, spectral_phase, occupation, bin_decay, bin_detune, group_bin
):
    lat_count = lax.axis_size("lat")
    time_count = lax.axis_size("tm")
    height = light_field.shape[1]
    span = light_field.shape[2]
    lateral_total = height * lat_count
    time_total = span * time_count
    groups = occupation.shape[0]
    slab = height // time_count
    narrow = span // lat_count
    exact = lax.Precision.HIGHEST
    lat_forward = angle_table(lateral_total, lateral_total, lateral_total, -1.0)
    lat_backward = angle_table(lateral_total, lateral_total, lateral_total, 1.0)
    lateral_turn = (jnp.cos(lateral_phase)[:, None], jnp.sin(lateral_phase)[:, None])
    small_back = angle_table(time_count, time_count, time_count, 1.0)
    twiddle_back = angle_table(time_count, span, time_total, 1.0)
    long_back = angle_table(span, span, span, 1.0)
    spectral_grid = spectral_phase.reshape(span, time_count).T
    spectral_turn = (jnp.cos(spectral_grid), jnp.sin(spectral_grid))
    bins = jnp.arange(bin_decay.shape[0], dtype=jnp.int32)
    onehot = (group_bin[:, None] == bins[None, :]).astype(jnp.float32)
    decay_rate = jnp.dot(onehot, bin_decay, precision=exact)
    detuning = jnp.dot(onehot, bin_detune, precision=exact)
    coupling = jnp.sqrt(-jnp.expm1(-2.0 * decay_rate))[:, None] * occupation
    lags = jnp.arange(STRETCH + 1, dtype=jnp.float32)[:, None]
    lag_powers = powers(decay_rate, detuning, lags)
    lag_grid = (
        jnp.arange(STRETCH, dtype=jnp.int32)[:, None]
        - jnp.arange(STRETCH, dtype=jnp.int32)[None, :]
    )
    inside = (lag_grid >= 0)[None]
    clipped = jnp.maximum(lag_grid, 0)
    leading = (lag_powers[0][1:].T, lag_powers[1][1:].T)
    trailing = (lag_powers[0][:STRETCH][::-1], lag_powers[1][:STRETCH][::-1])
    stretch_step = (lag_powers[0][STRETCH][:, None], lag_powers[1][STRETCH][:, None])
    device_step = powers(decay_rate, detuning, jnp.float32(span))
    weight = GAIN_SCALE / math.sqrt(groups)
    small_forward = angle_table(time_count, time_count, time_count, -1.0)
    twiddle_forward = angle_table(time_count, span, time_total, -1.0)
    long_forward = angle_table(span, span, span, -1.0)
    current = light_field
    block_toeplitz = (
        jnp.where(
            inside,
            jnp.take(
                jnp.dot(coupling.T, lag_powers[0][:STRETCH].T, precision=exact), clipped, axis=1
            ),
            0.0,
        ),
        jnp.where(
            inside,
            jnp.take(
                jnp.dot(coupling.T, lag_powers[1][:STRETCH].T, precision=exact), clipped, axis=1
            ),
            0.0,
        ),
    )
    for repeat in range(STEPS):
        diffract_stacked = current.reshape(2, height, lat_count, narrow)
        lateral_block = lax.all_to_all(
            diffract_stacked, "lat", split_axis=2, concat_axis=1, tiled=True
        )
        piece = (lateral_block[0, :, 0, :], lateral_block[1, :, 0, :])
        lateral_spectrum = complex_einsum("kx,xn->kn", lat_forward, piece)
        lateral_spectrum = complex_times(lateral_spectrum, lateral_turn)
        lateral_result = complex_einsum("xk,kn->xn", lat_backward, lateral_spectrum)
        lateral_joined = (
            jnp.stack([lateral_result[0], lateral_result[1]])[:, :, None, :] / lateral_total
        )
        diffract_turned = lax.all_to_all(
            lateral_joined, "lat", split_axis=1, concat_axis=2, tiled=True
        )
        stacked = diffract_turned.reshape(2, height, span).reshape(2, time_count, slab, span)
        rows = lax.all_to_all(stacked, "tm", split_axis=1, concat_axis=3, tiled=True)[:, 0]
        rows_here = rows.shape[1]
        grid = (
            rows[0].reshape(rows_here, time_count, span),
            rows[1].reshape(rows_here, time_count, span),
        )
        spectrum = time_forward(grid, small_forward, twiddle_forward, long_forward)
        spectrum = complex_times(spectrum, spectral_turn)
        result = time_inverse(spectrum, small_back, twiddle_back, long_back, time_total)
        joined = jnp.stack(
            [result[0].reshape(rows_here, time_total), result[1].reshape(rows_here, time_total)]
        )[:, None]
        turned = lax.all_to_all(joined, "tm", split_axis=3, concat_axis=1, tiled=True)
        current = turned.reshape(2, height, span)
        amplify_rows_here = current.shape[1]
        length = current.shape[2]
        count = length // STRETCH
        amplify_grid = (
            current[0].reshape(amplify_rows_here, count, STRETCH),
            current[1].reshape(amplify_rows_here, count, STRETCH),
        )
        direct = complex_einsum("xji,xci->xcj", block_toeplitz, amplify_grid)
        projected = complex_einsum("xci,ig->cgx", amplify_grid, trailing)
        stretch_ends = (coupling[None] * projected[0], coupling[None] * projected[1])

        def chain_step(running, ends):
            moved = complex_times(stretch_step, running)
            return ((moved[0] + ends[0], moved[1] + ends[1]), running)

        zero_state = jnp.zeros((groups, amplify_rows_here), jnp.float32)
        running, chain = lax.scan(chain_step, (zero_state, zero_state), stretch_ends)

        def combine(earlier, later):
            joint = complex_times((earlier[0], earlier[1]), (later[0], later[1]))
            carried = complex_times(
                (later[0][:, None], later[1][:, None]), (earlier[2], earlier[3])
            )
            return (joint[0], joint[1], carried[0] + later[2], carried[1] + later[3])

        identity = (
            jnp.ones((groups,), jnp.float32),
            jnp.zeros((groups,), jnp.float32),
            jnp.zeros_like(running[0]),
            jnp.zeros_like(running[1]),
        )
        prefix = carried_in(
            (device_step[0], device_step[1], running[0], running[1]), "tm", combine, identity
        )
        starts = powers(
            decay_rate, detuning, (jnp.arange(count, dtype=jnp.float32) * STRETCH)[:, None]
        )
        before = complex_times(
            (starts[0][:, :, None], starts[1][:, :, None]), (prefix[2][None], prefix[3][None])
        )
        states = (before[0] + chain[0], before[1] + chain[1])
        delayed = complex_einsum("cgx,gj->xcj", states, leading)
        summed_re = (direct[0] + delayed[0]).reshape(amplify_rows_here, length)
        summed_im = (direct[1] + delayed[1]).reshape(amplify_rows_here, length)
        current = jnp.stack([current[0] - weight * summed_im, current[1] + weight * summed_re])
    return current


LATS, TIMES, SIDE, BIN_COUNT = 4, 8, 256, 32
TOTAL = LATS * TIMES
WIDE = LATS * SIDE
LONG = TIMES * SIDE
ROWS = SIDE // TIMES
PART = ROWS // 2
F32, BF16 = jnp.float32, jnp.bfloat16
MESH = pl.DeviceIdType.MESH


@functools.cache
def constants():
    j = np.arange(SIDE)
    w = np.exp(-2j * np.pi * (np.outer(j, j) % SIDE) / SIDE)
    big = np.block([[w.real, w.imag], [-w.imag, w.real]]).astype(np.float32)
    big_hi = big.astype(jnp.bfloat16)
    big_lo = (big - big_hi.astype(np.float32)).astype(jnp.bfloat16)
    tw8 = np.exp(-2j * np.pi * np.outer(np.arange(TIMES), j) / LONG)
    tau = np.exp(-1j * np.pi * np.arange(LONG).reshape(TIMES, SIDE) / LONG)
    tau2 = np.exp(-1j * np.pi * j / SIDE)[None]
    rows = np.concatenate([tw8, tau, tau2, np.zeros((7, SIDE))])
    rows = np.stack([rows.real, rows.imag]).astype(np.float32)
    tw4 = np.exp(-2j * np.pi * np.outer(j, np.arange(LATS)) / WIDE)
    cols = np.concatenate([tw4.real, tw4.imag], axis=1).astype(np.float32)
    return (big_hi, big_lo, rows, cols)


def halves(x):
    hi = x.astype(BF16)
    return hi, (x - hi.astype(F32)).astype(BF16)


def dot(a, b):
    return jnp.dot(a, b, preferred_element_type=F32)


def dot3(a, b):
    return dot(a[0], b[0]) + dot(a[1], b[0]) + dot(a[0], b[1])


def cmul(a, b):
    return (a[0] * b[0] - a[1] * b[1], a[0] * b[1] + a[1] * b[0])


def conj(a):
    return (a[0], -a[1])


def small_fft(items, sign):
    count = len(items)
    if count == 1:
        return items
    even, odd = small_fft(items[0::2], sign), small_fft(items[1::2], sign)
    low, high = [], []
    for k in range(count // 2):
        re, im = odd[k]
        if 8 * k == count:
            r = math.sqrt(0.5)
            re, im = (re - sign * im) * r, (im + sign * re) * r
        elif 4 * k == count:
            re, im = -sign * im, sign * re
        elif 8 * k == 3 * count:
            r = math.sqrt(0.5)
            re, im = (-re - sign * im) * r, (-im + sign * re) * r
        low.append((even[k][0] + re, even[k][1] + im))
        high.append((even[k][0] - re, even[k][1] - im))
    return low + high


def lane_iota(shape):
    return lax.broadcasted_iota(jnp.int32, shape, len(shape) - 1)


def roll(x, shift):
    shift = shift % 128
    return pltpu.roll(x, shift, axis=x.ndim - 1) if shift else x


def pack(re, im):
    tiles = []
    first = lane_iota((re.shape[0], 128)) < 64
    for p in range(re.shape[1] // 128):
        a, b = re[:, 128 * p : 128 * p + 128], im[:, 128 * p : 128 * p + 128]
        tiles.append(jnp.where(first, a, roll(b, 64)))
        tiles.append(jnp.where(first, roll(a, 64), b))
    return tiles


def lane_part(shape):
    return lane_iota(shape) // 32


def pack_halves(re, im):
    part = lane_part((re[0].shape[0], 128))
    tiles = {}
    for l in range(LATS):
        for h in range(2):
            at = 2 * (l % 2) + h
            tile = None
            for q, source in enumerate((re[0], re[1], im[0], im[1])):
                piece = roll(source[:, 128 * (l // 2) : 128 * (l // 2) + 128], 32 * (q - at))
                tile = piece if tile is None else jnp.where(part == q, piece, tile)
            tiles[l, h] = tile
    return tiles


def unpack_halves(tiles):
    part = lane_part(tiles[0, 0].shape)
    done = []
    for q in range(4):
        joined = []
        for p in range(LATS // 2):
            value = None
            for at in range(4):
                piece = roll(tiles[2 * p + at // 2, at % 2], 32 * (at - q))
                value = piece if value is None else jnp.where(part == at, piece, value)
            joined.append(value)
        done.append(jnp.concatenate(joined, axis=1))
    return done[:2], done[2:]


def join_rows(a, b):
    count, width = a.shape
    a, b = (x.reshape(count // PART, PART, width) for x in (a, b))
    return jnp.stack([a, b], axis=1).reshape(2 * count, width)


def part_rows(x):
    x = x.reshape(x.shape[0] // ROWS, 2, PART, x.shape[1])
    return tuple(x[:, i].reshape(-1, x.shape[-1]) for i in (0, 1))


def turn(x):
    first = lane_iota(x.shape) < 64
    y = roll(x, 64)
    return jnp.where(first, -y, y)


def kernel(
    lf_hbm, latp, specp, occ_hbm, dec_ref, det_ref, gb_ref, wh_hbm, wl_hbm, rows_hbm, cols_hbm,
    out,
    s1, r1, s2, r2, s3a, r3a, s3b, r3b, s4a, r4a, s4b, r4b,
    tw_c, tw_s, th_c, th_s, ph_c, ph_s, ct, q_hi, q_lo, p_hi, p_lo, kev, kod, kfe, kfo, spec,
    lf, occ, wh, wl, rows_ref, cols_ref,
    ss1, rs1, ss2, rs2, ss3, rs3, ss4, rs4, load_sem,
):
    loads = []
    for i, (src, dst) in enumerate((
        (lf_hbm, lf), (cols_hbm, cols_ref), (wh_hbm, wh), (wl_hbm, wl), (occ_hbm, occ),
        (rows_hbm, rows_ref),
    )):
        loads.append(pltpu.make_async_copy(src, dst, load_sem.at[i]))
        loads[-1].start()
    l, m = lax.axis_index("lat"), lax.axis_index("tm")
    weight = GAIN_SCALE / math.sqrt(occ.shape[0])

    half = TIMES // 2

    lats = [l] + [lax.rem(l + d, LATS) for d in range(1, LATS)]
    side = m // half
    sides = [lax.rem(side + 1, 2) * half, side * half]
    steps = [lax.rem(m + d, half) for d in range(half)]
    times = [[sides[i] + step for step in steps] for i in (0, 1)]
    others = []
    for d in range(TOTAL // 2):
        for i in (0, 1):
            if i == 0 or d:
                others.append((lats[d // half], times[i][d % half]))

    def each(act):
        for tl, tm in others:
            act(tl, tm)

    barrier = pltpu.get_barrier_semaphore()

    def greet(tl, tm):
        pl.semaphore_signal(barrier, inc=1, device_id=(tl, tm), device_id_type=MESH)

    each(greet)

    def remote(src, dst, send, recv, tl, tm):
        return pltpu.make_async_remote_copy(
            src_ref=src, dst_ref=dst, send_sem=send, recv_sem=recv,
            device_id=(tl, tm), device_id_type=MESH,
        )

    def lat_send(s, r, ss, rs, d):
        return remote(s.at[lats[d]], r.at[l], ss, rs, lats[d], m)

    def all_of(ref, count, ss, rs):
        part = ref.at[pl.ds(0, count)]
        return remote(part, part, ss, rs, lats[1], m)

    s3, r3 = (s3a, s3b), (r3a, r3b)

    def to_rows(h, tl, tm):
        src = s2.at[h, tl, pl.ds(pl.multiple_of(tm * PART, PART), PART)]
        return remote(src, r2.at[h, m * LATS + l], ss2.at[h], rs2.at[h], tl, tm)

    def to_columns(h, tl, tm):
        dst = r3[h].at[l * TIMES + m]
        return remote(s3[h].at[tm * LATS + tl], dst, ss3.at[h], rs3.at[h], tl, tm)

    def rows_all(h):
        return all_of(r2.at[h], TOTAL - 1, ss2.at[h], rs2.at[h])

    def columns_all(h):
        return all_of(r3[h], TOTAL - 1, ss3.at[h], rs3.at[h])

    loads[0].wait()
    for (t, h), tile in pack_halves(part_rows(lf[0]), part_rows(lf[1])).items():
        s1[h, t] = tile
    pl.semaphore_wait(barrier, TOTAL - 1)
    first = [
        [lat_send(s1.at[h], r1.at[h], ss1.at[h], rs1.at[h], d) for d in range(1, LATS)]
        for h in range(2)
    ]
    for copy in first[0]:
        copy.start()
    for h in range(2):
        r1[h, l] = s1[h, l]

    loads[1].wait()
    whole = (SIDE, 128)
    group = lax.rem(lane_iota(whole), 64) // 16
    sign = jnp.where(lane_iota(whole) < 64, -1.0, 1.0)
    phase = latp[...]
    turn_c, turn_s = jnp.cos(phase) * (1.0 / WIDE), jnp.sin(phase) * (1.0 / WIDE)
    second_set = lax.rem(lane_part((SIDE // 2, 128)), 2) == 1
    second_key = lax.rem(lane_part(whole), 2) == 1
    for k in range(LATS):
        tw_c[k] = jnp.broadcast_to(cols_ref[:, k : k + 1], whole)
        tw_s[k] = jnp.broadcast_to(cols_ref[:, LATS + k : LATS + k + 1], whole) * sign
        ph_c[k] = jnp.broadcast_to(turn_c[:, k : k + 1], whole)
        ph_s[k] = jnp.broadcast_to(turn_s[:, k : k + 1], whole) * sign
        for full, parted in ((tw_c, th_c), (tw_s, th_s)):
            one, two = part_rows(full[k])
            parted[k] = jnp.where(second_set, two, one)

    def wide_dft(re, im):
        x = halves(jnp.concatenate([re, im], axis=1))
        y = dot3(x, (wh[...], wl[...]))
        return y[:, :SIDE], y[:, SIDE:]

    def wide_inverse(re, im):
        return conj(wide_dft(re, -im))

    def row(k):
        return rows_ref[0, k : k + 1, :], rows_ref[1, k : k + 1, :]

    def stack(items):
        return tuple(jnp.concatenate([item[c] for item in items], axis=0) for c in (0, 1))

    def unstack(value):
        return [tuple(v[ROWS * k : ROWS * (k + 1)] for v in value) for k in range(TIMES)]

    def time_dft(items):
        items = small_fft(items, -1)
        return wide_dft(*stack([cmul(item, row(k)) for k, item in enumerate(items)]))

    def time_inverse_dft(value):
        items = unstack(wide_inverse(*value))
        return small_fft([cmul(item, conj(row(k))) for k, item in enumerate(items)], 1)

    def twist(items, back):
        rows = [row(TIMES + k) for k in range(TIMES)]
        return [cmul(x, conj(r) if back else r) for x, r in zip(items, rows)]

    def column_dft(x, low, high):
        w = [
            jnp.concatenate([ref[low:high, :SIDE], ref[SIDE + low : SIDE + high, :SIDE]], axis=0)
            for ref in (wh, wl)
        ]
        y = dot3(w, halves(x))
        count = high - low
        return [
            (y[:count, k : k + 128], y[count:, k : k + 128]) for k in range(0, x.shape[1], 128)
        ]

    def butterfly(x, tables, back):
        a, b, c, d = x[0] + x[2], x[0] - x[2], x[1] + x[3], turn(x[1] - x[3])
        if back:
            return [a + c, b + d, a - c, b - d]
        across, along = tables
        y = [a + c, b - d, a - c, b + d]
        return [y[0]] + [y[k] * across[k] + roll(y[k], 64) * along[k] for k in (1, 2, 3)]

    def lateral_spectrum(x, states):
        y = butterfly(x, (th_c, th_s), False)
        spectrum, turns = [], []
        for k in (0, 2):
            one = jnp.where(second_set, roll(y[k + 1], 32), y[k])
            two = jnp.where(second_set, y[k + 1], roll(y[k], -32))
            spectrum.append(join_rows(one, two))
            turns.append(tuple(jnp.where(second_key, t[k + 1], t[k]) for t in (ph_c, ph_s)))
        if states:
            y = butterfly(states, (tw_c, tw_s), False)
            tile, across, along = y[0], ph_c[0], ph_s[0]
            for k in range(1, LATS):
                tile = jnp.where(group == k, roll(y[k], 16 * k), tile)
                across = jnp.where(group == k, ph_c[k], across)
                along = jnp.where(group == k, ph_s[k], along)
            spectrum.append(tile)
            turns.append((across, along))
        spectrum = column_dft(jnp.concatenate(spectrum, axis=1), 0, SIDE)
        done = []
        for (top, bottom), (across, along) in zip(spectrum, turns):
            y = top - turn(bottom)
            done.append(y * across + roll(y, 64) * along)
        return jnp.concatenate(done, axis=1)

    def untwiddle(y, tables, low, high):
        across, along = tables
        for k in (1, 2, 3):
            y[k] = y[k] * across[k, low:high, :] - roll(y[k], 64) * along[k, low:high, :]
        return butterfly(y, None, True)

    def lateral_inverse(spectrum, low, high):
        result = [top + turn(bottom) for top, bottom in column_dft(spectrum, low, high)]
        mask = second_set[: (high - low) // 2]
        y = []
        for tile in result[:2]:
            one, two = part_rows(tile)
            y.append(jnp.where(mask, roll(two, 32), one))
            y.append(jnp.where(mask, two, roll(one, -32)))
        done = [untwiddle(y, (th_c, th_s), low // 2, high // 2)]
        if len(result) > 2:
            y = [roll(result[2], -16 * k) for k in range(LATS)]
            done.append(untwiddle(y, (tw_c, tw_s), low, high))
        return done

    loads[2].wait()
    loads[3].wait()
    def first_all(h):
        return all_of(r1.at[h], LATS - 1, ss1.at[h], rs1.at[h])

    first_all(0).wait_send()
    for copy in first[1]:
        copy.start()
    for h in range(2):
        first_all(h).wait_recv()
        spectrum = lateral_spectrum([r1[h, a] for a in range(LATS)], None)
        for a, tile in enumerate(lateral_inverse(spectrum, 0, SIDE)[0]):
            s2[h, a] = tile
        each(lambda tl, tm, h=h: to_rows(h, tl, tm).start())
        r2[h, m * LATS + l] = s2[h, l, pl.ds(pl.multiple_of(m * PART, PART), PART)]

    loads[4].wait()
    loads[5].wait()
    spec[0] = jnp.cos(specp[...]) * (1.0 / LONG)
    spec[1] = jnp.sin(specp[...]) * (1.0 / LONG)

    dec_row, det_row = dec_ref[...], det_ref[...]
    square = (BIN_COUNT, BIN_COUNT)
    eye = lax.broadcasted_iota(jnp.int32, square, 0) == lax.broadcasted_iota(jnp.int32, square, 1)
    dec_col = jnp.sum(jnp.where(eye, dec_row, 0.0), axis=1, keepdims=True)
    det_col = jnp.sum(jnp.where(eye, det_row, 0.0), axis=1, keepdims=True)
    lag = lane_iota((BIN_COUNT, SIDE)).astype(F32)

    def power(exponent, rate, angle):
        size = jnp.exp(-rate * exponent)
        return size * jnp.cos(angle * exponent), -size * jnp.sin(angle * exponent)

    def bin_of(q):
        part = lax.rem(q, 64)
        within = lax.rem(part, 16)
        return jnp.where(within < 8, (part // 16) * 8 + within, -1)

    q_row = lax.broadcasted_iota(jnp.int32, (128, BIN_COUNT), 0)
    spread = (bin_of(q_row) == lane_iota((128, BIN_COUNT))).astype(BF16)
    q_lane = lane_iota((BIN_COUNT, 128))
    pick = bin_of(q_lane) == lax.broadcasted_iota(jnp.int32, (BIN_COUNT, 128), 0)
    dec_lane = jnp.sum(jnp.where(pick, dec_col, 0.0), axis=0, keepdims=True)
    det_lane = jnp.sum(jnp.where(pick, det_col, 0.0), axis=0, keepdims=True)
    ahead = power(lag, dec_col, det_col)
    is_re = lax.broadcasted_iota(jnp.int32, (128, SIDE), 0) < 64
    (re_hi, re_lo), (im_hi, im_lo) = halves(ahead[0]), halves(ahead[1])
    for ref, re, im in ((q_hi, re_hi, im_hi), (q_lo, re_lo, im_lo)):
        re, im = dot(spread, re), dot(spread, im)
        ref[:, :SIDE] = jnp.where(is_re, re, -im).astype(BF16)
        ref[:, SIDE:] = jnp.where(is_re, im, re).astype(BF16)
    lane = lane_iota((BIN_COUNT, SIDE))
    inner = lax.rem(lane, 16)
    held = jnp.where(inner < 8, (lane // 64) * 8 + inner, -1)
    held = held == lax.broadcasted_iota(jnp.int32, (BIN_COUNT, SIDE), 0)
    held_b = held.astype(BF16)
    step_dec = jnp.sum(jnp.where(held, dec_col, 0.0), axis=0, keepdims=True)
    step_det = jnp.sum(jnp.where(held, det_col, 0.0), axis=0, keepdims=True)
    behind = power(SIDE - lag, dec_col, det_col)
    for ref, which in ((p_hi, 0), (p_lo, 1)):
        re = halves(behind[0])[which].astype(F32).T.astype(BF16)
        im = halves(behind[1])[which].astype(F32).T.astype(BF16)
        re, im = dot(re, held_b), dot(im, held_b)
        ref[:SIDE, :SIDE] = re.astype(BF16)
        ref[:SIDE, SIDE:] = im.astype(BF16)
        ref[SIDE:, :SIDE] = (-im).astype(BF16)
        ref[SIDE:, SIDE:] = re.astype(BF16)
    y = 2.0 * dec_lane
    series = jnp.ones_like(y)
    for n in range(9, 1, -1):
        series = 1.0 - series * y * (1.0 / n)
    drive = jnp.sqrt(y * series)
    bins_here = bin_of(lax.broadcasted_iota(jnp.int32, (128, occ.shape[0]), 0))
    member = (bins_here == gb_ref[...]).astype(BF16)
    occ_hi, occ_lo = halves(occ[...])
    ct[...] = (dot(member, occ_hi) + dot(member, occ_lo)).T * drive

    first_half = lane_iota((1, 128)) < 64
    far = []
    for k in range(TIMES):
        far.append(jnp.where(first_half, *power(float(SIDE * k), dec_lane, det_lane)))
    mine = ct[pl.ds(pl.multiple_of(m * ROWS, ROWS), ROWS), :]
    q = (q_hi[...], q_lo[...])
    response = dot3(halves(jnp.concatenate([mine * f for f in far], axis=0)), q)
    response = unstack((response[:, :SIDE], response[:, SIDE:]))
    even = time_dft(response)
    kev[0] = LONG * (1.0 - (0.5 * weight) * even[1])
    kev[1] = (LONG * 0.5 * weight) * even[0]
    odd = time_dft(twist(response, False))
    kod[0] = (-0.5 * weight / LONG) * odd[1]
    kod[1] = (0.5 * weight / LONG) * odd[0]

    for h in range(2):
        rows_all(h).wait_recv()
    field = []
    for k in range(TIMES):
        re, im = unpack_halves({(a, h): r2[h, k * LATS + a] for a in range(LATS) for h in range(2)})
        field.append((jnp.concatenate(re, axis=0), jnp.concatenate(im, axis=0)))
    turn_row = stack([
        tuple(jnp.broadcast_to(spec[c, k : k + 1, :], (ROWS, SIDE)) for c in (0, 1))
        for k in range(TIMES)
    ])
    once = cmul(time_dft(field), turn_row)
    twisted = time_dft(twist(time_inverse_dft(once), False))
    twisted = time_inverse_dft(cmul(twisted, (kod[0], kod[1])))
    late = time_dft(twist(twisted, True))
    straight = cmul(once, (kev[0], kev[1]))
    once = cmul((straight[0] + late[0], straight[1] + late[1]), turn_row)
    field = time_inverse_dft(once)
    flat = stack(field)
    ends = dot3(halves(jnp.concatenate(flat, axis=1)), (p_hi[...], p_lo[...]))
    ends = unstack((ends[:, :SIDE], ends[:, SIDE:]))
    step = power(float(SIDE), step_dec, step_det)
    slot = lax.rem(lane_iota((8, SIDE)) // 16, 4)
    state = (jnp.zeros((ROWS, SIDE), F32), jnp.zeros((ROWS, SIDE), F32))
    for k in range(TIMES):
        folded = []
        for c in (0, 1):
            total = state[c][:8]
            for g in range(1, 4):
                total = jnp.where(slot == g, state[c][8 * g : 8 * g + 8], total)
            folded.append(total)
        for a, tile in enumerate(pack(*folded)):
            s3a[k * LATS + a, PART:, :] = tile
        moved = cmul(state, step)
        state = (moved[0] + ends[k][0], moved[1] + ends[k][1])
        re, im = ((v[:PART], v[PART:]) for v in field[k])
        for (a, h), tile in pack_halves(re, im).items():
            s3[h][k * LATS + a, :PART, :] = tile
    each(lambda tl, tm: to_columns(0, tl, tm).start())
    for h in range(2):
        r3[h][l * TIMES + m] = s3[h][m * LATS + l]

    t2 = rows_ref[0, 2 * TIMES : 2 * TIMES + 1, :], rows_ref[1, 2 * TIMES : 2 * TIMES + 1, :]
    q = (q_hi[...], q_lo[...])
    response = dot3(halves(jnp.where(lane_iota(whole) < 64, ct[...], 0.0)), q)
    response = (response[:, :SIDE], response[:, SIDE:])
    even, odd = wide_dft(*response), wide_dft(*cmul(response, t2))
    gain = 0.5 * weight / SIDE
    kfe[0], kfe[1] = -gain * even[1], gain * even[0]
    kfo[0], kfo[1] = -gain * odd[1], gain * odd[0]

    columns_all(0).wait_send()
    each(lambda tl, tm: to_columns(1, tl, tm).start())
    span = SIDE // 2
    fold = span // 8
    slot = lax.rem(lane_iota((fold, 128)), 64) // 8
    s4, r4 = (s4a, s4b), (r4a, r4b)

    def last_all(h, u):
        return all_of(r4[h].at[u], LATS - 1, ss4.at[h, u], rs4.at[h, u])

    for h in range(2):
        columns_all(h).wait_recv()
        tiles, states = [], []
        for a in range(LATS):
            mine = slice(a * TIMES, (a + 1) * TIMES)
            tiles.append(r3[h][mine, :PART, :].reshape(span, 128))
            if h == 0:
                extra = r3a[mine, PART:, :].reshape(8 * TIMES, 128)
                extra = [roll(extra, -16 * g).reshape(TIMES, 8, 128) for g in range(4)]
                states.append(jnp.stack(extra, axis=1).reshape(SIDE, 128))
        spectrum = lateral_spectrum(tiles, states)
        for u in range(2):
            done = lateral_inverse(spectrum, span * u, span * (u + 1))
            for a in range(LATS):
                s4[h][u, a, : span // 2, :] = done[0][a]
                if h == 0:
                    total = done[1][a][:fold]
                    for g in range(1, 8):
                        piece = roll(done[1][a][fold * g : fold * (g + 1)], 8 * g)
                        total = jnp.where(slot == g, piece, total)
                    s4a[u, a, span // 2 :, :] = total
            for d in range(1, LATS):
                sems = ss4.at[h, u], rs4.at[h, u]
                lat_send(s4[h].at[u], r4[h].at[u], *sems, d).start()
            r4[h][u, l] = s4[h][u, l]

    slot = lax.rem(lane_iota((fold, 128)), 64) // 16
    for u in range(2):
        for h in range(2):
            last_all(h, u).wait_recv()
        here = pl.ds(span * u, span)
        re, im = unpack_halves({
            (a, h): r4[h][u, a, : span // 2, :] for a in range(LATS) for h in range(2)
        })
        field = join_rows(*re), join_rows(*im)
        carried = []
        for g in range(8):
            total = jnp.zeros((fold, 128), F32)
            for a in range(LATS):
                piece = roll(r4a[u, a, span // 2 :, :], 16 * a - 8 * g)
                total = jnp.where(slot == a, piece, total)
            carried.append(total)
        carried = halves(jnp.concatenate(carried, axis=0) * ct[here, :])
        carried = dot3(carried, (q_hi[...], q_lo[...]))
        even = wide_inverse(*cmul(wide_dft(*field), (kfe[0, here, :], kfe[1, here, :])))
        odd = wide_dft(*cmul(field, t2))
        odd = wide_inverse(*cmul(odd, (kfo[0, here, :], kfo[1, here, :])))
        odd = cmul(odd, conj(t2))
        out[0, here, :] = field[0] + even[0] + odd[0] - weight * carried[:, SIDE:]
        out[1, here, :] = field[1] + even[1] + odd[1] + weight * carried[:, :SIDE]

    first_all(1).wait_send()
    for h in range(2):
        rows_all(h).wait_send()
        for u in range(2):
            last_all(h, u).wait_send()
    columns_all(1).wait_send()


def fused(light_field, lateral_phase, spectral_phase, occupation, bin_decay, bin_detune, group_bin):
    tile = (SIDE, 128)
    vmem, sems = pltpu.VMEM, pltpu.SemaphoreType.DMA
    exchange = [
        vmem((2, LATS, SIDE // 2, 128), F32), vmem((2, LATS, SIDE // 2, 128), F32),
        vmem((2, LATS, SIDE // 2, 128), F32), vmem((2, TOTAL, PART, 128), F32),
        vmem((TOTAL, PART + 8, 128), F32), vmem((TOTAL, PART + 8, 128), F32),
        vmem((TOTAL, PART, 128), F32), vmem((TOTAL, PART, 128), F32),
        vmem((2, LATS, 5 * SIDE // 16, 128), F32), vmem((2, LATS, 5 * SIDE // 16, 128), F32),
        vmem((2, LATS, SIDE // 4, 128), F32), vmem((2, LATS, SIDE // 4, 128), F32),
    ]
    tables = [vmem((LATS,) + tile, F32)] * 2 + [vmem((LATS, SIDE // 2, 128), F32)] * 2
    tables += [vmem((LATS,) + tile, F32)] * 2 + [vmem(tile, F32)]
    tables += [vmem((128, 2 * SIDE), BF16)] * 2 + [vmem((2 * SIDE, 2 * SIDE), BF16)] * 2
    tables += [vmem((2, SIDE, SIDE), F32)] * 4
    tables += [vmem((2, TIMES, SIDE), F32)]
    fixed = constants()
    tables += [vmem(light_field.shape, F32), vmem(occupation.shape, F32)]
    tables += [vmem(c.shape, c.dtype) for c in fixed]
    semaphores = [sems((2,))] * 6 + [sems((2, 2))] * 2
    semaphores += [sems((2 + len(fixed),))]
    in_vmem, anywhere = pl.BlockSpec(memory_space=pltpu.VMEM), pl.BlockSpec(memory_space=pl.ANY)
    return pl.pallas_call(
        kernel,
        out_shape=jax.ShapeDtypeStruct(light_field.shape, F32),
        in_specs=[anywhere] + [in_vmem] * 2 + [anywhere] + [in_vmem] * 3 + [anywhere] * len(fixed),
        out_specs=pl.BlockSpec(memory_space=pltpu.VMEM),
        scratch_shapes=exchange + tables + semaphores,
        compiler_params=pltpu.CompilerParams(
            collective_id=0, has_side_effects=True, vmem_limit_bytes=56 * 1024 * 1024
        ),
    )(
        light_field,
        lateral_phase.reshape(SIDE, LATS),
        spectral_phase.reshape(SIDE, TIMES).T,
        occupation,
        bin_decay[None],
        bin_detune[None],
        group_bin[None],
        *[jnp.asarray(c) for c in fixed],
    )


def solution(mesh):
    def local(light_field, *rest):
        fits = (lax.axis_size("lat"), lax.axis_size("tm")) == (LATS, TIMES)
        fits = fits and light_field.shape == (2, SIDE, SIDE)
        fits = fits and rest[2].shape == (128, SIDE) and rest[3].shape == (BIN_COUNT,)
        return (fused if fits else on_device)(light_field, *rest)

    return jax.shard_map(
        local,
        mesh=mesh,
        in_specs=(P(None, "lat", "tm"), P(), P(), P(None, "lat"), P(), P(), P()),
        out_specs=P(None, "lat", "tm"),
        check_vma=False,
    )
```

```python
import functools
import math

import jax
import jax.numpy as jnp
import numpy as np
from jax import lax
from jax.experimental import pallas as pl
from jax.experimental.pallas import tpu as pltpu
from jax.sharding import PartitionSpec as P

STRETCH = 128
STEPS = 2


GAIN_SCALE = 0.5


def carried_in(value, axis, join, neutral):
    count, mine = (lax.axis_size(axis), lax.axis_index(axis))
    pieces = jax.tree.map(lambda part: lax.all_gather(part, axis), value)
    so_far = jax.tree.map(
        lambda part, zero: jnp.full_like(part, 0) + jnp.asarray(zero, part.dtype), value, neutral
    )

    def lap(position, so_far):
        longer = join(so_far, jax.tree.map(lambda part: part[position], pieces))
        return jax.tree.map(lambda new, old: jnp.where(position < mine, new, old), longer, so_far)

    return lax.fori_loop(0, count - 1, lap, so_far)


def complex_einsum(form, left, right):
    exact = lax.Precision.HIGHEST
    real_part = jnp.einsum(form, left[0], right[0], precision=exact) - jnp.einsum(
        form, left[1], right[1], precision=exact
    )
    imag_part = jnp.einsum(form, left[0], right[1], precision=exact) + jnp.einsum(
        form, left[1], right[0], precision=exact
    )
    return (real_part, imag_part)


def complex_times(left, right):
    return (left[0] * right[0] - left[1] * right[1], left[0] * right[1] + left[1] * right[0])


def angle_table(height, breadth, modulus, sign):
    first = jnp.arange(height, dtype=jnp.int32)[:, None]
    second = jnp.arange(breadth, dtype=jnp.int32)[None, :]
    turns = (first * second % modulus).astype(jnp.float32) * (2.0 * math.pi / modulus)
    return (jnp.cos(turns), sign * jnp.sin(turns))


def time_forward(grid, small_table, twiddle, long_table):
    mixed = complex_einsum("ka,rab->rkb", small_table, grid)
    mixed = complex_times(mixed, twiddle)
    return complex_einsum("rkb,bq->rkq", mixed, long_table)


def time_inverse(spectrum, small_table, twiddle, long_table, length):
    mixed = complex_einsum("rkq,qb->rkb", spectrum, long_table)
    mixed = complex_times(mixed, twiddle)
    result = complex_einsum("ak,rkb->rab", small_table, mixed)
    return (result[0] / length, result[1] / length)


def powers(decay_rate, detuning, exponent):
    magnitude = jnp.exp(-decay_rate * exponent)
    phase_angle = detuning * exponent
    return (magnitude * jnp.cos(phase_angle), -magnitude * jnp.sin(phase_angle))


def on_device(
    light_field, lateral_phase, spectral_phase, occupation, bin_decay, bin_detune, group_bin
):
    lat_count = lax.axis_size("lat")
    time_count = lax.axis_size("tm")
    height = light_field.shape[1]
    span = light_field.shape[2]
    lateral_total = height * lat_count
    time_total = span * time_count
    groups = occupation.shape[0]
    slab = height // time_count
    narrow = span // lat_count
    exact = lax.Precision.HIGHEST
    lat_forward = angle_table(lateral_total, lateral_total, lateral_total, -1.0)
    lat_backward = angle_table(lateral_total, lateral_total, lateral_total, 1.0)
    lateral_turn = (jnp.cos(lateral_phase)[:, None], jnp.sin(lateral_phase)[:, None])
    small_back = angle_table(time_count, time_count, time_count, 1.0)
    twiddle_back = angle_table(time_count, span, time_total, 1.0)
    long_back = angle_table(span, span, span, 1.0)
    spectral_grid = spectral_phase.reshape(span, time_count).T
    spectral_turn = (jnp.cos(spectral_grid), jnp.sin(spectral_grid))
    bins = jnp.arange(bin_decay.shape[0], dtype=jnp.int32)
    onehot = (group_bin[:, None] == bins[None, :]).astype(jnp.float32)
    decay_rate = jnp.dot(onehot, bin_decay, precision=exact)
    detuning = jnp.dot(onehot, bin_detune, precision=exact)
    coupling = jnp.sqrt(-jnp.expm1(-2.0 * decay_rate))[:, None] * occupation
    lags = jnp.arange(STRETCH + 1, dtype=jnp.float32)[:, None]
    lag_powers = powers(decay_rate, detuning, lags)
    lag_grid = (
        jnp.arange(STRETCH, dtype=jnp.int32)[:, None]
        - jnp.arange(STRETCH, dtype=jnp.int32)[None, :]
    )
    inside = (lag_grid >= 0)[None]
    clipped = jnp.maximum(lag_grid, 0)
    leading = (lag_powers[0][1:].T, lag_powers[1][1:].T)
    trailing = (lag_powers[0][:STRETCH][::-1], lag_powers[1][:STRETCH][::-1])
    stretch_step = (lag_powers[0][STRETCH][:, None], lag_powers[1][STRETCH][:, None])
    device_step = powers(decay_rate, detuning, jnp.float32(span))
    weight = GAIN_SCALE / math.sqrt(groups)
    small_forward = angle_table(time_count, time_count, time_count, -1.0)
    twiddle_forward = angle_table(time_count, span, time_total, -1.0)
    long_forward = angle_table(span, span, span, -1.0)
    current = light_field
    block_toeplitz = (
        jnp.where(
            inside,
            jnp.take(
                jnp.dot(coupling.T, lag_powers[0][:STRETCH].T, precision=exact), clipped, axis=1
            ),
            0.0,
        ),
        jnp.where(
            inside,
            jnp.take(
                jnp.dot(coupling.T, lag_powers[1][:STRETCH].T, precision=exact), clipped, axis=1
            ),
            0.0,
        ),
    )
    for repeat in range(STEPS):
        diffract_stacked = current.reshape(2, height, lat_count, narrow)
        lateral_block = lax.all_to_all(
            diffract_stacked, "lat", split_axis=2, concat_axis=1, tiled=True
        )
        piece = (lateral_block[0, :, 0, :], lateral_block[1, :, 0, :])
        lateral_spectrum = complex_einsum("kx,xn->kn", lat_forward, piece)
        lateral_spectrum = complex_times(lateral_spectrum, lateral_turn)
        lateral_result = complex_einsum("xk,kn->xn", lat_backward, lateral_spectrum)
        lateral_joined = (
            jnp.stack([lateral_result[0], lateral_result[1]])[:, :, None, :] / lateral_total
        )
        diffract_turned = lax.all_to_all(
            lateral_joined, "lat", split_axis=1, concat_axis=2, tiled=True
        )
        stacked = diffract_turned.reshape(2, height, span).reshape(2, time_count, slab, span)
        rows = lax.all_to_all(stacked, "tm", split_axis=1, concat_axis=3, tiled=True)[:, 0]
        rows_here = rows.shape[1]
        grid = (
            rows[0].reshape(rows_here, time_count, span),
            rows[1].reshape(rows_here, time_count, span),
        )
        spectrum = time_forward(grid, small_forward, twiddle_forward, long_forward)
        spectrum = complex_times(spectrum, spectral_turn)
        result = time_inverse(spectrum, small_back, twiddle_back, long_back, time_total)
        joined = jnp.stack(
            [result[0].reshape(rows_here, time_total), result[1].reshape(rows_here, time_total)]
        )[:, None]
        turned = lax.all_to_all(joined, "tm", split_axis=3, concat_axis=1, tiled=True)
        current = turned.reshape(2, height, span)
        amplify_rows_here = current.shape[1]
        length = current.shape[2]
        count = length // STRETCH
        amplify_grid = (
            current[0].reshape(amplify_rows_here, count, STRETCH),
            current[1].reshape(amplify_rows_here, count, STRETCH),
        )
        direct = complex_einsum("xji,xci->xcj", block_toeplitz, amplify_grid)
        projected = complex_einsum("xci,ig->cgx", amplify_grid, trailing)
        stretch_ends = (coupling[None] * projected[0], coupling[None] * projected[1])

        def chain_step(running, ends):
            moved = complex_times(stretch_step, running)
            return ((moved[0] + ends[0], moved[1] + ends[1]), running)

        zero_state = jnp.zeros((groups, amplify_rows_here), jnp.float32)
        running, chain = lax.scan(chain_step, (zero_state, zero_state), stretch_ends)

        def combine(earlier, later):
            joint = complex_times((earlier[0], earlier[1]), (later[0], later[1]))
            carried = complex_times(
                (later[0][:, None], later[1][:, None]), (earlier[2], earlier[3])
            )
            return (joint[0], joint[1], carried[0] + later[2], carried[1] + later[3])

        identity = (
            jnp.ones((groups,), jnp.float32),
            jnp.zeros((groups,), jnp.float32),
            jnp.zeros_like(running[0]),
            jnp.zeros_like(running[1]),
        )
        prefix = carried_in(
            (device_step[0], device_step[1], running[0], running[1]), "tm", combine, identity
        )
        starts = powers(
            decay_rate, detuning, (jnp.arange(count, dtype=jnp.float32) * STRETCH)[:, None]
        )
        before = complex_times(
            (starts[0][:, :, None], starts[1][:, :, None]), (prefix[2][None], prefix[3][None])
        )
        states = (before[0] + chain[0], before[1] + chain[1])
        delayed = complex_einsum("cgx,gj->xcj", states, leading)
        summed_re = (direct[0] + delayed[0]).reshape(amplify_rows_here, length)
        summed_im = (direct[1] + delayed[1]).reshape(amplify_rows_here, length)
        current = jnp.stack([current[0] - weight * summed_im, current[1] + weight * summed_re])
    return current


LATS, TIMES, SIDE, BIN_COUNT = 4, 8, 256, 32
TOTAL = LATS * TIMES
WIDE = LATS * SIDE
LONG = TIMES * SIDE
ROWS = SIDE // TIMES
PART = ROWS // 2
F32, BF16 = jnp.float32, jnp.bfloat16
MESH = pl.DeviceIdType.MESH


@functools.cache
def constants():
    j = np.arange(SIDE)
    w = np.exp(-2j * np.pi * (np.outer(j, j) % SIDE) / SIDE)
    big = np.block([[w.real, w.imag], [-w.imag, w.real]]).astype(np.float32)
    big_hi = big.astype(jnp.bfloat16)
    big_lo = (big - big_hi.astype(np.float32)).astype(jnp.bfloat16)
    tw8 = np.exp(-2j * np.pi * np.outer(np.arange(TIMES), j) / LONG)
    tau = np.exp(-1j * np.pi * np.arange(LONG).reshape(TIMES, SIDE) / LONG)
    tau2 = np.exp(-1j * np.pi * j / SIDE)[None]
    rows = np.concatenate([tw8, tau, tau2, np.zeros((7, SIDE))])
    rows = np.stack([rows.real, rows.imag]).astype(np.float32)
    tw4 = np.exp(-2j * np.pi * np.outer(j, np.arange(LATS)) / WIDE)
    cols = np.concatenate([tw4.real, tw4.imag], axis=1).astype(np.float32)
    return (big_hi, big_lo, rows, cols)


def halves(x):
    hi = x.astype(BF16)
    return hi, (x - hi.astype(F32)).astype(BF16)


def dot(a, b):
    return jnp.dot(a, b, preferred_element_type=F32)


def dot3(a, b):
    return dot(
        jnp.concatenate([a[0], a[1], a[0]], axis=1), jnp.concatenate([b[0], b[0], b[1]], axis=0)
    )


def cmul(a, b):
    return (a[0] * b[0] - a[1] * b[1], a[0] * b[1] + a[1] * b[0])


def conj(a):
    return (a[0], -a[1])


def small_fft(items, sign):
    count = len(items)
    if count == 1:
        return items
    even, odd = small_fft(items[0::2], sign), small_fft(items[1::2], sign)
    low, high = [], []
    for k in range(count // 2):
        re, im = odd[k]
        if 8 * k == count:
            r = math.sqrt(0.5)
            re, im = (re - sign * im) * r, (im + sign * re) * r
        elif 4 * k == count:
            re, im = -sign * im, sign * re
        elif 8 * k == 3 * count:
            r = math.sqrt(0.5)
            re, im = (-re - sign * im) * r, (-im + sign * re) * r
        low.append((even[k][0] + re, even[k][1] + im))
        high.append((even[k][0] - re, even[k][1] - im))
    return low + high


def lane_iota(shape):
    return lax.broadcasted_iota(jnp.int32, shape, len(shape) - 1)


def roll(x, shift):
    shift = shift % 128
    return pltpu.roll(x, shift, axis=x.ndim - 1) if shift else x


def pack(re, im):
    tiles = []
    first = lane_iota((re.shape[0], 128)) < 64
    for p in range(re.shape[1] // 128):
        a, b = re[:, 128 * p : 128 * p + 128], im[:, 128 * p : 128 * p + 128]
        tiles.append(jnp.where(first, a, roll(b, 64)))
        tiles.append(jnp.where(first, roll(a, 64), b))
    return tiles


def lane_part(shape):
    return lane_iota(shape) // 32


def pack_halves(re, im):
    part = lane_part((re[0].shape[0], 128))
    tiles = {}
    for l in range(LATS):
        for h in range(2):
            at = 2 * (l % 2) + h
            tile = None
            for q, source in enumerate((re[0], re[1], im[0], im[1])):
                piece = roll(source[:, 128 * (l // 2) : 128 * (l // 2) + 128], 32 * (q - at))
                tile = piece if tile is None else jnp.where(part == q, piece, tile)
            tiles[l, h] = tile
    return tiles


def unpack_halves(tiles):
    part = lane_part(tiles[0, 0].shape)
    done = []
    for q in range(4):
        joined = []
        for p in range(LATS // 2):
            value = None
            for at in range(4):
                piece = roll(tiles[2 * p + at // 2, at % 2], 32 * (at - q))
                value = piece if value is None else jnp.where(part == at, piece, value)
            joined.append(value)
        done.append(jnp.concatenate(joined, axis=1))
    return done[:2], done[2:]


def join_rows(a, b):
    count, width = a.shape
    a, b = (x.reshape(count // PART, PART, width) for x in (a, b))
    return jnp.stack([a, b], axis=1).reshape(2 * count, width)


def part_rows(x):
    x = x.reshape(x.shape[0] // ROWS, 2, PART, x.shape[1])
    return tuple(x[:, i].reshape(-1, x.shape[-1]) for i in (0, 1))


def turn(x):
    first = lane_iota(x.shape) < 64
    y = roll(x, 64)
    return jnp.where(first, -y, y)


def kernel(
    lf_hbm, latp, specp, occ_hbm, dec_ref, det_ref, gb_ref, wh_hbm, wl_hbm, rows_hbm, cols_hbm,
    out_hbm,
    out, s1, r1, s2, r2, s3a, r3a, s3b, r3b, s4a, r4a, s4b, r4b,
    tw_c, tw_s, th_c, th_s, ph_c, ph_s, ct, q_hi, q_lo, p_hi, p_lo, kev, kod, kfe, kfo, spec,
    lf, occ, wh, wl, rows_ref, cols_ref,
    ss1, rs1, ss2, rs2, ss3, rs3, ss4, rs4, load_sem, store_sem,
):
    loads = []
    for i, (src, dst) in enumerate((
        (lf_hbm, lf), (cols_hbm, cols_ref), (wh_hbm, wh), (wl_hbm, wl), (occ_hbm, occ),
        (rows_hbm, rows_ref),
    )):
        loads.append(pltpu.make_async_copy(src, dst, load_sem.at[i]))
        loads[-1].start()
    l, m = lax.axis_index("lat"), lax.axis_index("tm")
    weight = GAIN_SCALE / math.sqrt(occ.shape[0])

    half = TIMES // 2

    lats = [l] + [lax.rem(l + d, LATS) for d in range(1, LATS)]
    side = m // half
    sides = [lax.rem(side + 1, 2) * half, side * half]
    steps = [lax.rem(m + d, half) for d in range(half)]
    times = [[sides[i] + step for step in steps] for i in (0, 1)]
    others = []
    for d in range(TOTAL // 2):
        for i in (0, 1):
            if i == 0 or d:
                others.append((lats[d // half], times[i][d % half]))

    def each(act):
        for tl, tm in others:
            act(tl, tm)

    barrier = pltpu.get_barrier_semaphore()

    def greet(tl, tm):
        pl.semaphore_signal(barrier, inc=1, device_id=(tl, tm), device_id_type=MESH)

    each(greet)

    def remote(src, dst, send, recv, tl, tm):
        return pltpu.make_async_remote_copy(
            src_ref=src, dst_ref=dst, send_sem=send, recv_sem=recv,
            device_id=(tl, tm), device_id_type=MESH,
        )

    def lat_send(s, r, ss, rs, d):
        return remote(s.at[lats[d]], r.at[l], ss, rs, lats[d], m)

    def all_of(ref, count, ss, rs):
        part = ref.at[pl.ds(0, count)]
        return remote(part, part, ss, rs, lats[1], m)

    s3, r3 = (s3a, s3b), (r3a, r3b)

    def to_rows(h, tl, tm):
        src = s2.at[h, tl, pl.ds(pl.multiple_of(tm * PART, PART), PART)]
        return remote(src, r2.at[h, m * LATS + l], ss2.at[h], rs2.at[h], tl, tm)

    def to_columns(h, tl, tm):
        dst = r3[h].at[l * TIMES + m]
        return remote(s3[h].at[tm * LATS + tl], dst, ss3.at[h], rs3.at[h], tl, tm)

    def rows_all(h):
        return all_of(r2.at[h], TOTAL - 1, ss2.at[h], rs2.at[h])

    def columns_all(h):
        return all_of(r3[h], TOTAL - 1, ss3.at[h], rs3.at[h])

    loads[0].wait()
    for (t, h), tile in pack_halves(part_rows(lf[0]), part_rows(lf[1])).items():
        s1[h, t] = tile
    pl.semaphore_wait(barrier, TOTAL - 1)
    first = [
        [lat_send(s1.at[h], r1.at[h], ss1.at[h], rs1.at[h], d) for d in range(1, LATS)]
        for h in range(2)
    ]
    for copy in first[0]:
        copy.start()
    for h in range(2):
        r1[h, l] = s1[h, l]

    loads[1].wait()
    whole = (SIDE, 128)
    group = lax.rem(lane_iota(whole), 64) // 16
    sign = jnp.where(lane_iota(whole) < 64, -1.0, 1.0)
    phase = latp[...]
    turns = jnp.cos(phase) * (1.0 / WIDE), jnp.sin(phase) * (1.0 / WIDE)
    per_row = 128 // LATS
    chosen = lane_iota((per_row, 128))
    chosen = chosen - LATS * lax.broadcasted_iota(jnp.int32, (per_row, 128), 0)

    def spread_out(table, k):
        rows = []
        for i in range(WIDE // 128):
            one = jnp.where(chosen == k, table[i : i + 1], 0.0)
            rows.append(jnp.broadcast_to(jnp.sum(one, axis=1, keepdims=True), (per_row, 128)))
        return jnp.concatenate(rows, axis=0)

    second_set = lax.rem(lane_part((SIDE // 2, 128)), 2) == 1
    second_key = lax.rem(lane_part(whole), 2) == 1
    for k in range(LATS):
        tw_c[k] = jnp.broadcast_to(cols_ref[:, k : k + 1], whole)
        tw_s[k] = jnp.broadcast_to(cols_ref[:, LATS + k : LATS + k + 1], whole) * sign
        ph_c[k] = spread_out(turns[0], k)
        ph_s[k] = spread_out(turns[1], k) * sign
        for full, parted in ((tw_c, th_c), (tw_s, th_s)):
            one, two = part_rows(full[k])
            parted[k] = jnp.where(second_set, two, one)

    def wide_dft(re, im):
        x = halves(jnp.concatenate([re, im], axis=1))
        y = dot3(x, (wh[...], wl[...]))
        return y[:, :SIDE], y[:, SIDE:]

    def wide_inverse(re, im):
        return conj(wide_dft(re, -im))

    def row(k):
        return rows_ref[0, k : k + 1, :], rows_ref[1, k : k + 1, :]

    def stack(items):
        return tuple(jnp.concatenate([item[c] for item in items], axis=0) for c in (0, 1))

    def unstack(value):
        return [tuple(v[ROWS * k : ROWS * (k + 1)] for v in value) for k in range(TIMES)]

    def time_dft(items):
        items = small_fft(items, -1)
        return wide_dft(*stack([cmul(item, row(k)) for k, item in enumerate(items)]))

    def time_inverse_dft(value):
        items = unstack(wide_inverse(*value))
        return small_fft([cmul(item, conj(row(k))) for k, item in enumerate(items)], 1)

    def twist(items, back):
        rows = [row(TIMES + k) for k in range(TIMES)]
        return [cmul(x, conj(r) if back else r) for x, r in zip(items, rows)]

    def column_dft(x, low, high):
        w = [
            jnp.concatenate([ref[low:high, :SIDE], ref[SIDE + low : SIDE + high, :SIDE]], axis=0)
            for ref in (wh, wl)
        ]
        y = dot3(w, halves(x))
        count = high - low
        return [
            (y[:count, k : k + 128], y[count:, k : k + 128]) for k in range(0, x.shape[1], 128)
        ]

    def butterfly(x, tables, back):
        a, b, c, d = x[0] + x[2], x[0] - x[2], x[1] + x[3], turn(x[1] - x[3])
        if back:
            return [a + c, b + d, a - c, b - d]
        across, along = tables
        y = [a + c, b - d, a - c, b + d]
        return [y[0]] + [y[k] * across[k] + roll(y[k], 64) * along[k] for k in (1, 2, 3)]

    def lateral_spectrum(x, states):
        y = butterfly(x, (th_c, th_s), False)
        spectrum, turns = [], []
        for k in (0, 2):
            one = jnp.where(second_set, roll(y[k + 1], 32), y[k])
            two = jnp.where(second_set, y[k + 1], roll(y[k], -32))
            spectrum.append(join_rows(one, two))
            turns.append(tuple(jnp.where(second_key, t[k + 1], t[k]) for t in (ph_c, ph_s)))
        if states:
            y = butterfly(states, (tw_c, tw_s), False)
            tile, across, along = y[0], ph_c[0], ph_s[0]
            for k in range(1, LATS):
                tile = jnp.where(group == k, roll(y[k], 16 * k), tile)
                across = jnp.where(group == k, ph_c[k], across)
                along = jnp.where(group == k, ph_s[k], along)
            spectrum.append(tile)
            turns.append((across, along))
        spectrum = column_dft(jnp.concatenate(spectrum, axis=1), 0, SIDE)
        done = []
        for (top, bottom), (across, along) in zip(spectrum, turns):
            y = top - turn(bottom)
            done.append(y * across + roll(y, 64) * along)
        return jnp.concatenate(done, axis=1)

    def untwiddle(y, tables, low, high):
        across, along = tables
        for k in (1, 2, 3):
            y[k] = y[k] * across[k, low:high, :] - roll(y[k], 64) * along[k, low:high, :]
        return butterfly(y, None, True)

    def lateral_inverse(spectrum, low, high):
        result = [top + turn(bottom) for top, bottom in column_dft(spectrum, low, high)]
        mask = second_set[: (high - low) // 2]
        y = []
        for tile in result[:2]:
            one, two = part_rows(tile)
            y.append(jnp.where(mask, roll(two, 32), one))
            y.append(jnp.where(mask, two, roll(one, -32)))
        done = [untwiddle(y, (th_c, th_s), low // 2, high // 2)]
        if len(result) > 2:
            y = [roll(result[2], -16 * k) for k in range(LATS)]
            done.append(untwiddle(y, (tw_c, tw_s), low, high))
        return done

    loads[2].wait()
    loads[3].wait()
    def first_all(h):
        return all_of(r1.at[h], LATS - 1, ss1.at[h], rs1.at[h])

    first_all(0).wait_send()
    for copy in first[1]:
        copy.start()
    for h in range(2):
        first_all(h).wait_recv()
        spectrum = lateral_spectrum([r1[h, a] for a in range(LATS)], None)
        for a, tile in enumerate(lateral_inverse(spectrum, 0, SIDE)[0]):
            s2[h, a] = tile
        each(lambda tl, tm, h=h: to_rows(h, tl, tm).start())
        r2[h, m * LATS + l] = s2[h, l, pl.ds(pl.multiple_of(m * PART, PART), PART)]

    loads[4].wait()
    loads[5].wait()
    phase = specp[...].T
    spec[0] = jnp.cos(phase) * (1.0 / LONG)
    spec[1] = jnp.sin(phase) * (1.0 / LONG)

    dec_row, det_row = dec_ref[...], det_ref[...]
    square = (BIN_COUNT, BIN_COUNT)
    eye = lax.broadcasted_iota(jnp.int32, square, 0) == lax.broadcasted_iota(jnp.int32, square, 1)
    dec_col = jnp.sum(jnp.where(eye, dec_row, 0.0), axis=1, keepdims=True)
    det_col = jnp.sum(jnp.where(eye, det_row, 0.0), axis=1, keepdims=True)
    lag = lane_iota((BIN_COUNT, SIDE)).astype(F32)

    def power(exponent, rate, angle):
        size = jnp.exp(-rate * exponent)
        return size * jnp.cos(angle * exponent), -size * jnp.sin(angle * exponent)

    def bin_of(q):
        part = lax.rem(q, 64)
        within = lax.rem(part, 16)
        return jnp.where(within < 8, (part // 16) * 8 + within, -1)

    q_row = lax.broadcasted_iota(jnp.int32, (128, BIN_COUNT), 0)
    spread = (bin_of(q_row) == lane_iota((128, BIN_COUNT))).astype(BF16)
    q_lane = lane_iota((BIN_COUNT, 128))
    pick = bin_of(q_lane) == lax.broadcasted_iota(jnp.int32, (BIN_COUNT, 128), 0)
    dec_lane = jnp.sum(jnp.where(pick, dec_col, 0.0), axis=0, keepdims=True)
    det_lane = jnp.sum(jnp.where(pick, det_col, 0.0), axis=0, keepdims=True)
    ahead = power(lag, dec_col, det_col)
    is_re = lax.broadcasted_iota(jnp.int32, (128, SIDE), 0) < 64
    (re_hi, re_lo), (im_hi, im_lo) = halves(ahead[0]), halves(ahead[1])
    for ref, re, im in ((q_hi, re_hi, im_hi), (q_lo, re_lo, im_lo)):
        re, im = dot(spread, re), dot(spread, im)
        ref[:, :SIDE] = jnp.where(is_re, re, -im).astype(BF16)
        ref[:, SIDE:] = jnp.where(is_re, im, re).astype(BF16)
    lane = lane_iota((BIN_COUNT, SIDE))
    inner = lax.rem(lane, 16)
    held = jnp.where(inner < 8, (lane // 64) * 8 + inner, -1)
    held = held == lax.broadcasted_iota(jnp.int32, (BIN_COUNT, SIDE), 0)
    held_b = held.astype(BF16)
    step_dec = jnp.sum(jnp.where(held, dec_col, 0.0), axis=0, keepdims=True)
    step_det = jnp.sum(jnp.where(held, det_col, 0.0), axis=0, keepdims=True)
    behind = power(SIDE - lag, dec_col, det_col)
    for ref, which in ((p_hi, 0), (p_lo, 1)):
        re = halves(behind[0])[which].astype(F32).T.astype(BF16)
        im = halves(behind[1])[which].astype(F32).T.astype(BF16)
        re, im = dot(re, held_b), dot(im, held_b)
        ref[:SIDE, :SIDE] = re.astype(BF16)
        ref[:SIDE, SIDE:] = im.astype(BF16)
        ref[SIDE:, :SIDE] = (-im).astype(BF16)
        ref[SIDE:, SIDE:] = re.astype(BF16)
    y = 2.0 * dec_lane
    series = jnp.ones_like(y)
    for n in range(9, 1, -1):
        series = 1.0 - series * y * (1.0 / n)
    drive = jnp.sqrt(y * series)
    bins_here = bin_of(lax.broadcasted_iota(jnp.int32, (128, occ.shape[0]), 0))
    member = (bins_here == gb_ref[...]).astype(BF16)
    occ_hi, occ_lo = halves(occ[...])
    ct[...] = (dot(member, occ_hi) + dot(member, occ_lo)).T * drive

    first_half = lane_iota((1, 128)) < 64
    far = []
    for k in range(TIMES):
        far.append(jnp.where(first_half, *power(float(SIDE * k), dec_lane, det_lane)))
    mine = ct[pl.ds(pl.multiple_of(m * ROWS, ROWS), ROWS), :]
    q = (q_hi[...], q_lo[...])
    response = dot3(halves(jnp.concatenate([mine * f for f in far], axis=0)), q)
    response = unstack((response[:, :SIDE], response[:, SIDE:]))
    even = time_dft(response)
    kev[0] = LONG * (1.0 - (0.5 * weight) * even[1])
    kev[1] = (LONG * 0.5 * weight) * even[0]
    odd = time_dft(twist(response, False))
    kod[0] = (-0.5 * weight / LONG) * odd[1]
    kod[1] = (0.5 * weight / LONG) * odd[0]

    for h in range(2):
        rows_all(h).wait_recv()
    field = []
    for k in range(TIMES):
        re, im = unpack_halves({(a, h): r2[h, k * LATS + a] for a in range(LATS) for h in range(2)})
        field.append((jnp.concatenate(re, axis=0), jnp.concatenate(im, axis=0)))
    turn_row = stack([
        tuple(jnp.broadcast_to(spec[c, k : k + 1, :], (ROWS, SIDE)) for c in (0, 1))
        for k in range(TIMES)
    ])
    once = cmul(time_dft(field), turn_row)
    twisted = time_dft(twist(time_inverse_dft(once), False))
    twisted = time_inverse_dft(cmul(twisted, (kod[0], kod[1])))
    late = time_dft(twist(twisted, True))
    straight = cmul(once, (kev[0], kev[1]))
    once = cmul((straight[0] + late[0], straight[1] + late[1]), turn_row)
    field = time_inverse_dft(once)
    flat = stack(field)
    ends = dot3(halves(jnp.concatenate(flat, axis=1)), (p_hi[...], p_lo[...]))
    ends = unstack((ends[:, :SIDE], ends[:, SIDE:]))
    step = power(float(SIDE), step_dec, step_det)
    slot = lax.rem(lane_iota((8, SIDE)) // 16, 4)
    state = (jnp.zeros((ROWS, SIDE), F32), jnp.zeros((ROWS, SIDE), F32))
    for k in range(TIMES):
        folded = []
        for c in (0, 1):
            total = state[c][:8]
            for g in range(1, 4):
                total = jnp.where(slot == g, state[c][8 * g : 8 * g + 8], total)
            folded.append(total)
        for a, tile in enumerate(pack(*folded)):
            s3a[k * LATS + a, PART:, :] = tile
        moved = cmul(state, step)
        state = (moved[0] + ends[k][0], moved[1] + ends[k][1])
        re, im = ((v[:PART], v[PART:]) for v in field[k])
        for (a, h), tile in pack_halves(re, im).items():
            s3[h][k * LATS + a, :PART, :] = tile
    each(lambda tl, tm: to_columns(0, tl, tm).start())
    for h in range(2):
        r3[h][l * TIMES + m] = s3[h][m * LATS + l]

    t2 = rows_ref[0, 2 * TIMES : 2 * TIMES + 1, :], rows_ref[1, 2 * TIMES : 2 * TIMES + 1, :]
    q = (q_hi[...], q_lo[...])
    response = dot3(halves(jnp.where(lane_iota(whole) < 64, ct[...], 0.0)), q)
    response = (response[:, :SIDE], response[:, SIDE:])
    even, odd = wide_dft(*response), wide_dft(*cmul(response, t2))
    gain = 0.5 * weight / SIDE
    kfe[0], kfe[1] = -gain * even[1], gain * even[0]
    kfo[0], kfo[1] = -gain * odd[1], gain * odd[0]

    columns_all(0).wait_send()
    each(lambda tl, tm: to_columns(1, tl, tm).start())
    span = SIDE // 2
    fold = span // 8
    slot = lax.rem(lane_iota((fold, 128)), 64) // 8
    s4, r4 = (s4a, s4b), (r4a, r4b)

    def last_all(h, u):
        return all_of(r4[h].at[u], LATS - 1, ss4.at[h, u], rs4.at[h, u])

    for h in range(2):
        columns_all(h).wait_recv()
        tiles, states = [], []
        for a in range(LATS):
            mine = slice(a * TIMES, (a + 1) * TIMES)
            tiles.append(r3[h][mine, :PART, :].reshape(span, 128))
            if h == 0:
                extra = r3a[mine, PART:, :].reshape(8 * TIMES, 128)
                extra = [roll(extra, -16 * g).reshape(TIMES, 8, 128) for g in range(4)]
                states.append(jnp.stack(extra, axis=1).reshape(SIDE, 128))
        spectrum = lateral_spectrum(tiles, states)
        for u in range(2):
            done = lateral_inverse(spectrum, span * u, span * (u + 1))
            for a in range(LATS):
                s4[h][u, a, : span // 2, :] = done[0][a]
                if h == 0:
                    total = done[1][a][:fold]
                    for g in range(1, 8):
                        piece = roll(done[1][a][fold * g : fold * (g + 1)], 8 * g)
                        total = jnp.where(slot == g, piece, total)
                    s4a[u, a, span // 2 :, :] = total
            for d in range(1, LATS):
                sems = ss4.at[h, u], rs4.at[h, u]
                lat_send(s4[h].at[u], r4[h].at[u], *sems, d).start()
            r4[h][u, l] = s4[h][u, l]

    stores = []
    slot = lax.rem(lane_iota((fold, 128)), 64) // 16
    for u in range(2):
        for h in range(2):
            last_all(h, u).wait_recv()
        here = pl.ds(span * u, span)
        re, im = unpack_halves({
            (a, h): r4[h][u, a, : span // 2, :] for a in range(LATS) for h in range(2)
        })
        field = join_rows(*re), join_rows(*im)
        carried = []
        for g in range(8):
            total = jnp.zeros((fold, 128), F32)
            for a in range(LATS):
                piece = roll(r4a[u, a, span // 2 :, :], 16 * a - 8 * g)
                total = jnp.where(slot == a, piece, total)
            carried.append(total)
        carried = halves(jnp.concatenate(carried, axis=0) * ct[here, :])
        carried = dot3(carried, (q_hi[...], q_lo[...]))
        even = wide_inverse(*cmul(wide_dft(*field), (kfe[0, here, :], kfe[1, here, :])))
        odd = wide_dft(*cmul(field, t2))
        odd = wide_inverse(*cmul(odd, (kfo[0, here, :], kfo[1, here, :])))
        odd = cmul(odd, conj(t2))
        out[0, here, :] = field[0] + even[0] + odd[0] - weight * carried[:, SIDE:]
        out[1, here, :] = field[1] + even[1] + odd[1] + weight * carried[:, :SIDE]
        stores.append(
            pltpu.make_async_copy(out.at[:, here], out_hbm.at[:, here], store_sem.at[u])
        )
        stores[-1].start()

    first_all(1).wait_send()
    for h in range(2):
        rows_all(h).wait_send()
        for u in range(2):
            last_all(h, u).wait_send()
    columns_all(1).wait_send()
    for copy in stores:
        copy.wait()


def fused(light_field, lateral_phase, spectral_phase, occupation, bin_decay, bin_detune, group_bin):
    tile = (SIDE, 128)
    vmem, sems = pltpu.VMEM, pltpu.SemaphoreType.DMA
    exchange = [
        vmem(light_field.shape, F32),
        vmem((2, LATS, SIDE // 2, 128), F32), vmem((2, LATS, SIDE // 2, 128), F32),
        vmem((2, LATS, SIDE // 2, 128), F32), vmem((2, TOTAL, PART, 128), F32),
        vmem((TOTAL, PART + 8, 128), F32), vmem((TOTAL, PART + 8, 128), F32),
        vmem((TOTAL, PART, 128), F32), vmem((TOTAL, PART, 128), F32),
        vmem((2, LATS, 5 * SIDE // 16, 128), F32), vmem((2, LATS, 5 * SIDE // 16, 128), F32),
        vmem((2, LATS, SIDE // 4, 128), F32), vmem((2, LATS, SIDE // 4, 128), F32),
    ]
    tables = [vmem((LATS,) + tile, F32)] * 2 + [vmem((LATS, SIDE // 2, 128), F32)] * 2
    tables += [vmem((LATS,) + tile, F32)] * 2 + [vmem(tile, F32)]
    tables += [vmem((128, 2 * SIDE), BF16)] * 2 + [vmem((2 * SIDE, 2 * SIDE), BF16)] * 2
    tables += [vmem((2, SIDE, SIDE), F32)] * 4
    tables += [vmem((2, TIMES, SIDE), F32)]
    fixed = constants()
    tables += [vmem(light_field.shape, F32), vmem(occupation.shape, F32)]
    tables += [vmem(c.shape, c.dtype) for c in fixed]
    semaphores = [sems((2,))] * 6 + [sems((2, 2))] * 2
    semaphores += [sems((2 + len(fixed),)), sems((2,))]
    in_vmem, anywhere = pl.BlockSpec(memory_space=pltpu.VMEM), pl.BlockSpec(memory_space=pl.ANY)
    return pl.pallas_call(
        kernel,
        out_shape=jax.ShapeDtypeStruct(light_field.shape, F32),
        in_specs=[anywhere] + [in_vmem] * 2 + [anywhere] + [in_vmem] * 3 + [anywhere] * len(fixed),
        out_specs=anywhere,
        scratch_shapes=exchange + tables + semaphores,
        compiler_params=pltpu.CompilerParams(
            collective_id=0, has_side_effects=True, vmem_limit_bytes=56 * 1024 * 1024
        ),
    )(
        light_field,
        lateral_phase.reshape(WIDE // 128, 128),
        spectral_phase.reshape(SIDE, TIMES),
        occupation,
        bin_decay[None],
        bin_detune[None],
        group_bin[None],
        *[jnp.asarray(c) for c in fixed],
    )


def solution(mesh):
    def local(light_field, *rest):
        fits = (lax.axis_size("lat"), lax.axis_size("tm")) == (LATS, TIMES)
        fits = fits and light_field.shape == (2, SIDE, SIDE)
        fits = fits and rest[2].shape == (128, SIDE) and rest[3].shape == (BIN_COUNT,)
        return (fused if fits else on_device)(light_field, *rest)

    return jax.shard_map(
        local,
        mesh=mesh,
        in_specs=(P(None, "lat", "tm"), P(), P(), P(None, "lat"), P(), P(), P()),
        out_specs=P(None, "lat", "tm"),
        check_vma=False,
    )
```

```python
import functools
import math

import jax
import jax.numpy as jnp
import numpy as np
from jax import lax
from jax.experimental import pallas as pl
from jax.experimental.pallas import tpu as pltpu
from jax.sharding import PartitionSpec as P

STRETCH = 128
STEPS = 2


GAIN_SCALE = 0.5


def carried_in(value, axis, join, neutral):
    count, mine = (lax.axis_size(axis), lax.axis_index(axis))
    pieces = jax.tree.map(lambda part: lax.all_gather(part, axis), value)
    so_far = jax.tree.map(
        lambda part, zero: jnp.full_like(part, 0) + jnp.asarray(zero, part.dtype), value, neutral
    )

    def lap(position, so_far):
        longer = join(so_far, jax.tree.map(lambda part: part[position], pieces))
        return jax.tree.map(lambda new, old: jnp.where(position < mine, new, old), longer, so_far)

    return lax.fori_loop(0, count - 1, lap, so_far)


def complex_einsum(form, left, right):
    exact = lax.Precision.HIGHEST
    real_part = jnp.einsum(form, left[0], right[0], precision=exact) - jnp.einsum(
        form, left[1], right[1], precision=exact
    )
    imag_part = jnp.einsum(form, left[0], right[1], precision=exact) + jnp.einsum(
        form, left[1], right[0], precision=exact
    )
    return (real_part, imag_part)


def complex_times(left, right):
    return (left[0] * right[0] - left[1] * right[1], left[0] * right[1] + left[1] * right[0])


def angle_table(height, breadth, modulus, sign):
    first = jnp.arange(height, dtype=jnp.int32)[:, None]
    second = jnp.arange(breadth, dtype=jnp.int32)[None, :]
    turns = (first * second % modulus).astype(jnp.float32) * (2.0 * math.pi / modulus)
    return (jnp.cos(turns), sign * jnp.sin(turns))


def time_forward(grid, small_table, twiddle, long_table):
    mixed = complex_einsum("ka,rab->rkb", small_table, grid)
    mixed = complex_times(mixed, twiddle)
    return complex_einsum("rkb,bq->rkq", mixed, long_table)


def time_inverse(spectrum, small_table, twiddle, long_table, length):
    mixed = complex_einsum("rkq,qb->rkb", spectrum, long_table)
    mixed = complex_times(mixed, twiddle)
    result = complex_einsum("ak,rkb->rab", small_table, mixed)
    return (result[0] / length, result[1] / length)


def powers(decay_rate, detuning, exponent):
    magnitude = jnp.exp(-decay_rate * exponent)
    phase_angle = detuning * exponent
    return (magnitude * jnp.cos(phase_angle), -magnitude * jnp.sin(phase_angle))


def on_device(
    light_field, lateral_phase, spectral_phase, occupation, bin_decay, bin_detune, group_bin
):
    lat_count = lax.axis_size("lat")
    time_count = lax.axis_size("tm")
    height = light_field.shape[1]
    span = light_field.shape[2]
    lateral_total = height * lat_count
    time_total = span * time_count
    groups = occupation.shape[0]
    slab = height // time_count
    narrow = span // lat_count
    exact = lax.Precision.HIGHEST
    lat_forward = angle_table(lateral_total, lateral_total, lateral_total, -1.0)
    lat_backward = angle_table(lateral_total, lateral_total, lateral_total, 1.0)
    lateral_turn = (jnp.cos(lateral_phase)[:, None], jnp.sin(lateral_phase)[:, None])
    small_back = angle_table(time_count, time_count, time_count, 1.0)
    twiddle_back = angle_table(time_count, span, time_total, 1.0)
    long_back = angle_table(span, span, span, 1.0)
    spectral_grid = spectral_phase.reshape(span, time_count).T
    spectral_turn = (jnp.cos(spectral_grid), jnp.sin(spectral_grid))
    bins = jnp.arange(bin_decay.shape[0], dtype=jnp.int32)
    onehot = (group_bin[:, None] == bins[None, :]).astype(jnp.float32)
    decay_rate = jnp.dot(onehot, bin_decay, precision=exact)
    detuning = jnp.dot(onehot, bin_detune, precision=exact)
    coupling = jnp.sqrt(-jnp.expm1(-2.0 * decay_rate))[:, None] * occupation
    lags = jnp.arange(STRETCH + 1, dtype=jnp.float32)[:, None]
    lag_powers = powers(decay_rate, detuning, lags)
    lag_grid = (
        jnp.arange(STRETCH, dtype=jnp.int32)[:, None]
        - jnp.arange(STRETCH, dtype=jnp.int32)[None, :]
    )
    inside = (lag_grid >= 0)[None]
    clipped = jnp.maximum(lag_grid, 0)
    leading = (lag_powers[0][1:].T, lag_powers[1][1:].T)
    trailing = (lag_powers[0][:STRETCH][::-1], lag_powers[1][:STRETCH][::-1])
    stretch_step = (lag_powers[0][STRETCH][:, None], lag_powers[1][STRETCH][:, None])
    device_step = powers(decay_rate, detuning, jnp.float32(span))
    weight = GAIN_SCALE / math.sqrt(groups)
    small_forward = angle_table(time_count, time_count, time_count, -1.0)
    twiddle_forward = angle_table(time_count, span, time_total, -1.0)
    long_forward = angle_table(span, span, span, -1.0)
    current = light_field
    block_toeplitz = (
        jnp.where(
            inside,
            jnp.take(
                jnp.dot(coupling.T, lag_powers[0][:STRETCH].T, precision=exact), clipped, axis=1
            ),
            0.0,
        ),
        jnp.where(
            inside,
            jnp.take(
                jnp.dot(coupling.T, lag_powers[1][:STRETCH].T, precision=exact), clipped, axis=1
            ),
            0.0,
        ),
    )
    for repeat in range(STEPS):
        diffract_stacked = current.reshape(2, height, lat_count, narrow)
        lateral_block = lax.all_to_all(
            diffract_stacked, "lat", split_axis=2, concat_axis=1, tiled=True
        )
        piece = (lateral_block[0, :, 0, :], lateral_block[1, :, 0, :])
        lateral_spectrum = complex_einsum("kx,xn->kn", lat_forward, piece)
        lateral_spectrum = complex_times(lateral_spectrum, lateral_turn)
        lateral_result = complex_einsum("xk,kn->xn", lat_backward, lateral_spectrum)
        lateral_joined = (
            jnp.stack([lateral_result[0], lateral_result[1]])[:, :, None, :] / lateral_total
        )
        diffract_turned = lax.all_to_all(
            lateral_joined, "lat", split_axis=1, concat_axis=2, tiled=True
        )
        stacked = diffract_turned.reshape(2, height, span).reshape(2, time_count, slab, span)
        rows = lax.all_to_all(stacked, "tm", split_axis=1, concat_axis=3, tiled=True)[:, 0]
        rows_here = rows.shape[1]
        grid = (
            rows[0].reshape(rows_here, time_count, span),
            rows[1].reshape(rows_here, time_count, span),
        )
        spectrum = time_forward(grid, small_forward, twiddle_forward, long_forward)
        spectrum = complex_times(spectrum, spectral_turn)
        result = time_inverse(spectrum, small_back, twiddle_back, long_back, time_total)
        joined = jnp.stack(
            [result[0].reshape(rows_here, time_total), result[1].reshape(rows_here, time_total)]
        )[:, None]
        turned = lax.all_to_all(joined, "tm", split_axis=3, concat_axis=1, tiled=True)
        current = turned.reshape(2, height, span)
        amplify_rows_here = current.shape[1]
        length = current.shape[2]
        count = length // STRETCH
        amplify_grid = (
            current[0].reshape(amplify_rows_here, count, STRETCH),
            current[1].reshape(amplify_rows_here, count, STRETCH),
        )
        direct = complex_einsum("xji,xci->xcj", block_toeplitz, amplify_grid)
        projected = complex_einsum("xci,ig->cgx", amplify_grid, trailing)
        stretch_ends = (coupling[None] * projected[0], coupling[None] * projected[1])

        def chain_step(running, ends):
            moved = complex_times(stretch_step, running)
            return ((moved[0] + ends[0], moved[1] + ends[1]), running)

        zero_state = jnp.zeros((groups, amplify_rows_here), jnp.float32)
        running, chain = lax.scan(chain_step, (zero_state, zero_state), stretch_ends)

        def combine(earlier, later):
            joint = complex_times((earlier[0], earlier[1]), (later[0], later[1]))
            carried = complex_times(
                (later[0][:, None], later[1][:, None]), (earlier[2], earlier[3])
            )
            return (joint[0], joint[1], carried[0] + later[2], carried[1] + later[3])

        identity = (
            jnp.ones((groups,), jnp.float32),
            jnp.zeros((groups,), jnp.float32),
            jnp.zeros_like(running[0]),
            jnp.zeros_like(running[1]),
        )
        prefix = carried_in(
            (device_step[0], device_step[1], running[0], running[1]), "tm", combine, identity
        )
        starts = powers(
            decay_rate, detuning, (jnp.arange(count, dtype=jnp.float32) * STRETCH)[:, None]
        )
        before = complex_times(
            (starts[0][:, :, None], starts[1][:, :, None]), (prefix[2][None], prefix[3][None])
        )
        states = (before[0] + chain[0], before[1] + chain[1])
        delayed = complex_einsum("cgx,gj->xcj", states, leading)
        summed_re = (direct[0] + delayed[0]).reshape(amplify_rows_here, length)
        summed_im = (direct[1] + delayed[1]).reshape(amplify_rows_here, length)
        current = jnp.stack([current[0] - weight * summed_im, current[1] + weight * summed_re])
    return current


LATS, TIMES, SIDE, BIN_COUNT = 4, 8, 256, 32
TOTAL = LATS * TIMES
WIDE = LATS * SIDE
LONG = TIMES * SIDE
ROWS = SIDE // TIMES
PART = ROWS // 2
F32, BF16 = jnp.float32, jnp.bfloat16
MESH = pl.DeviceIdType.MESH


@functools.cache
def constants():
    j = np.arange(SIDE)
    w = np.exp(-2j * np.pi * (np.outer(j, j) % SIDE) / SIDE)
    big = np.block([[w.real, w.imag], [-w.imag, w.real]]).astype(np.float32)
    big_hi = big.astype(jnp.bfloat16)
    big_lo = (big - big_hi.astype(np.float32)).astype(jnp.bfloat16)
    tw8 = np.exp(-2j * np.pi * np.outer(np.arange(TIMES), j) / LONG)
    tau = np.exp(-1j * np.pi * np.arange(LONG).reshape(TIMES, SIDE) / LONG)
    tau2 = np.exp(-1j * np.pi * j / SIDE)[None]
    rows = np.concatenate([tw8, tau, tau2, np.zeros((7, SIDE))])
    rows = np.stack([rows.real, rows.imag]).astype(np.float32)
    tw4 = np.exp(-2j * np.pi * np.outer(j, np.arange(LATS)) / WIDE)
    cols = np.concatenate([tw4.real, tw4.imag], axis=1).astype(np.float32)
    return (big_hi, big_lo, rows, cols)


def halves(x):
    hi = x.astype(BF16)
    return hi, (x - hi.astype(F32)).astype(BF16)


def dot(a, b):
    return jnp.dot(a, b, preferred_element_type=F32)


def dot3(a, b):
    return dot(
        jnp.concatenate([a[0], a[1], a[0]], axis=1), jnp.concatenate([b[0], b[0], b[1]], axis=0)
    )


def cmul(a, b):
    return (a[0] * b[0] - a[1] * b[1], a[0] * b[1] + a[1] * b[0])


def conj(a):
    return (a[0], -a[1])


def small_fft(items, sign):
    count = len(items)
    if count == 1:
        return items
    even, odd = small_fft(items[0::2], sign), small_fft(items[1::2], sign)
    low, high = [], []
    for k in range(count // 2):
        re, im = odd[k]
        if 8 * k == count:
            r = math.sqrt(0.5)
            re, im = (re - sign * im) * r, (im + sign * re) * r
        elif 4 * k == count:
            re, im = -sign * im, sign * re
        elif 8 * k == 3 * count:
            r = math.sqrt(0.5)
            re, im = (-re - sign * im) * r, (-im + sign * re) * r
        low.append((even[k][0] + re, even[k][1] + im))
        high.append((even[k][0] - re, even[k][1] - im))
    return low + high


def lane_iota(shape):
    return lax.broadcasted_iota(jnp.int32, shape, len(shape) - 1)


def roll(x, shift):
    shift = shift % 128
    return pltpu.roll(x, shift, axis=x.ndim - 1) if shift else x


def pack(re, im):
    tiles = []
    first = lane_iota((re.shape[0], 128)) < 64
    for p in range(re.shape[1] // 128):
        a, b = re[:, 128 * p : 128 * p + 128], im[:, 128 * p : 128 * p + 128]
        tiles.append(jnp.where(first, a, roll(b, 64)))
        tiles.append(jnp.where(first, roll(a, 64), b))
    return tiles


def lane_part(shape):
    return lane_iota(shape) // 32


def pack_halves(re, im):
    part = lane_part((re[0].shape[0], 128))
    tiles = {}
    for l in range(LATS):
        for h in range(2):
            at = 2 * (l % 2) + h
            tile = None
            for q, source in enumerate((re[0], re[1], im[0], im[1])):
                piece = roll(source[:, 128 * (l // 2) : 128 * (l // 2) + 128], 32 * (q - at))
                tile = piece if tile is None else jnp.where(part == q, piece, tile)
            tiles[l, h] = tile
    return tiles


def unpack_halves(tiles):
    part = lane_part(tiles[0, 0].shape)
    done = []
    for q in range(4):
        joined = []
        for p in range(LATS // 2):
            value = None
            for at in range(4):
                piece = roll(tiles[2 * p + at // 2, at % 2], 32 * (at - q))
                value = piece if value is None else jnp.where(part == at, piece, value)
            joined.append(value)
        done.append(jnp.concatenate(joined, axis=1))
    return done[:2], done[2:]


def join_rows(a, b):
    count, width = a.shape
    a, b = (x.reshape(count // PART, PART, width) for x in (a, b))
    return jnp.stack([a, b], axis=1).reshape(2 * count, width)


def part_rows(x):
    x = x.reshape(x.shape[0] // ROWS, 2, PART, x.shape[1])
    return tuple(x[:, i].reshape(-1, x.shape[-1]) for i in (0, 1))


def turn(x):
    first = lane_iota(x.shape) < 64
    y = roll(x, 64)
    return jnp.where(first, -y, y)


def kernel(
    lf_hbm, latp, specp, occ_hbm, dec_ref, det_ref, gb_ref, wh_hbm, wl_hbm, rows_hbm, cols_hbm,
    out_hbm,
    out, s1, r1, s2, r2, s3a, r3a, s3b, r3b, s3c, r3c, s3d, r3d, s4a, r4a, s4b, r4b,
    tw_c, tw_s, th_c, th_s, ph_c, ph_s, ct, q_hi, q_lo, p_hi, p_lo, kev, kod, kfe, kfo, spec,
    lf, occ, wh, wl, rows_ref, cols_ref,
    ss1, rs1, ss2, rs2, ss3, rs3, ss4, rs4, load_sem, store_sem,
):
    loads = []
    for i, (src, dst) in enumerate((
        (lf_hbm, lf), (cols_hbm, cols_ref), (wh_hbm, wh), (wl_hbm, wl), (occ_hbm, occ),
        (rows_hbm, rows_ref),
    )):
        loads.append(pltpu.make_async_copy(src, dst, load_sem.at[i]))
        loads[-1].start()
    l, m = lax.axis_index("lat"), lax.axis_index("tm")
    weight = GAIN_SCALE / math.sqrt(occ.shape[0])

    half = TIMES // 2

    lats = [l] + [lax.rem(l + d, LATS) for d in range(1, LATS)]
    side = m // half
    sides = [lax.rem(side + 1, 2) * half, side * half]
    steps = [lax.rem(m + d, half) for d in range(half)]
    times = [[sides[i] + step for step in steps] for i in (0, 1)]
    others = []
    for d in range(TOTAL // 2):
        for i in (0, 1):
            if i == 0 or d:
                others.append((lats[d // half], times[i][d % half]))

    def each(act):
        for tl, tm in others:
            act(tl, tm)

    barrier = pltpu.get_barrier_semaphore()

    def greet(tl, tm):
        pl.semaphore_signal(barrier, inc=1, device_id=(tl, tm), device_id_type=MESH)

    each(greet)

    def remote(src, dst, send, recv, tl, tm):
        return pltpu.make_async_remote_copy(
            src_ref=src, dst_ref=dst, send_sem=send, recv_sem=recv,
            device_id=(tl, tm), device_id_type=MESH,
        )

    def lat_send(s, r, ss, rs, d):
        return remote(s.at[lats[d]], r.at[l], ss, rs, lats[d], m)

    def all_of(ref, count, ss, rs):
        part = ref.at[pl.ds(0, count)]
        return remote(part, part, ss, rs, lats[1], m)

    s3, r3 = ((s3a, s3b), (s3c, s3d)), ((r3a, r3b), (r3c, r3d))

    def to_rows(h, tl, tm):
        src = s2.at[h, tl, pl.ds(pl.multiple_of(tm * PART, PART), PART)]
        return remote(src, r2.at[h, m * LATS + l], ss2.at[h], rs2.at[h], tl, tm)

    def to_columns(v, h, tl, tm):
        dst = r3[v][h].at[l * TIMES + m]
        return remote(s3[v][h].at[tm * LATS + tl], dst, ss3.at[v, h], rs3.at[v, h], tl, tm)

    def rows_all(h):
        return all_of(r2.at[h], TOTAL - 1, ss2.at[h], rs2.at[h])

    def columns_all(v, h):
        return all_of(r3[v][h], TOTAL - 1, ss3.at[v, h], rs3.at[v, h])

    loads[0].wait()
    for (t, h), tile in pack_halves(part_rows(lf[0]), part_rows(lf[1])).items():
        s1[h, t] = tile
    pl.semaphore_wait(barrier, TOTAL - 1)
    first = [
        [lat_send(s1.at[h], r1.at[h], ss1.at[h], rs1.at[h], d) for d in range(1, LATS)]
        for h in range(2)
    ]
    for copy in first[0]:
        copy.start()
    for h in range(2):
        r1[h, l] = s1[h, l]

    loads[1].wait()
    whole = (SIDE, 128)
    group = lax.rem(lane_iota(whole), 64) // 16
    sign = jnp.where(lane_iota(whole) < 64, -1.0, 1.0)
    phase = latp[...]
    turns = jnp.cos(phase) * (1.0 / WIDE), jnp.sin(phase) * (1.0 / WIDE)
    per_row = 128 // LATS
    chosen = lane_iota((per_row, 128))
    chosen = chosen - LATS * lax.broadcasted_iota(jnp.int32, (per_row, 128), 0)

    def spread_out(table, k):
        rows = []
        for i in range(WIDE // 128):
            one = jnp.where(chosen == k, table[i : i + 1], 0.0)
            rows.append(jnp.broadcast_to(jnp.sum(one, axis=1, keepdims=True), (per_row, 128)))
        return jnp.concatenate(rows, axis=0)

    second_set = lax.rem(lane_part((SIDE // 2, 128)), 2) == 1
    second_key = lax.rem(lane_part(whole), 2) == 1
    for k in range(LATS):
        tw_c[k] = jnp.broadcast_to(cols_ref[:, k : k + 1], whole)
        tw_s[k] = jnp.broadcast_to(cols_ref[:, LATS + k : LATS + k + 1], whole) * sign
        ph_c[k] = spread_out(turns[0], k)
        ph_s[k] = spread_out(turns[1], k) * sign
        for full, parted in ((tw_c, th_c), (tw_s, th_s)):
            one, two = part_rows(full[k])
            parted[k] = jnp.where(second_set, two, one)

    def wide_dft(re, im):
        x = halves(jnp.concatenate([re, im], axis=1))
        y = dot3(x, (wh[...], wl[...]))
        return y[:, :SIDE], y[:, SIDE:]

    def wide_inverse(re, im):
        return conj(wide_dft(re, -im))

    def row(k):
        return rows_ref[0, k : k + 1, :], rows_ref[1, k : k + 1, :]

    def stack(items):
        return tuple(jnp.concatenate([item[c] for item in items], axis=0) for c in (0, 1))

    def unstack(value):
        size = value[0].shape[0] // TIMES
        return [tuple(v[size * k : size * (k + 1)] for v in value) for k in range(TIMES)]

    def time_dft(items):
        items = small_fft(items, -1)
        return wide_dft(*stack([cmul(item, row(k)) for k, item in enumerate(items)]))

    def time_inverse_dft(value):
        items = unstack(wide_inverse(*value))
        return small_fft([cmul(item, conj(row(k))) for k, item in enumerate(items)], 1)

    def twist(items, back):
        rows = [row(TIMES + k) for k in range(TIMES)]
        return [cmul(x, conj(r) if back else r) for x, r in zip(items, rows)]

    def column_dft(x, low, high):
        w = [
            jnp.concatenate([ref[low:high, :SIDE], ref[SIDE + low : SIDE + high, :SIDE]], axis=0)
            for ref in (wh, wl)
        ]
        y = dot3(w, halves(x))
        count = high - low
        return [
            (y[:count, k : k + 128], y[count:, k : k + 128]) for k in range(0, x.shape[1], 128)
        ]

    def butterfly(x, tables, back):
        a, b, c, d = x[0] + x[2], x[0] - x[2], x[1] + x[3], turn(x[1] - x[3])
        if back:
            return [a + c, b + d, a - c, b - d]
        across, along = tables
        y = [a + c, b - d, a - c, b + d]
        return [y[0]] + [y[k] * across[k] + roll(y[k], 64) * along[k] for k in (1, 2, 3)]

    def lateral_spectrum(x, states):
        y = butterfly(x, (th_c, th_s), False)
        spectrum, turns = [], []
        for k in (0, 2):
            one = jnp.where(second_set, roll(y[k + 1], 32), y[k])
            two = jnp.where(second_set, y[k + 1], roll(y[k], -32))
            spectrum.append(join_rows(one, two))
            turns.append(tuple(jnp.where(second_key, t[k + 1], t[k]) for t in (ph_c, ph_s)))
        if states:
            y = butterfly(states, (tw_c, tw_s), False)
            tile, across, along = y[0], ph_c[0], ph_s[0]
            for k in range(1, LATS):
                tile = jnp.where(group == k, roll(y[k], 16 * k), tile)
                across = jnp.where(group == k, ph_c[k], across)
                along = jnp.where(group == k, ph_s[k], along)
            spectrum.append(tile)
            turns.append((across, along))
        spectrum = column_dft(jnp.concatenate(spectrum, axis=1), 0, SIDE)
        done = []
        for (top, bottom), (across, along) in zip(spectrum, turns):
            y = top - turn(bottom)
            done.append(y * across + roll(y, 64) * along)
        return jnp.concatenate(done, axis=1)

    def untwiddle(y, tables, low, high):
        across, along = tables
        for k in (1, 2, 3):
            y[k] = y[k] * across[k, low:high, :] - roll(y[k], 64) * along[k, low:high, :]
        return butterfly(y, None, True)

    def lateral_inverse(spectrum, low, high):
        result = [top + turn(bottom) for top, bottom in column_dft(spectrum, low, high)]
        mask = second_set[: (high - low) // 2]
        y = []
        for tile in result[:2]:
            one, two = part_rows(tile)
            y.append(jnp.where(mask, roll(two, 32), one))
            y.append(jnp.where(mask, two, roll(one, -32)))
        done = [untwiddle(y, (th_c, th_s), low // 2, high // 2)]
        if len(result) > 2:
            y = [roll(result[2], -16 * k) for k in range(LATS)]
            done.append(untwiddle(y, (tw_c, tw_s), low, high))
        return done

    loads[2].wait()
    loads[3].wait()
    def first_all(h):
        return all_of(r1.at[h], LATS - 1, ss1.at[h], rs1.at[h])

    first_all(0).wait_send()
    for copy in first[1]:
        copy.start()
    for h in range(2):
        first_all(h).wait_recv()
        spectrum = lateral_spectrum([r1[h, a] for a in range(LATS)], None)
        for a, tile in enumerate(lateral_inverse(spectrum, 0, SIDE)[0]):
            s2[h, a] = tile
        each(lambda tl, tm, h=h: to_rows(h, tl, tm).start())
        r2[h, m * LATS + l] = s2[h, l, pl.ds(pl.multiple_of(m * PART, PART), PART)]

    loads[4].wait()
    loads[5].wait()
    phase = specp[...].T
    spec[0] = jnp.cos(phase) * (1.0 / LONG)
    spec[1] = jnp.sin(phase) * (1.0 / LONG)

    dec_row, det_row = dec_ref[...], det_ref[...]
    square = (BIN_COUNT, BIN_COUNT)
    eye = lax.broadcasted_iota(jnp.int32, square, 0) == lax.broadcasted_iota(jnp.int32, square, 1)
    dec_col = jnp.sum(jnp.where(eye, dec_row, 0.0), axis=1, keepdims=True)
    det_col = jnp.sum(jnp.where(eye, det_row, 0.0), axis=1, keepdims=True)
    lag = lane_iota((BIN_COUNT, SIDE)).astype(F32)

    def power(exponent, rate, angle):
        size = jnp.exp(-rate * exponent)
        return size * jnp.cos(angle * exponent), -size * jnp.sin(angle * exponent)

    def bin_of(q):
        part = lax.rem(q, 64)
        within = lax.rem(part, 16)
        return jnp.where(within < 8, (part // 16) * 8 + within, -1)

    q_row = lax.broadcasted_iota(jnp.int32, (128, BIN_COUNT), 0)
    spread = (bin_of(q_row) == lane_iota((128, BIN_COUNT))).astype(BF16)
    q_lane = lane_iota((BIN_COUNT, 128))
    pick = bin_of(q_lane) == lax.broadcasted_iota(jnp.int32, (BIN_COUNT, 128), 0)
    dec_lane = jnp.sum(jnp.where(pick, dec_col, 0.0), axis=0, keepdims=True)
    det_lane = jnp.sum(jnp.where(pick, det_col, 0.0), axis=0, keepdims=True)
    ahead = power(lag, dec_col, det_col)
    is_re = lax.broadcasted_iota(jnp.int32, (128, SIDE), 0) < 64
    (re_hi, re_lo), (im_hi, im_lo) = halves(ahead[0]), halves(ahead[1])
    for ref, re, im in ((q_hi, re_hi, im_hi), (q_lo, re_lo, im_lo)):
        re, im = dot(spread, re), dot(spread, im)
        ref[:, :SIDE] = jnp.where(is_re, re, -im).astype(BF16)
        ref[:, SIDE:] = jnp.where(is_re, im, re).astype(BF16)
    lane = lane_iota((BIN_COUNT, SIDE))
    inner = lax.rem(lane, 16)
    held = jnp.where(inner < 8, (lane // 64) * 8 + inner, -1)
    held = held == lax.broadcasted_iota(jnp.int32, (BIN_COUNT, SIDE), 0)
    held_b = held.astype(BF16)
    step_dec = jnp.sum(jnp.where(held, dec_col, 0.0), axis=0, keepdims=True)
    step_det = jnp.sum(jnp.where(held, det_col, 0.0), axis=0, keepdims=True)
    behind = power(SIDE - lag, dec_col, det_col)
    for ref, which in ((p_hi, 0), (p_lo, 1)):
        re = halves(behind[0])[which].astype(F32).T.astype(BF16)
        im = halves(behind[1])[which].astype(F32).T.astype(BF16)
        re, im = dot(re, held_b), dot(im, held_b)
        ref[:SIDE, :SIDE] = re.astype(BF16)
        ref[:SIDE, SIDE:] = im.astype(BF16)
        ref[SIDE:, :SIDE] = (-im).astype(BF16)
        ref[SIDE:, SIDE:] = re.astype(BF16)
    y = 2.0 * dec_lane
    series = jnp.ones_like(y)
    for n in range(9, 1, -1):
        series = 1.0 - series * y * (1.0 / n)
    drive = jnp.sqrt(y * series)
    bins_here = bin_of(lax.broadcasted_iota(jnp.int32, (128, occ.shape[0]), 0))
    member = (bins_here == gb_ref[...]).astype(BF16)
    occ_hi, occ_lo = halves(occ[...])
    ct[...] = (dot(member, occ_hi) + dot(member, occ_lo)).T * drive

    first_half = lane_iota((1, 128)) < 64
    far = []
    for k in range(TIMES):
        far.append(jnp.where(first_half, *power(float(SIDE * k), dec_lane, det_lane)))
    mine = ct[pl.ds(pl.multiple_of(m * ROWS, ROWS), ROWS), :]
    q = (q_hi[...], q_lo[...])
    response = dot3(halves(jnp.concatenate([mine * f for f in far], axis=0)), q)
    response = unstack((response[:, :SIDE], response[:, SIDE:]))
    even = time_dft(response)
    kev[0] = LONG * (1.0 - (0.5 * weight) * even[1])
    kev[1] = (LONG * 0.5 * weight) * even[0]
    odd = time_dft(twist(response, False))
    kod[0] = (-0.5 * weight / LONG) * odd[1]
    kod[1] = (0.5 * weight / LONG) * odd[0]

    for h in range(2):
        rows_all(h).wait_recv()
    step = power(float(SIDE), step_dec, step_det)
    slot = lax.rem(lane_iota((8, SIDE)) // 16, 4)
    turn_row = stack([
        tuple(jnp.broadcast_to(spec[c, k : k + 1, :], (PART, SIDE)) for c in (0, 1))
        for k in range(TIMES)
    ])

    def half_of(table, v):
        picked = []
        for c in (0, 1):
            x = table[c].reshape(TIMES, 2, 2, 8, SIDE)[:, :, v]
            picked.append(x.reshape(SIDE // 2, SIDE))
        return tuple(picked)

    folded = [[jnp.zeros((8, SIDE), F32) for c in (0, 1)] for k in range(TIMES)]
    for v in range(2):
        rows = slice(8 * v, 8 * v + 8)
        field = []
        for k in range(TIMES):
            tiles = {(a, h): r2[h, k * LATS + a, rows] for a in range(LATS) for h in range(2)}
            re, im = unpack_halves(tiles)
            field.append((jnp.concatenate(re, axis=0), jnp.concatenate(im, axis=0)))
        once = cmul(time_dft(field), turn_row)
        twisted = time_dft(twist(time_inverse_dft(once), False))
        twisted = time_inverse_dft(cmul(twisted, half_of(kod, v)))
        late = time_dft(twist(twisted, True))
        straight = cmul(once, half_of(kev, v))
        once = cmul((straight[0] + late[0], straight[1] + late[1]), turn_row)
        field = time_inverse_dft(once)
        for k in range(TIMES):
            re, im = ((x[:8], x[8:]) for x in field[k])
            for (a, h), tile in pack_halves(re, im).items():
                s3[v][h][k * LATS + a, :8, :] = tile
        if v == 0:
            for h in range(2):
                each(lambda tl, tm, h=h: to_columns(0, h, tl, tm).start())
        flat = stack(field)
        ends = dot3(halves(jnp.concatenate(flat, axis=1)), (p_hi[...], p_lo[...]))
        ends = unstack((ends[:, :SIDE], ends[:, SIDE:]))
        state = (jnp.zeros((PART, SIDE), F32), jnp.zeros((PART, SIDE), F32))
        for k in range(TIMES):
            for c in (0, 1):
                for g in range(2):
                    piece = state[c][8 * g : 8 * g + 8]
                    folded[k][c] = jnp.where(slot == 2 * g + v, piece, folded[k][c])
            moved = cmul(state, step)
            state = (moved[0] + ends[k][0], moved[1] + ends[k][1])
    for k in range(TIMES):
        for a, tile in enumerate(pack(*folded[k])):
            s3c[k * LATS + a, 8:, :] = tile
    each(lambda tl, tm: to_columns(1, 0, tl, tm).start())
    for v in range(2):
        for h in range(2):
            r3[v][h][l * TIMES + m] = s3[v][h][m * LATS + l]

    t2 = rows_ref[0, 2 * TIMES : 2 * TIMES + 1, :], rows_ref[1, 2 * TIMES : 2 * TIMES + 1, :]
    q = (q_hi[...], q_lo[...])
    response = dot3(halves(jnp.where(lane_iota(whole) < 64, ct[...], 0.0)), q)
    response = (response[:, :SIDE], response[:, SIDE:])
    even, odd = wide_dft(*response), wide_dft(*cmul(response, t2))
    gain = 0.5 * weight / SIDE
    kfe[0], kfe[1] = -gain * even[1], gain * even[0]
    kfo[0], kfo[1] = -gain * odd[1], gain * odd[0]

    columns_all(1, 0).wait_send()
    each(lambda tl, tm: to_columns(1, 1, tl, tm).start())
    span = SIDE // 2
    fold = span // 8
    slot = lax.rem(lane_iota((fold, 128)), 64) // 8
    s4, r4 = (s4a, s4b), (r4a, r4b)

    def last_all(h, u):
        return all_of(r4[h].at[u], LATS - 1, ss4.at[h, u], rs4.at[h, u])

    for h in range(2):
        columns_all(0, h).wait_recv()
        columns_all(1, h).wait_recv()
        tiles, states = [], []
        for a in range(LATS):
            mine = slice(a * TIMES, (a + 1) * TIMES)
            both = jnp.stack([r3[v][h][mine, :8, :] for v in range(2)], axis=1)
            tiles.append(both.reshape(span, 128))
            if h == 0:
                extra = r3c[mine, 8:, :].reshape(8 * TIMES, 128)
                extra = [roll(extra, -16 * g).reshape(TIMES, 8, 128) for g in range(4)]
                states.append(jnp.stack(extra, axis=1).reshape(SIDE, 128))
        spectrum = lateral_spectrum(tiles, states)
        for u in range(2):
            done = lateral_inverse(spectrum, span * u, span * (u + 1))
            for a in range(LATS):
                s4[h][u, a, : span // 2, :] = done[0][a]
                if h == 0:
                    total = done[1][a][:fold]
                    for g in range(1, 8):
                        piece = roll(done[1][a][fold * g : fold * (g + 1)], 8 * g)
                        total = jnp.where(slot == g, piece, total)
                    s4a[u, a, span // 2 :, :] = total
            for d in range(1, LATS):
                sems = ss4.at[h, u], rs4.at[h, u]
                lat_send(s4[h].at[u], r4[h].at[u], *sems, d).start()
            r4[h][u, l] = s4[h][u, l]

    stores = []
    slot = lax.rem(lane_iota((fold, 128)), 64) // 16
    for u in range(2):
        for h in range(2):
            last_all(h, u).wait_recv()
        here = pl.ds(span * u, span)
        re, im = unpack_halves({
            (a, h): r4[h][u, a, : span // 2, :] for a in range(LATS) for h in range(2)
        })
        field = join_rows(*re), join_rows(*im)
        carried = []
        for g in range(8):
            total = jnp.zeros((fold, 128), F32)
            for a in range(LATS):
                piece = roll(r4a[u, a, span // 2 :, :], 16 * a - 8 * g)
                total = jnp.where(slot == a, piece, total)
            carried.append(total)
        carried = halves(jnp.concatenate(carried, axis=0) * ct[here, :])
        carried = dot3(carried, (q_hi[...], q_lo[...]))
        even = wide_inverse(*cmul(wide_dft(*field), (kfe[0, here, :], kfe[1, here, :])))
        odd = wide_dft(*cmul(field, t2))
        odd = wide_inverse(*cmul(odd, (kfo[0, here, :], kfo[1, here, :])))
        odd = cmul(odd, conj(t2))
        out[0, here, :] = field[0] + even[0] + odd[0] - weight * carried[:, SIDE:]
        out[1, here, :] = field[1] + even[1] + odd[1] + weight * carried[:, :SIDE]
        stores.append(
            pltpu.make_async_copy(out.at[:, here], out_hbm.at[:, here], store_sem.at[u])
        )
        stores[-1].start()

    first_all(1).wait_send()
    for h in range(2):
        rows_all(h).wait_send()
        for u in range(2):
            last_all(h, u).wait_send()
    for v, h in ((0, 0), (0, 1), (1, 1)):
        columns_all(v, h).wait_send()
    for copy in stores:
        copy.wait()


def fused(light_field, lateral_phase, spectral_phase, occupation, bin_decay, bin_detune, group_bin):
    tile = (SIDE, 128)
    vmem, sems = pltpu.VMEM, pltpu.SemaphoreType.DMA
    exchange = [
        vmem(light_field.shape, F32),
        vmem((2, LATS, SIDE // 2, 128), F32), vmem((2, LATS, SIDE // 2, 128), F32),
        vmem((2, LATS, SIDE // 2, 128), F32), vmem((2, TOTAL, PART, 128), F32),
        *[vmem((TOTAL, rows, 128), F32) for rows in (8, 8, 8, 8, 16, 16, 8, 8)],
        vmem((2, LATS, 5 * SIDE // 16, 128), F32), vmem((2, LATS, 5 * SIDE // 16, 128), F32),
        vmem((2, LATS, SIDE // 4, 128), F32), vmem((2, LATS, SIDE // 4, 128), F32),
    ]
    tables = [vmem((LATS,) + tile, F32)] * 2 + [vmem((LATS, SIDE // 2, 128), F32)] * 2
    tables += [vmem((LATS,) + tile, F32)] * 2 + [vmem(tile, F32)]
    tables += [vmem((128, 2 * SIDE), BF16)] * 2 + [vmem((2 * SIDE, 2 * SIDE), BF16)] * 2
    tables += [vmem((2, SIDE, SIDE), F32)] * 4
    tables += [vmem((2, TIMES, SIDE), F32)]
    fixed = constants()
    tables += [vmem(light_field.shape, F32), vmem(occupation.shape, F32)]
    tables += [vmem(c.shape, c.dtype) for c in fixed]
    semaphores = [sems((2,))] * 4 + [sems((2, 2))] * 4
    semaphores += [sems((2 + len(fixed),)), sems((2,))]
    in_vmem, anywhere = pl.BlockSpec(memory_space=pltpu.VMEM), pl.BlockSpec(memory_space=pl.ANY)
    return pl.pallas_call(
        kernel,
        out_shape=jax.ShapeDtypeStruct(light_field.shape, F32),
        in_specs=[anywhere] + [in_vmem] * 2 + [anywhere] + [in_vmem] * 3 + [anywhere] * len(fixed),
        out_specs=anywhere,
        scratch_shapes=exchange + tables + semaphores,
        compiler_params=pltpu.CompilerParams(
            collective_id=0, has_side_effects=True, vmem_limit_bytes=56 * 1024 * 1024
        ),
    )(
        light_field,
        lateral_phase.reshape(WIDE // 128, 128),
        spectral_phase.reshape(SIDE, TIMES),
        occupation,
        bin_decay[None],
        bin_detune[None],
        group_bin[None],
        *[jnp.asarray(c) for c in fixed],
    )


def solution(mesh):
    def local(light_field, *rest):
        fits = (lax.axis_size("lat"), lax.axis_size("tm")) == (LATS, TIMES)
        fits = fits and light_field.shape == (2, SIDE, SIDE)
        fits = fits and rest[2].shape == (128, SIDE) and rest[3].shape == (BIN_COUNT,)
        return (fused if fits else on_device)(light_field, *rest)

    return jax.shard_map(
        local,
        mesh=mesh,
        in_specs=(P(None, "lat", "tm"), P(), P(), P(None, "lat"), P(), P(), P()),
        out_specs=P(None, "lat", "tm"),
        check_vma=False,
    )
```
